32 devices in a mesh: dp: 8 (over z, core), tensor: 4 (over y, x).
Axes of the slice: x: 2, y: 2, z: 4, core: 2. Of those that a mesh axis runs over, the one named last changes fastest.
Arguments:
- hidden: bfloat16 [2048, 4096], P(('dp', 'tensor')), may hold values from -3.6 to 3.6
- lengths: int32 [8, 32], P('dp'), may hold values from 1 to 80, 256 in all within a row
- positives: int32 [64], replicated, may hold values from 0 to 191, as said below
- negatives: int32 [64, 7], replicated, may hold values from 1 to 190, as said below
- in_gain: float32 [4096], replicated, may hold values from 0.25 to 1.75
- wq: bfloat16 [4096, 512], P(None, 'tensor'), may hold values from -0.09375 to 0.09375
- wkv: bfloat16 [4096, 512], P(None, 'tensor'), may hold values from -0.09375 to 0.09375
- q_gain: float32 [128], replicated, may hold values from 0.25 to 1.75
- k_gain: float32 [128], replicated, may hold values from 0.25 to 1.75
- wo: bfloat16 [512, 4096], P('tensor'), may hold values from -0.25 to 0.25
- out_gain: float32 [4096], replicated, may hold values from 0.25 to 1.75
Outputs:
- d_hidden: bfloat16 [2048, 4096], P(('dp', 'tensor'))
- loss: float32 [], replicated
The draws below stay inside these ranges and needn't reach their ends.
Inputs may be any that keep to these rules, and one draw needn't show every extreme that they name: Each group's 32 lengths sum to 256, and one of them is exactly 80. The 64 positives are distinct passages. The 7 hard negatives of a query are distinct, and none of them is any query's positive.
All inputs are finite; a program needn't handle non-finite values.
Results may differ from the reference program's by a relative error of at most 0.023.
Values may be sent and summed in bfloat16 or wider, within the bound.
A program may use at most 64 MiB of HBM per device.

```python
import math
import jax
import jax.numpy as jnp
import numpy as np
from jax import lax

D = 4096
HD = 128
QH = 4
KVH = 2
TOK_DEV = 256
QDEV = 8
NNEG = 7
NSEQ = 32
LMAX = 80
QALL = 64
PALL = 192
TOKENS = 2048
N_DP = 8


def place_value(order, value, target_labels):
    where_now = jnp.argmax(order == value).astype(jnp.int32)
    return order.at[where_now].set(order[target_labels]).at[target_labels].set(value)


def passage_order(key):
    order = jax.random.permutation(jax.random.fold_in(key, 11), PALL).astype(jnp.int32)
    order = place_value(order, 0, 0)
    order = place_value(order, PALL - 1, QALL - 1)
    order = place_value(order, 1, QALL)
    order = place_value(order, PALL - 2, QALL + 1)
    return order


def draw_positives(key, part):
    order = passage_order(key)
    return order[:QALL].astype(jnp.int32)


def draw_negatives(key, part):
    order = passage_order(key)
    key = jax.random.fold_in(key, 7)
    favour_key, noise_key = jax.random.split(key)
    pool = order[QALL:]
    pool_size = PALL - QALL
    favoured = (pool == 1) | (pool == PALL - 2)
    favour = jnp.where(favoured, 4, jax.random.randint(favour_key, (pool_size,), 0, 4))
    noise = jax.random.randint(noise_key, (QALL, pool_size), 0, 32768)
    score = (favour[None, :] * 65536 + noise) * pool_size + jnp.arange(pool_size, dtype=jnp.int32)[None, :]
    picked = lax.top_k(score.astype(jnp.int32), NNEG)[1]
    return jnp.take(pool, picked).astype(jnp.int32)


def draw_hidden(key, part):
    key = jax.random.fold_in(key, 3)
    row_key, column_key, base_key = jax.random.split(key, 3)
    row_scale = 0.03 * jnp.exp(jax.random.uniform(row_key, (TOKENS, 1), jnp.float32, 0.0, math.log(10.0)))
    column_scale = 0.3 * jnp.exp(jax.random.uniform(column_key, (1, D), jnp.float32, 0.0, math.log(10.0)))
    base = jax.random.truncated_normal(base_key, -4.0, 4.0, (TOKENS, D), jnp.float32)
    return (base * row_scale * column_scale).astype(jnp.bfloat16)


def shard_levels(key, extent, pieces, least, top_value):
    def one(axis_at, shards_of):
        draws = jax.random.uniform(jax.random.fold_in(jax.random.fold_in(key, 6), axis_at), (shards_of,), jnp.float32, least / len(pieces), top_value / len(pieces))
        return jnp.repeat(jnp.exp(draws), extent[axis_at] // shards_of).reshape((-1,) + (1,) * (len(extent) - axis_at - 1))

    factor_of = one(*pieces[0])
    for cut in pieces[1:]:
        factor_of = factor_of * one(*cut)
    return factor_of


def length_profile(amount, total, bound, slope):
    portions = [(1 << 20) // math.isqrt(standing ** slope) + 1 for standing in range(2, amount + 1)]
    rest, counts = total - bound - (amount - 1), [1] * (amount - 1)
    while rest > 0:
        free = [i for i in range(amount - 1) if counts[i] < bound]
        mass, remaining = sum([portions[i] for i in free]), rest
        for i in free:
            addition = min(bound - counts[i], max(1, remaining * portions[i] // mass), rest)
            counts[i] = counts[i] + addition
            rest = rest - addition
    return np.array([bound] + counts)


def uneven_parts(own_key, number_of, total, limit, slope):
    if number_of == 2:
        one = jax.random.randint(own_key, (), max(1, total - limit), min(limit, total - 1) + 1)
        return jnp.stack([one, total - one])
    tallies = jnp.asarray(length_profile(number_of, total, limit, slope), jnp.int32)
    couples = (number_of - 1) // 2
    donor, receiver = tallies[1:1 + 2 * couples:2], tallies[2:2 + 2 * couples:2]
    slack = jnp.minimum(donor - 1, limit - receiver)
    moved = jax.random.randint(jax.random.fold_in(own_key, 1), (couples,), 0, 1 << 20) % (slack + 1)
    tallies = tallies.at[1:1 + 2 * couples:2].set(donor - moved).at[2:2 + 2 * couples:2].set(receiver + moved)
    return tallies[jax.random.permutation(jax.random.fold_in(own_key, 2), number_of)]


def normal_values(rng, extent, scale, most, cuts=(), kind=jnp.bfloat16):
    entries = jax.random.normal(rng, extent, jnp.float32) * scale
    if len(cuts) > 0:
        entries = shard_levels(rng, extent, cuts, -0.22, 0.18) * entries
    return jnp.clip(entries, min=-most, max=most).astype(kind)


def setup_inputs(seed: int = 0) -> dict:
    streams_of = jax.random.split(jax.random.key(seed), 12)
    return {
        "hidden": draw_hidden(jax.random.fold_in(streams_of[11], 71), 0),
        "lengths": jax.vmap(lambda own: uneven_parts(own, NSEQ, TOK_DEV, LMAX, 2))(jax.random.split(streams_of[1], N_DP)).reshape((N_DP, NSEQ)).astype(jnp.int32),
        "positives": draw_positives(jax.random.fold_in(streams_of[11], 71), 0),
        "negatives": draw_negatives(jax.random.fold_in(streams_of[11], 71), 0),
        "in_gain": jnp.clip(1.0 + 0.15 * jax.random.normal(streams_of[4], (D,), jnp.float32), 0.25, 1.75),
        "wq": normal_values(streams_of[5], (D, QH * HD), D ** -0.5, 0.09375, ((1, 4),)),
        "wkv": normal_values(streams_of[6], (D, 2 * KVH * HD), D ** -0.5, 0.09375, ((1, 4),)),
        "q_gain": jnp.clip(1.0 + 0.15 * jax.random.normal(streams_of[7], (HD,), jnp.float32), 0.25, 1.75),
        "k_gain": jnp.clip(1.0 + 0.15 * jax.random.normal(streams_of[8], (HD,), jnp.float32), 0.25, 1.75),
        "wo": normal_values(streams_of[9], (QH * HD, D), (QH * HD) ** -0.5, 0.25, ((0, 4),)),
        "out_gain": jnp.clip(1.0 + 0.15 * jax.random.normal(streams_of[10], (D,), jnp.float32), 0.25, 1.75),
    }


EPSILON = 1e-06
SOFTMAX_TEMPER = 0.05
LOSS_MULTIPLIER = 8192.0
ROPE_BASE = 1000000.0

def rms_scale(tensor):
    return lax.rsqrt(lax.optimization_barrier(jnp.mean(tensor * tensor, axis=-1, keepdims=True)) + EPSILON)

def rope_tables(position, head_width):
    halfway = head_width // 2
    frequency = ROPE_BASE ** (-(jnp.arange(halfway, dtype=jnp.float32) * (2.0 / head_width)))
    angles = position[:, None] * frequency[None, :]
    angles = jnp.concatenate([angles, angles], axis=-1)
    return (jnp.cos(angles), jnp.sin(angles))

def rotate(tensor, cosine, sine):
    halfway = tensor.shape[-1] // 2
    turned = jnp.concatenate([-tensor[..., halfway:], tensor[..., :halfway]], axis=-1)
    return tensor * cosine + turned * sine

def segment_layout(lengths_row, total_tokens):
    seq_ends = jnp.cumsum(lengths_row).astype(jnp.int32)
    starts = seq_ends - lengths_row.astype(jnp.int32)
    token_index = jnp.arange(total_tokens, dtype=jnp.int32)
    inside = (token_index[:, None] >= starts[None, :]) & (token_index[:, None] < seq_ends[None, :])
    offset = lax.optimization_barrier(jnp.sum(jnp.where(inside, starts[None, :], 0), axis=1)).astype(jnp.int32)
    position = (token_index - offset).astype(jnp.float32)
    return (inside, position, (seq_ends - 1).astype(jnp.int32))

def head_forward(raw, gain, cosine, sine):
    inverse = rms_scale(raw)
    unit_form = raw * inverse
    return (unit_form, inverse, rotate(unit_form * gain, cosine, sine))

def norm_backward(grad, unit_form, inverse, gain):
    scaled = grad * gain
    return inverse * (scaled - unit_form * lax.optimization_barrier(jnp.mean(unit_form * scaled, axis=-1, keepdims=True)))

def head_backward(grad_rot, unit_form, inverse, gain, cosine, sine):
    return norm_backward(rotate(grad_rot, cosine, -sine), unit_form, inverse, gain)

def contrast(embeds16, positives, negatives):
    groups = embeds16.shape[0]
    feature_count = embeds16.shape[2]
    query_rows = embeds16[:, :QDEV].reshape(groups * QDEV, feature_count)
    passage_rows = embeds16[:, QDEV:].reshape(-1, feature_count)
    query_total_count = query_rows.shape[0]
    passage_ids = jnp.arange(passage_rows.shape[0], dtype=jnp.int32)
    similarity_logits = jnp.dot(query_rows, passage_rows.T, preferred_element_type=jnp.float32) / SOFTMAX_TEMPER
    positive_hot = positives[:, None] == passage_ids[None, :]
    hard_hot = jnp.any(negatives[:, :, None] == passage_ids[None, None, :], axis=1)
    permitted_mask = jnp.any(positive_hot, axis=0)[None, :] | hard_hot
    weight_params = jnp.where(permitted_mask, jnp.exp(similarity_logits - 1.0 / SOFTMAX_TEMPER), 0.0)
    running_totals = lax.optimization_barrier(jnp.sum(weight_params, axis=1, keepdims=True))
    target_labels = lax.optimization_barrier(jnp.sum(jnp.where(positive_hot, similarity_logits, 0.0), axis=1))
    loss = jnp.mean(jnp.log(running_totals[:, 0]) + 1.0 / SOFTMAX_TEMPER - target_labels)
    scaling_factor = LOSS_MULTIPLIER / (query_total_count * SOFTMAX_TEMPER)
    coef16 = (scaling_factor * (weight_params / running_totals - positive_hot.astype(jnp.float32))).astype(jnp.bfloat16)
    d_queries = jnp.dot(coef16, passage_rows, preferred_element_type=jnp.float32)
    d_passages = jnp.dot(coef16.T, query_rows, preferred_element_type=jnp.float32)
    joined = jnp.concatenate([d_queries.reshape(groups, QDEV, feature_count), d_passages.reshape(groups, -1, feature_count)], axis=1)
    return (loss, joined)

def group_forward(hidden_rows, lengths_row, in_gain, wq, wkv, q_gain, k_gain, wo, out_gain):
    tokens_count = hidden_rows.shape[0]
    inside, position, last = segment_layout(lengths_row, tokens_count)
    hidden32 = hidden_rows.astype(jnp.float32)
    inverse_in = rms_scale(hidden32)
    normed = (hidden32 * inverse_in * in_gain).astype(jnp.bfloat16)
    kv_raw = jnp.dot(normed, wkv, preferred_element_type=jnp.float32).reshape(tokens_count, KVH, 2, HD)
    key_raw = kv_raw[:, :, 0]
    value16 = kv_raw[:, :, 1].astype(jnp.bfloat16)
    cos_key, sin_key = rope_tables(position, HD)
    key_unit, key_inverse, key_rot = head_forward(key_raw, k_gain, cos_key[:, None], sin_key[:, None])
    key16 = key_rot.astype(jnp.bfloat16)
    last_rows = jnp.take(normed, last, axis=0)
    query_raw = jnp.dot(last_rows, wq, preferred_element_type=jnp.float32).reshape(NSEQ, QH, HD)
    cos_query, sin_query = rope_tables(jnp.take(position, last), HD)
    query_unit, query_inverse, query_rot = head_forward(query_raw, q_gain, cos_query[:, None], sin_query[:, None])
    query16 = query_rot.astype(jnp.bfloat16)
    shift = math.sqrt(HD) * jnp.max(q_gain) * jnp.max(k_gain)
    key_heads = jnp.repeat(key16, 2, axis=1).astype(jnp.float32)
    value_heads = jnp.repeat(value16, 2, axis=1).astype(jnp.float32)
    scores = jnp.einsum('shd,thd->sht', query16.astype(jnp.float32), key_heads) / math.sqrt(HD)
    weight_params = jnp.where(inside.T[:, None, :], jnp.exp(scores - shift), 0.0)
    probs = weight_params / lax.optimization_barrier(jnp.sum(weight_params, axis=-1, keepdims=True))
    probs16 = probs.astype(jnp.bfloat16)
    attn16 = jnp.einsum('sht,thd->shd', probs16.astype(jnp.float32), value_heads).astype(jnp.bfloat16).reshape(NSEQ, QH * HD)
    resid = jnp.take(hidden32, last, axis=0) + jnp.dot(attn16, wo, preferred_element_type=jnp.float32)
    resid_inverse = rms_scale(resid)
    resid_unit = resid * resid_inverse
    final = resid_unit * out_gain
    final_inverse = lax.rsqrt(lax.optimization_barrier(jnp.sum(final * final, axis=-1, keepdims=True)) + EPSILON)
    embed = final * final_inverse
    saved = (inverse_in, last, key_unit, key_inverse, key16, value16, query_unit, query_inverse, query16, probs, probs16, resid_unit, resid_inverse, embed, final_inverse, cos_key, sin_key, cos_query, sin_query)
    return (embed.astype(jnp.bfloat16), saved)

def group_backward(hidden_rows, d_embed, saved, in_gain, wq, wkv, q_gain, k_gain, wo, out_gain):
    inverse_in, last, key_unit, key_inverse, key16, value16, query_unit, query_inverse, query16, probs, probs16, resid_unit, resid_inverse, embed, final_inverse, cos_key, sin_key, cos_query, sin_query = saved
    tokens_count = hidden_rows.shape[0]
    hidden32 = hidden_rows.astype(jnp.float32)
    d_final = final_inverse * (d_embed - embed * lax.optimization_barrier(jnp.sum(embed * d_embed, axis=-1, keepdims=True)))
    d_resid = norm_backward(d_final, resid_unit, resid_inverse, out_gain)
    d_attn16 = jnp.dot(d_resid.astype(jnp.bfloat16), wo.T, preferred_element_type=jnp.float32).astype(jnp.bfloat16).reshape(NSEQ, QH, HD)
    key_heads = jnp.repeat(key16, 2, axis=1).astype(jnp.float32)
    value_heads = jnp.repeat(value16, 2, axis=1).astype(jnp.float32)
    d_probs = jnp.einsum('shd,thd->sht', d_attn16.astype(jnp.float32), value_heads)
    d_scores16 = (probs * (d_probs - lax.optimization_barrier(jnp.sum(probs * d_probs, axis=-1, keepdims=True))) / math.sqrt(HD)).astype(jnp.bfloat16)
    d_query_rot = jnp.einsum('sht,thd->shd', d_scores16.astype(jnp.float32), key_heads)
    d_key_heads = jnp.einsum('sht,shd->thd', d_scores16.astype(jnp.float32), query16.astype(jnp.float32))
    d_value_heads = jnp.einsum('sht,shd->thd', probs16.astype(jnp.float32), d_attn16.astype(jnp.float32))
    d_key_rot = lax.optimization_barrier(jnp.sum(d_key_heads.reshape(tokens_count, KVH, 2, HD), axis=2))
    d_value = lax.optimization_barrier(jnp.sum(d_value_heads.reshape(tokens_count, KVH, 2, HD), axis=2))
    d_key_raw = head_backward(d_key_rot, key_unit, key_inverse, k_gain, cos_key[:, None], sin_key[:, None])
    d_query_raw = head_backward(d_query_rot, query_unit, query_inverse, q_gain, cos_query[:, None], sin_query[:, None])
    d_kv16 = jnp.stack([d_key_raw, d_value], axis=2).reshape(tokens_count, QH, HD).astype(jnp.bfloat16)
    d_query16 = d_query_raw.astype(jnp.bfloat16)
    kv_blocks = jnp.transpose(d_kv16, (1, 0, 2))
    wkv_blocks = jnp.transpose(wkv.reshape(D, QH, HD), (1, 0, 2))
    query_blocks = jnp.transpose(d_query16, (1, 0, 2))
    wq_blocks = jnp.transpose(wq.reshape(D, QH, HD), (1, 0, 2))

    def add_block(total, items):
        kv_part, wkv_part, query_part, wq_part = items
        term = jnp.dot(kv_part, wkv_part.T, preferred_element_type=jnp.float32)
        term = term.at[last].add(jnp.dot(query_part, wq_part.T, preferred_element_type=jnp.float32))
        rounded = lax.optimization_barrier(term.astype(jnp.bfloat16))
        return (total + rounded.astype(jnp.float32), None)
    start_total = jnp.zeros((tokens_count, D), jnp.float32)
    d_normed, _ = lax.scan(add_block, start_total, (kv_blocks, wkv_blocks, query_blocks, wq_blocks))
    d_hidden = norm_backward(d_normed, hidden32 * inverse_in, inverse_in, in_gain)
    d_hidden = d_hidden.at[last].add(d_resid)
    return d_hidden.astype(jnp.bfloat16)

def reference(hidden, lengths, positives, negatives, in_gain, wq, wkv, q_gain, k_gain, wo, out_gain):
    groups = hidden.reshape(N_DP, TOK_DEV, D)

    def forward_one(items):
        return group_forward(items[0], items[1], in_gain, wq, wkv, q_gain, k_gain, wo, out_gain)
    embeds, saved = lax.map(forward_one, (groups, lengths))
    loss, d_embeds = contrast(embeds, positives, negatives)

    def backward_one(items):
        return group_backward(items[0], items[1], items[2], in_gain, wq, wkv, q_gain, k_gain, wo, out_gain)
    d_hidden = lax.map(backward_one, (groups, d_embeds, saved))
    return (d_hidden.reshape(TOKENS, D), loss)
```

```python
import functools
import math

import jax
import jax.numpy as jnp
from jax import lax
from jax.experimental import pallas as pl
from jax.experimental.pallas import tpu as pltpu
from jax.sharding import PartitionSpec as P

QDEV = 8
EPSILON = 1e-06
SOFTMAX_TEMPER = 0.05
LOSS_MULTIPLIER = 8192.0
ROPE_BASE = 1000000.0

F32 = jnp.float32
BF16 = jnp.bfloat16
MESH = pl.DeviceIdType.MESH
EXACT = lax.Precision.HIGHEST


def nn(a, b, precision=None):
    return jnp.dot(a, b, preferred_element_type=F32, precision=precision)


def nt(a, b, precision=None):
    dims = (((1,), (1,)), ((), ()))
    return lax.dot_general(a, b, dims, preferred_element_type=F32, precision=precision)


def iota(shape, axis):
    return lax.broadcasted_iota(jnp.int32, shape, axis)


def onehot(mask, kind=BF16):
    return jnp.where(mask, 1.0, 0.0).astype(F32).astype(kind)


def rms_scale(x):
    return lax.rsqrt(jnp.mean(x * x, axis=-1, keepdims=True) + EPSILON)


def rope_tables(position, width):
    half = width // 2
    lane = iota((1, width), 1)
    lane = jnp.where(lane >= half, lane - half, lane).astype(F32)
    frequency = jnp.exp(lane * (-2.0 / width * math.log(ROPE_BASE)))
    angles = position * frequency
    return jnp.cos(angles), jnp.sin(angles)


def rotate(x, cosine, sine):
    half = x.shape[-1] // 2
    sign = jnp.where(iota((1, x.shape[-1]), 1) < half, -1.0, 1.0)
    return x * cosine + pltpu.roll(x, half, 1) * sign * sine


def head_forward(raw, gain, cosine, sine):
    inverse = rms_scale(raw)
    unit = raw * inverse
    return unit, inverse, rotate(unit * gain, cosine, sine)


def head_backward(grad, unit, inverse, gain, cosine, sine):
    scaled = rotate(grad, cosine, -sine) * gain
    return inverse * (scaled - unit * jnp.mean(unit * scaled, axis=-1, keepdims=True))


def kernel(
    tensors, groups,
    hidden, lens, positives, negatives, in_gain, wq, wkv, q_gain, k_gain, wo, out_gain,
    out, loss,
    hid_own, hid_all, inv_all, normed, wkv_all, wq_all, wo_all,
    kvp_out, kvp_in, qp_out, qp_in, attn_all, sums_all, embeds, logit_all,
    dap_out, dap_in, pair_out, pair_in, dkv_all, dq_all, rows_all, out16,
    local_sem, tsend, trecv, fsend, frecv, zsend, zrecv, psend, precv,
):
    T, G = tensors, groups
    Z = G // 2
    own, D = hidden.shape
    F = D // T
    HD = wq.shape[1]
    N = own * T
    S = lens.shape[1]
    Q = positives.shape[1]
    H = F // 2
    HH = HD // 2
    root = math.sqrt(HD)
    t = lax.axis_index("tensor")
    g = lax.axis_index("dp")
    zz = g // 2
    core = g % 2
    buddy = g + 1 - 2 * core
    mate = t + 1 - 2 * (t % 2)
    even = t % 2 == 0
    peers = [lax.rem(t + k, T) for k in range(1, T)]
    sources = [lax.rem(t + T - k, T) for k in range(1, T)]
    slots = list(range(T))
    columns = pl.ds(pl.multiple_of(t * F, 128), F)

    own_copies = [
        pltpu.make_async_copy(hidden, hid_own, local_sem.at[0]),
        pltpu.make_async_copy(
            hidden.at[:, columns], hid_all.at[pl.ds(t * own, own)], local_sem.at[1]
        ),
        pltpu.make_async_copy(wkv.at[pl.ds(t * F, F)], wkv_all.at[t], local_sem.at[2]),
        pltpu.make_async_copy(wq.at[pl.ds(t * F, F)], wq_all.at[t], local_sem.at[3]),
        pltpu.make_async_copy(wo.at[:, columns], wo_all.at[t], local_sem.at[4]),
    ]
    for copy in own_copies:
        copy.start()

    barrier = pltpu.get_barrier_semaphore()
    for p in peers:
        pl.semaphore_signal(barrier, inc=1, device_id=(g, p), device_id_type=MESH)
    for k in range(1, Z):
        far = lax.rem(zz + k, Z) * 2 + core
        pl.semaphore_signal(barrier, inc=1, device_id=(far, t), device_id_type=MESH)
    pl.semaphore_signal(barrier, inc=1, device_id=(buddy, t), device_id_type=MESH)
    pl.semaphore_wait(barrier, T - 1 + Z - 1 + 1)

    waits = []

    def to_peer(kind, k, src, dst):
        copy = pltpu.make_async_remote_copy(
            src_ref=src, dst_ref=dst, send_sem=tsend.at[kind, k], recv_sem=trecv.at[kind, k],
            device_id=(g, peers[k]), device_id_type=MESH,
        )
        copy.start()
        waits.append(copy)
        return copy

    def to_buddy(kind, k, src, dst):
        copy = pltpu.make_async_remote_copy(
            src_ref=src, dst_ref=dst, send_sem=fsend.at[kind, k], recv_sem=frecv.at[kind, k],
            device_id=(buddy, t), device_id_type=MESH,
        )
        copy.start()
        waits.append(copy)
        return copy

    def landed(copies):
        for copy in copies:
            copy.wait_recv()

    rest = range(T - 1)
    my_rows = pl.ds(pl.multiple_of(t * own, own), own)

    def cols(p):
        return pl.ds(pl.multiple_of(p * F, 128), F)

    hid_copies = [
        to_peer(0, k, hidden.at[:, cols(peers[k])], hid_all.at[my_rows]) for k in rest
    ]

    def half_rows(p):
        return pl.ds(pl.multiple_of(p * F + core * H, H), H)

    my_half = pl.ds(pl.multiple_of(core * H, H), H)
    my_head_half = pl.ds(pl.multiple_of(core * HH, HH), HH)
    wkv_copies = [
        to_peer(1, k, wkv.at[half_rows(peers[k])], wkv_all.at[t, my_half]) for k in rest
    ]

    own_copies[0].wait()
    mine = hid_own[...].astype(F32)
    inv_all[my_rows, :] = jnp.broadcast_to(rms_scale(mine), (own, HD))
    inv_copies = [to_peer(2, k, inv_all.at[my_rows], inv_all.at[my_rows]) for k in rest]

    lens_row = lens[...].astype(F32)
    square_r, square_c = iota((S, S), 0), iota((S, S), 1)
    lens_col = jnp.sum(jnp.where(square_r == square_c, lens_row, 0.0), axis=1, keepdims=True)
    ends_col = jnp.sum(jnp.where(square_c <= square_r, lens_row, 0.0), axis=1, keepdims=True)
    ends_row = jnp.sum(jnp.where(square_r <= square_c, lens_col, 0.0), axis=0, keepdims=True)
    starts_col, starts_row = ends_col - lens_col, ends_row - lens_row
    token_row = iota((S, N), 1).astype(F32)
    token_col = iota((N, S), 0).astype(F32)
    inside = (token_row >= starts_col) & (token_row < ends_col)
    inside_t = (token_col >= starts_row) & (token_col < ends_row)
    offset = jnp.sum(jnp.where(inside_t, starts_row, 0.0), axis=1, keepdims=True)
    position = iota((N, 1), 0).astype(F32) - offset
    last_hot = onehot(token_row == ends_col - 1.0)
    last_hot_t = onehot(token_col == ends_row - 1.0)
    cos_key, sin_key = rope_tables(position, HD)
    cos_query, sin_query = rope_tables(lens_col - 1.0, HD)
    qg, kg = q_gain[...], k_gain[...]
    shift = root * jnp.max(qg, axis=1, keepdims=True) * jnp.max(kg, axis=1, keepdims=True)
    gain = in_gain[:, columns]
    ogain = out_gain[:, columns]

    wkv_fwd = []
    for k in rest:
        wkv_copies[k].wait_recv()
        spot = wkv_all.at[sources[k], my_half]
        wkv_fwd.append(to_buddy(0, k, spot, spot))
    wq_copies = [
        to_peer(3, k, wq.at[half_rows(peers[k])], wq_all.at[t, my_half]) for k in rest
    ]

    own_copies[1].wait()
    landed(hid_copies)
    landed(inv_copies)
    hid32 = hid_all[...].astype(F32)
    normed[...] = (hid32 * inv_all[:, 0:1] * gain).astype(BF16)
    own_copies[2].wait()
    landed(wkv_fwd)
    for b in slots:
        kvp_out[b] = nn(normed[...], wkv_all[b]).astype(BF16)

    def pair(p):
        return pl.ds((p // 2) * 2, 2)

    kvp_copies = [to_peer(4, k, kvp_out.at[pair(peers[k])], kvp_in.at[t]) for k in rest]
    kvp_in[t] = kvp_out[pair(t)]

    wq_fwd = []
    for k in rest:
        wq_copies[k].wait_recv()
        spot = wq_all.at[sources[k], my_half]
        wq_fwd.append(to_buddy(1, k, spot, spot))
    wo_copies = [
        to_peer(
            5, k, wo.at[my_head_half, cols(peers[k])], wo_all.at[t, my_head_half]
        )
        for k in rest
    ]
    last16 = nn(last_hot, normed[...]).astype(BF16)
    hid_last = nn(last_hot, hid_all[...])
    own_copies[3].wait()
    landed(wq_fwd)
    for b in slots:
        qp_out[b] = nn(last16, wq_all[b])
    qp_copies = [to_peer(6, k, qp_out.at[peers[k]], qp_in.at[t]) for k in rest]
    qp_in[t] = qp_out[t]

    landed(kvp_copies)
    key_raw = kvp_in[0, 0].astype(F32)
    value_raw = kvp_in[0, 1].astype(F32)
    for s in slots[1:]:
        key_raw = key_raw + kvp_in[s, 0].astype(F32)
        value_raw = value_raw + kvp_in[s, 1].astype(F32)
    value16 = value_raw.astype(BF16)
    key_unit, key_inverse, key_rot = head_forward(key_raw, kg, cos_key, sin_key)
    key16 = key_rot.astype(BF16)

    landed(qp_copies)
    query_raw = qp_in[0]
    for s in slots[1:]:
        query_raw = query_raw + qp_in[s]
    query_unit, query_inverse, query_rot = head_forward(query_raw, qg, cos_query, sin_query)
    query16 = query_rot.astype(BF16)
    scores = nt(query16, key16) / root
    weight = jnp.where(inside, jnp.exp(scores - shift), 0.0)
    probs = weight / jnp.sum(weight, axis=-1, keepdims=True)
    probs16 = probs.astype(BF16)
    attn_all[t] = nn(probs16, value16).astype(BF16)
    attn_copies = [to_peer(7, k, attn_all.at[t], attn_all.at[t]) for k in rest]

    wo_fwd = []
    for k in rest:
        wo_copies[k].wait_recv()
        spot = wo_all.at[sources[k], my_head_half]
        wo_fwd.append(to_buddy(2, k, spot, spot))
    own_copies[4].wait()
    landed(wo_fwd)
    landed(attn_copies)

    resid = hid_last
    for s in slots:
        resid = resid + nn(attn_all[s], wo_all[s])
    scaled = resid * ogain
    lane = iota((S, HD), 1)
    sums_all[t] = jnp.where(
        lane == 0,
        jnp.sum(resid * resid, axis=1, keepdims=True),
        jnp.sum(scaled * scaled, axis=1, keepdims=True),
    )
    sums_copies = [to_peer(8, k, sums_all.at[t], sums_all.at[t]) for k in rest]
    landed(sums_copies)
    sums = sums_all[0]
    for s in slots[1:]:
        sums = sums + sums_all[s]
    resid_inverse = lax.rsqrt(sums[:, 0:1] / D + EPSILON)
    final_inverse = lax.rsqrt(resid_inverse * resid_inverse * sums[:, 1:2] + EPSILON)
    resid_unit = resid * resid_inverse
    embed = resid_unit * ogain * final_inverse

    my_seqs = pl.ds(pl.multiple_of(g * S, S), S)
    embeds[my_seqs, :] = embed.astype(BF16)
    z_copies = []
    for k in range(1, Z):
        far = lax.rem(zz + k, Z) * 2 + core
        copy = pltpu.make_async_remote_copy(
            src_ref=embeds.at[my_seqs], dst_ref=embeds.at[my_seqs],
            send_sem=zsend.at[k - 1], recv_sem=zrecv.at[k - 1],
            device_id=(far, t), device_id_type=MESH,
        )
        copy.start()
        waits.append(copy)
        z_copies.append(copy)

    def chip_copy(index, spot):
        copy = pltpu.make_async_remote_copy(
            src_ref=spot, dst_ref=spot, send_sem=psend.at[index], recv_sem=precv.at[index],
            device_id=(buddy, t), device_id_type=MESH,
        )
        copy.start()
        waits.append(copy)
        return copy

    shared = [chip_copy(0, embeds.at[my_seqs])]

    E = G * S
    seq_of = iota((1, E), 1) % S
    passage = jnp.where(seq_of >= QDEV, (iota((1, E), 1) // S) * (S - QDEV) + seq_of - QDEV, -1)
    eye_q = iota((Q, Q), 0) == iota((Q, Q), 1)
    pos_col = jnp.sum(
        jnp.where(eye_q, positives[...].astype(F32), 0.0), axis=1, keepdims=True
    ).astype(jnp.int32)
    pos_hot = pos_col == passage
    neg = negatives[...]
    hard = neg[:, 0:1] == passage
    for j in range(1, neg.shape[1]):
        hard = hard | (neg[:, j : j + 1] == passage)
    positive_f = jnp.where(pos_hot, 1.0, 0.0)
    allowed = (jnp.max(positive_f, axis=0, keepdims=True) > 0.5) | hard
    q_id = iota((Q, E), 0)
    pick_q = onehot(iota((Q, E), 1) == (q_id // QDEV) * S + q_id % QDEV)
    row_s = iota((S, Q), 0)
    own_q = (row_s < QDEV) & (iota((S, Q), 1) == g * QDEV + row_s)
    own_p = iota((S, E), 1) == g * S + iota((S, E), 0)

    for k in range(1, Z):
        z_copies[k - 1].wait_recv()
        origin = lax.rem(zz + Z - k, Z) * 2 + core
        shared.append(chip_copy(k, embeds.at[pl.ds(pl.multiple_of(origin * S, S), S)]))
    landed(shared)

    queries = nn(pick_q, embeds[...]).astype(BF16)
    logit_all[t] = nt(queries, embeds[...])
    logit_copies = [to_peer(9, k, logit_all.at[t], logit_all.at[t]) for k in rest]
    landed(logit_copies)
    dots = logit_all[0]
    for s in slots[1:]:
        dots = dots + logit_all[s]
    logits = dots / SOFTMAX_TEMPER
    grown = jnp.where(allowed, jnp.exp(logits - 1.0 / SOFTMAX_TEMPER), 0.0)
    totals = jnp.sum(grown, axis=1, keepdims=True)
    target = jnp.sum(jnp.where(pos_hot, logits, 0.0), axis=1, keepdims=True)
    each = jnp.log(totals) + 1.0 / SOFTMAX_TEMPER - target
    loss[...] = jnp.broadcast_to(jnp.sum(each, axis=0, keepdims=True) / Q, loss.shape)
    factor = LOSS_MULTIPLIER / (Q * SOFTMAX_TEMPER)
    coef16 = (factor * (grown / totals - positive_f)).astype(BF16)
    along = coef16.astype(F32) * dots
    own_q16, own_p16 = onehot(own_q), onehot(own_p)
    coef_q = nn(own_q16, coef16).astype(BF16)
    coef_p = nt(own_p16, coef16).astype(BF16)
    d_embed = nn(coef_q, embeds[...]) + nn(coef_p, queries)
    inner = jnp.sum(nn(onehot(own_q, F32), along, EXACT), axis=1, keepdims=True) + jnp.sum(
        nt(onehot(own_p, F32), along, EXACT), axis=1, keepdims=True
    )
    d_final = final_inverse * (d_embed - embed * inner)
    middle = inner * (EPSILON / D) * final_inverse * final_inverse
    d_resid = resid_inverse * (ogain * d_final - resid_unit * middle)
    d_resid16 = d_resid.astype(BF16)
    d_resid_low = (d_resid - d_resid16.astype(F32)).astype(BF16)

    for b in slots:
        dap_out[b] = nt(d_resid16, wo_all[b])
    dap_copies = [to_peer(10, k, dap_out.at[peers[k]], dap_in.at[t]) for k in rest]
    dap_in[t] = dap_out[t]
    eye_n = iota((N, N), 0) == iota((N, N), 1)
    eye16 = onehot(eye_n)
    probs16_t = nt(eye16, probs16).astype(BF16)
    landed(dap_copies)
    d_attn = dap_in[0]
    for s in slots[1:]:
        d_attn = d_attn + dap_in[s]
    d_attn16 = d_attn.astype(BF16)
    d_probs = nt(d_attn16, value16)
    d_scores16 = (
        probs * (d_probs - jnp.sum(probs * d_probs, axis=-1, keepdims=True)) / root
    ).astype(BF16)
    d_key_rot = nn(nt(eye16, d_scores16).astype(BF16), query16)
    d_value = nn(probs16_t, d_attn16)
    pair_out[...] = jnp.where(even, d_value, d_key_rot).astype(BF16)
    pair_copy = pltpu.make_async_remote_copy(
        src_ref=pair_out, dst_ref=pair_in, send_sem=psend.at[Z], recv_sem=precv.at[Z],
        device_id=(g, mate), device_id_type=MESH,
    )
    pair_copy.start()
    waits.append(pair_copy)
    d_query_rot = nn(d_scores16, key16)
    d_query16 = head_backward(
        d_query_rot, query_unit, query_inverse, qg, cos_query, sin_query
    ).astype(BF16)
    dq_all[t] = d_query16
    dq_copies = [to_peer(11, k, dq_all.at[t], dq_all.at[t]) for k in rest]
    query_rows = nn(
        last_hot_t.astype(F32), d_query16.astype(F32) * query_raw, EXACT
    )
    pair_copy.wait_recv()
    whole = jnp.where(even, d_key_rot, d_value) + pair_in[...].astype(F32)
    d_key_raw = head_backward(whole, key_unit, key_inverse, kg, cos_key, sin_key)
    column16 = jnp.where(even, d_key_raw, whole).astype(BF16)
    dkv_all[t] = column16
    dkv_copies = [to_peer(12, k, dkv_all.at[t], dkv_all.at[t]) for k in rest]
    raw = jnp.where(even, key_raw, value_raw)
    rows_all[t] = nt(
        jnp.ones((8, HD), F32), column16.astype(F32) * raw + query_rows, EXACT
    )
    row_copies = [to_peer(13, k, rows_all.at[t], rows_all.at[t]) for k in rest]
    landed(dq_copies)
    landed(dkv_copies)
    landed(row_copies)

    row_sums = rows_all[0]
    for s in slots[1:]:
        row_sums = row_sums + rows_all[s]
    out_copies = []
    for k, p in list(enumerate(peers)) + [(None, t)]:
        rows = pl.ds(pl.multiple_of(p * own, own), own)
        hit = iota((own, N), 1) == p * own + iota((own, N), 0)
        mean = jnp.sum(jnp.where(hit, row_sums[0:1, :], 0.0), axis=1, keepdims=True) / D
        last_here = onehot(
            (iota((own, S), 0) + p * own).astype(F32) == ends_row - 1.0
        )
        d_normed = nt(dkv_all[0, rows], wkv_all[0])
        for b in slots:
            if b > 0:
                d_normed = d_normed + nt(dkv_all[b, rows], wkv_all[b])
            d_normed = d_normed + nt(nn(last_here, dq_all[b]).astype(BF16), wq_all[b])
        inverse = inv_all[rows, 0:1]
        unit = hid_all[rows, :].astype(F32) * inverse
        grad = inverse * (d_normed * gain - unit * mean)
        grad = grad + nn(last_here, d_resid16) + nn(last_here, d_resid_low)
        out16[rows, :] = grad.astype(BF16)
        if k is None:
            local = pltpu.make_async_copy(out16.at[rows], out.at[:, columns], local_sem.at[5])
            local.start()
        else:
            out_copies.append(to_peer(14, k, out16.at[rows], out.at[:, columns]))
    landed(out_copies)
    local.wait()
    for copy in waits:
        copy.wait_send()


def on_device(
    tensors, groups,
    hidden, lengths, positives, negatives, in_gain, wq, wkv, q_gain, k_gain, wo, out_gain
):
    T, G = tensors, groups
    own, D = hidden.shape
    F = D // T
    HD = wq.shape[1]
    N = own * T
    S = lengths.shape[1]
    Q = positives.shape[0]
    Z = G // 2
    vmem = pl.BlockSpec(memory_space=pltpu.VMEM)
    anywhere = pl.BlockSpec(memory_space=pl.ANY)
    scratch = [
        pltpu.VMEM((own, D), BF16),
        pltpu.VMEM((N, F), BF16),
        pltpu.VMEM((N, HD), F32),
        pltpu.VMEM((N, F), BF16),
        pltpu.VMEM((T, F, HD), BF16),
        pltpu.VMEM((T, F, HD), BF16),
        pltpu.VMEM((T, HD, F), BF16),
        pltpu.VMEM((T, N, HD), BF16),
        pltpu.VMEM((T, 2, N, HD), BF16),
        pltpu.VMEM((T, S, HD), F32),
        pltpu.VMEM((T, S, HD), F32),
        pltpu.VMEM((T, S, HD), BF16),
        pltpu.VMEM((T, S, HD), F32),
        pltpu.VMEM((G * S, F), BF16),
        pltpu.VMEM((T, Q, G * S), F32),
        pltpu.VMEM((T, S, HD), F32),
        pltpu.VMEM((T, S, HD), F32),
        pltpu.VMEM((N, HD), BF16),
        pltpu.VMEM((N, HD), BF16),
        pltpu.VMEM((T, N, HD), BF16),
        pltpu.VMEM((T, S, HD), BF16),
        pltpu.VMEM((T, 8, N), F32),
        pltpu.VMEM((N, F), BF16),
        pltpu.SemaphoreType.DMA((6,)),
        pltpu.SemaphoreType.DMA((15, T - 1)),
        pltpu.SemaphoreType.DMA((15, T - 1)),
        pltpu.SemaphoreType.DMA((3, T - 1)),
        pltpu.SemaphoreType.DMA((3, T - 1)),
        pltpu.SemaphoreType.DMA((Z - 1,)),
        pltpu.SemaphoreType.DMA((Z - 1,)),
        pltpu.SemaphoreType.DMA((Z + 1,)),
        pltpu.SemaphoreType.DMA((Z + 1,)),
    ]
    d_hidden, loss = pl.pallas_call(
        functools.partial(kernel, T, G),
        out_shape=(
            jax.ShapeDtypeStruct((own, D), BF16),
            jax.ShapeDtypeStruct((8, 128), F32),
        ),
        in_specs=[
            anywhere, vmem, vmem, vmem, vmem, anywhere, anywhere, vmem, vmem, anywhere, vmem
        ],
        out_specs=(anywhere, vmem),
        scratch_shapes=scratch,
        compiler_params=pltpu.CompilerParams(
            collective_id=0, has_side_effects=True, vmem_limit_bytes=48 * 1024 * 1024
        ),
    )(
        hidden, lengths, positives.reshape(1, Q), negatives, in_gain.reshape(1, D), wq, wkv,
        q_gain.reshape(1, HD), k_gain.reshape(1, HD), wo, out_gain.reshape(1, D),
    )
    return d_hidden, loss[0, 0]


def solution(mesh):
    placed = (
        P(("dp", "tensor"), None),
        P("dp", None),
        P(),
        P(),
        P(),
        P(None, "tensor"),
        P(None, "tensor"),
        P(),
        P(),
        P("tensor", None),
        P(),
    )
    return jax.shard_map(
        functools.partial(on_device, mesh.shape["tensor"], mesh.shape["dp"]),
        mesh=mesh,
        in_specs=placed,
        out_specs=(P(("dp", "tensor"), None), P()),
        check_vma=False,
    )
```

```python
import functools
import math

import jax
import jax.numpy as jnp
from jax import lax
from jax.experimental import pallas as pl
from jax.experimental.pallas import tpu as pltpu
from jax.sharding import PartitionSpec as P

QDEV = 8
EPSILON = 1e-06
SOFTMAX_TEMPER = 0.05
LOSS_MULTIPLIER = 8192.0
ROPE_BASE = 1000000.0

F32 = jnp.float32
BF16 = jnp.bfloat16
MESH = pl.DeviceIdType.MESH
EXACT = lax.Precision.HIGHEST


def nn(a, b, precision=None):
    return jnp.dot(a, b, preferred_element_type=F32, precision=precision)


def nt(a, b, precision=None):
    dims = (((1,), (1,)), ((), ()))
    return lax.dot_general(a, b, dims, preferred_element_type=F32, precision=precision)


def iota(shape, axis):
    return lax.broadcasted_iota(jnp.int32, shape, axis)


def onehot(mask, kind=BF16):
    return jnp.where(mask, 1.0, 0.0).astype(F32).astype(kind)


def rms_scale(x):
    return lax.rsqrt(jnp.mean(x * x, axis=-1, keepdims=True) + EPSILON)


def rope_tables(position, width):
    half = width // 2
    lane = iota((1, width), 1)
    lane = jnp.where(lane >= half, lane - half, lane).astype(F32)
    frequency = jnp.exp(lane * (-2.0 / width * math.log(ROPE_BASE)))
    angles = position * frequency
    return jnp.cos(angles), jnp.sin(angles)


def rotate(x, cosine, sine):
    half = x.shape[-1] // 2
    sign = jnp.where(iota((1, x.shape[-1]), 1) < half, -1.0, 1.0)
    return x * cosine + pltpu.roll(x, half, 1) * sign * sine


def head_forward(raw, gain, cosine, sine):
    inverse = rms_scale(raw)
    unit = raw * inverse
    return unit, inverse, rotate(unit * gain, cosine, sine)


def head_backward(grad, unit, inverse, gain, cosine, sine):
    scaled = rotate(grad, cosine, -sine) * gain
    return inverse * (scaled - unit * jnp.mean(unit * scaled, axis=-1, keepdims=True))


def kernel(
    tensors, groups,
    hidden, lens, positives, negatives, in_gain, wq, wkv, q_gain, k_gain, wo, out_gain,
    out, loss,
    hid_own, hid_all, inv_rows, inv_all, normed, wkv_all, wq_all, wo_all,
    kvp_out, kvp_in, qp_out, qp_in, attn_all, embeds, logit_all,
    dap_out, dap_in, pair_out, pair_in, dkv_all, dq_all, rows_all, out16,
    local_sem, tsend, trecv, fsend, frecv, zsend, zrecv, psend, precv,
):
    T, G = tensors, groups
    Z = G // 2
    own, D = hidden.shape
    F = D // T
    HD = wq.shape[1]
    N = own * T
    S = lens.shape[1]
    Q = positives.shape[1]
    H = F // 2
    HH = HD // 2
    root = math.sqrt(HD)
    t = lax.axis_index("tensor")
    g = lax.axis_index("dp")
    zz = g // 2
    core = g % 2
    buddy = g + 1 - 2 * core
    mate = t + 1 - 2 * (t % 2)
    even = t % 2 == 0
    peers = [lax.rem(t + k, T) for k in range(1, T)]
    sources = [lax.rem(t + T - k, T) for k in range(1, T)]
    slots = list(range(T))
    columns = pl.ds(pl.multiple_of(t * F, 128), F)

    own_copies = [
        pltpu.make_async_copy(hidden, hid_own, local_sem.at[0]),
        pltpu.make_async_copy(
            hidden.at[:, columns], hid_all.at[pl.ds(t * own, own)], local_sem.at[1]
        ),
        pltpu.make_async_copy(wkv.at[pl.ds(t * F, F)], wkv_all.at[t], local_sem.at[2]),
        pltpu.make_async_copy(wq.at[pl.ds(t * F, F)], wq_all.at[t], local_sem.at[3]),
        pltpu.make_async_copy(wo.at[:, columns], wo_all.at[t], local_sem.at[4]),
    ]
    for copy in own_copies:
        copy.start()

    barrier = pltpu.get_barrier_semaphore()
    for p in peers:
        pl.semaphore_signal(barrier, inc=1, device_id=(g, p), device_id_type=MESH)
    for k in range(1, Z):
        far = lax.rem(zz + k, Z) * 2 + core
        pl.semaphore_signal(barrier, inc=1, device_id=(far, t), device_id_type=MESH)
    pl.semaphore_signal(barrier, inc=1, device_id=(buddy, t), device_id_type=MESH)
    pl.semaphore_wait(barrier, T - 1 + Z - 1 + 1)

    waits = []

    def to_peer(kind, k, src, dst):
        copy = pltpu.make_async_remote_copy(
            src_ref=src, dst_ref=dst, send_sem=tsend.at[kind, k], recv_sem=trecv.at[kind, k],
            device_id=(g, peers[k]), device_id_type=MESH,
        )
        copy.start()
        waits.append(copy)
        return copy

    def to_buddy(kind, k, src, dst):
        copy = pltpu.make_async_remote_copy(
            src_ref=src, dst_ref=dst, send_sem=fsend.at[kind, k], recv_sem=frecv.at[kind, k],
            device_id=(buddy, t), device_id_type=MESH,
        )
        copy.start()
        waits.append(copy)
        return copy

    def landed(copies):
        for copy in copies:
            copy.wait_recv()

    rest = range(T - 1)
    my_rows = pl.ds(pl.multiple_of(t * own, own), own)

    def cols(p):
        return pl.ds(pl.multiple_of(p * F, 128), F)

    hid_copies = [
        to_peer(0, k, hidden.at[:, cols(peers[k])], hid_all.at[my_rows]) for k in rest
    ]

    def half_rows(p):
        return pl.ds(pl.multiple_of(p * F + core * H, H), H)

    my_half = pl.ds(pl.multiple_of(core * H, H), H)
    my_head_half = pl.ds(pl.multiple_of(core * HH, HH), HH)
    wkv_copies = [
        to_peer(1, k, wkv.at[half_rows(peers[k])], wkv_all.at[t, my_half]) for k in rest
    ]

    own_copies[0].wait()
    mine = hid_own[...].astype(F32)
    diagonal = iota((own, HD), 0) == iota((own, HD), 1)
    inv_rows[t] = jnp.broadcast_to(
        jnp.sum(jnp.where(diagonal, rms_scale(mine), 0.0), axis=0, keepdims=True), (8, HD)
    )
    inv_copies = [to_peer(2, k, inv_rows.at[t], inv_rows.at[t]) for k in rest]

    lens_row = lens[...].astype(F32)
    square_r, square_c = iota((S, S), 0), iota((S, S), 1)
    lens_col = jnp.sum(jnp.where(square_r == square_c, lens_row, 0.0), axis=1, keepdims=True)
    ends_col = jnp.sum(jnp.where(square_c <= square_r, lens_row, 0.0), axis=1, keepdims=True)
    ends_row = jnp.sum(jnp.where(square_r <= square_c, lens_col, 0.0), axis=0, keepdims=True)
    starts_col, starts_row = ends_col - lens_col, ends_row - lens_row
    token_row = iota((S, N), 1).astype(F32)
    token_col = iota((N, S), 0).astype(F32)
    inside = (token_row >= starts_col) & (token_row < ends_col)
    inside_t = (token_col >= starts_row) & (token_col < ends_row)
    offset = jnp.sum(jnp.where(inside_t, starts_row, 0.0), axis=1, keepdims=True)
    position = iota((N, 1), 0).astype(F32) - offset
    last_hot = onehot(token_row == ends_col - 1.0)
    last_hot_t = onehot(token_col == ends_row - 1.0)
    cos_key, sin_key = rope_tables(position, HD)
    cos_query, sin_query = rope_tables(lens_col - 1.0, HD)
    qg, kg = q_gain[...], k_gain[...]
    shift = root * jnp.max(qg, axis=1, keepdims=True) * jnp.max(kg, axis=1, keepdims=True)
    gain = in_gain[:, columns]
    ogain = out_gain[:, columns]

    wkv_fwd = []
    for k in rest:
        wkv_copies[k].wait_recv()
        spot = wkv_all.at[sources[k], my_half]
        wkv_fwd.append(to_buddy(0, k, spot, spot))
    wq_copies = [
        to_peer(3, k, wq.at[half_rows(peers[k])], wq_all.at[t, my_half]) for k in rest
    ]

    own_copies[1].wait()
    landed(hid_copies)
    landed(inv_copies)
    for s in slots:
        rows = slice(s * own, (s + 1) * own)
        inverse = jnp.sum(
            jnp.where(diagonal, inv_rows[s, 0:1, :], 0.0), axis=1, keepdims=True
        )
        inv_all[rows, :] = jnp.broadcast_to(inverse, (own, HD))
        normed[rows, :] = (hid_all[rows, :].astype(F32) * inverse * gain).astype(BF16)
    own_copies[2].wait()
    landed(wkv_fwd)
    for b in slots:
        kvp_out[b] = nn(normed[...], wkv_all[b]).astype(BF16)

    def pair(p):
        return pl.ds((p // 2) * 2, 2)

    kvp_copies = [to_peer(4, k, kvp_out.at[pair(peers[k])], kvp_in.at[t]) for k in rest]
    kvp_in[t] = kvp_out[pair(t)]

    wq_fwd = []
    for k in rest:
        wq_copies[k].wait_recv()
        spot = wq_all.at[sources[k], my_half]
        wq_fwd.append(to_buddy(1, k, spot, spot))
    wo_copies = [
        to_peer(
            5, k, wo.at[my_head_half, cols(peers[k])], wo_all.at[t, my_head_half]
        )
        for k in rest
    ]
    last16 = nn(last_hot, normed[...]).astype(BF16)
    hid_last = nn(last_hot, hid_all[...])
    own_copies[3].wait()
    landed(wq_fwd)
    for b in slots:
        qp_out[b] = nn(last16, wq_all[b])
    qp_copies = [to_peer(6, k, qp_out.at[peers[k]], qp_in.at[t]) for k in rest]
    qp_in[t] = qp_out[t]

    landed(kvp_copies)
    key_raw = kvp_in[0, 0].astype(F32)
    value_raw = kvp_in[0, 1].astype(F32)
    for s in slots[1:]:
        key_raw = key_raw + kvp_in[s, 0].astype(F32)
        value_raw = value_raw + kvp_in[s, 1].astype(F32)
    value16 = value_raw.astype(BF16)
    key_unit, key_inverse, key_rot = head_forward(key_raw, kg, cos_key, sin_key)
    key16 = key_rot.astype(BF16)

    landed(qp_copies)
    query_raw = qp_in[0]
    for s in slots[1:]:
        query_raw = query_raw + qp_in[s]
    query_unit, query_inverse, query_rot = head_forward(query_raw, qg, cos_query, sin_query)
    query16 = query_rot.astype(BF16)
    scores = nt(query16, key16) / root
    weight = jnp.where(inside, jnp.exp(scores - shift), 0.0)
    probs = weight / jnp.sum(weight, axis=-1, keepdims=True)
    probs16 = probs.astype(BF16)
    attn_all[t] = nn(probs16, value16).astype(BF16)
    attn_copies = [to_peer(7, k, attn_all.at[t], attn_all.at[t]) for k in rest]

    wo_fwd = []
    for k in rest:
        wo_copies[k].wait_recv()
        spot = wo_all.at[sources[k], my_head_half]
        wo_fwd.append(to_buddy(2, k, spot, spot))
    own_copies[4].wait()
    landed(wo_fwd)
    landed(attn_copies)

    resid = hid_last
    for s in slots:
        resid = resid + nn(attn_all[s], wo_all[s])
    my_seqs = pl.ds(pl.multiple_of(g * S, S), S)
    embeds[my_seqs, :] = (resid * ogain).astype(BF16)
    z_copies = []
    for k in range(1, Z):
        far = lax.rem(zz + k, Z) * 2 + core
        copy = pltpu.make_async_remote_copy(
            src_ref=embeds.at[my_seqs], dst_ref=embeds.at[my_seqs],
            send_sem=zsend.at[k - 1], recv_sem=zrecv.at[k - 1],
            device_id=(far, t), device_id_type=MESH,
        )
        copy.start()
        waits.append(copy)
        z_copies.append(copy)

    def chip_copy(index, spot):
        copy = pltpu.make_async_remote_copy(
            src_ref=spot, dst_ref=spot, send_sem=psend.at[index], recv_sem=precv.at[index],
            device_id=(buddy, t), device_id_type=MESH,
        )
        copy.start()
        waits.append(copy)
        return copy

    shared = [chip_copy(0, embeds.at[my_seqs])]

    E = G * S
    seq_of = iota((1, E), 1) % S
    passage = jnp.where(seq_of >= QDEV, (iota((1, E), 1) // S) * (S - QDEV) + seq_of - QDEV, -1)
    eye_q = iota((Q, Q), 0) == iota((Q, Q), 1)

    def chosen(row):
        column = jnp.sum(jnp.where(eye_q, row.astype(F32), 0.0), axis=1, keepdims=True)
        return column.astype(jnp.int32) == passage

    pos_hot = chosen(positives[...])
    hard = chosen(negatives[0:1, :])
    for j in range(1, negatives.shape[0]):
        hard = hard | chosen(negatives[j : j + 1, :])
    positive_f = jnp.where(pos_hot, 1.0, 0.0)
    allowed = (jnp.max(positive_f, axis=0, keepdims=True) > 0.5) | hard
    q_id = iota((Q, E), 0)
    pick = iota((Q, E), 1) == (q_id // QDEV) * S + q_id % QDEV
    pick_q = onehot(pick)
    eye_e = iota((E, E), 0) == iota((E, E), 1)
    row_s = iota((S, Q), 0)
    own_q = (row_s < QDEV) & (iota((S, Q), 1) == g * QDEV + row_s)
    own_p = iota((S, E), 1) == g * S + iota((S, E), 0)

    for k in range(1, Z):
        z_copies[k - 1].wait_recv()
        origin = lax.rem(zz + Z - k, Z) * 2 + core
        shared.append(chip_copy(k, embeds.at[pl.ds(pl.multiple_of(origin * S, S), S)]))
    landed(shared)

    queries = nn(pick_q, embeds[...]).astype(BF16)
    plain = (embeds[...].astype(F32) * (1.0 / ogain)).astype(BF16)
    plain_sq = jnp.sum(jnp.where(eye_e, nt(plain, plain), 0.0), axis=0, keepdims=True)
    scaled_sq = jnp.sum(
        jnp.where(eye_e, nt(embeds[...], embeds[...]), 0.0), axis=0, keepdims=True
    )
    logit_all[t, 0:Q] = nt(queries, embeds[...])
    logit_all[t, Q : Q + 8] = jnp.where(iota((8, E), 0) == 0, plain_sq, scaled_sq)
    logit_copies = [to_peer(9, k, logit_all.at[t], logit_all.at[t]) for k in rest]
    landed(logit_copies)
    summed = logit_all[0]
    for s in slots[1:]:
        summed = summed + logit_all[s]
    raw_dots = summed[0:Q]
    inverse_row = lax.rsqrt(summed[Q : Q + 1] / D + EPSILON)
    final_row = lax.rsqrt(inverse_row * inverse_row * summed[Q + 1 : Q + 2] + EPSILON)
    scale_row = inverse_row * final_row
    scale_q = jnp.sum(jnp.where(pick, scale_row, 0.0), axis=1, keepdims=True)
    resid_inverse = jnp.sum(jnp.where(own_p, inverse_row, 0.0), axis=1, keepdims=True)
    final_inverse = jnp.sum(jnp.where(own_p, final_row, 0.0), axis=1, keepdims=True)
    resid_unit = resid * resid_inverse
    embed = resid_unit * ogain * final_inverse
    dots_q, dots_p = raw_dots * scale_q, raw_dots * scale_row
    logits = dots_q * scale_row / SOFTMAX_TEMPER
    grown = jnp.where(allowed, jnp.exp(logits - 1.0 / SOFTMAX_TEMPER), 0.0)
    totals = jnp.sum(grown, axis=1, keepdims=True)
    target = jnp.sum(jnp.where(pos_hot, logits, 0.0), axis=1, keepdims=True)
    each = jnp.log(totals) + 1.0 / SOFTMAX_TEMPER - target
    loss[0, 0] = jnp.sum(each) / Q
    factor = LOSS_MULTIPLIER / (Q * SOFTMAX_TEMPER)
    coef = factor * (grown / totals - positive_f)
    coef_q16 = (coef * scale_row).astype(BF16)
    coef_p16 = (coef * scale_q).astype(BF16)
    coef_q = nn(onehot(own_q), coef_q16).astype(BF16)
    coef_p = nt(onehot(own_p), coef_p16).astype(BF16)
    d_embed = nn(coef_q, embeds[...]) + nn(coef_p, queries)
    along_q = coef_q16.astype(F32) * dots_q
    along_p = coef_p16.astype(F32) * dots_p
    inner = jnp.sum(nn(onehot(own_q, F32), along_q, EXACT), axis=1, keepdims=True) + jnp.sum(
        nt(onehot(own_p, F32), along_p, EXACT), axis=1, keepdims=True
    )
    d_final = final_inverse * (d_embed - embed * inner)
    middle = inner * (EPSILON / D) * final_inverse * final_inverse
    d_resid = resid_inverse * (ogain * d_final - resid_unit * middle)
    d_resid16 = d_resid.astype(BF16)
    d_resid_low = (d_resid - d_resid16.astype(F32)).astype(BF16)

    for b in slots:
        dap_out[b] = nt(d_resid16, wo_all[b])
    dap_copies = [to_peer(10, k, dap_out.at[peers[k]], dap_in.at[t]) for k in rest]
    dap_in[t] = dap_out[t]
    eye_n = iota((N, N), 0) == iota((N, N), 1)
    eye16 = onehot(eye_n)
    probs16_t = nt(eye16, probs16).astype(BF16)
    landed(dap_copies)
    d_attn = dap_in[0]
    for s in slots[1:]:
        d_attn = d_attn + dap_in[s]
    d_attn16 = d_attn.astype(BF16)
    d_probs = nt(d_attn16, value16)
    d_scores16 = (
        probs * (d_probs - jnp.sum(probs * d_probs, axis=-1, keepdims=True)) / root
    ).astype(BF16)
    d_key_rot = nn(nt(eye16, d_scores16).astype(BF16), query16)
    d_value = nn(probs16_t, d_attn16)
    pair_out[...] = jnp.where(even, d_value, d_key_rot).astype(BF16)
    pair_copy = pltpu.make_async_remote_copy(
        src_ref=pair_out, dst_ref=pair_in, send_sem=psend.at[Z], recv_sem=precv.at[Z],
        device_id=(g, mate), device_id_type=MESH,
    )
    pair_copy.start()
    waits.append(pair_copy)
    d_query_rot = nn(d_scores16, key16)
    d_query16 = head_backward(
        d_query_rot, query_unit, query_inverse, qg, cos_query, sin_query
    ).astype(BF16)
    dq_all[t] = d_query16
    dq_copies = [to_peer(11, k, dq_all.at[t], dq_all.at[t]) for k in rest]
    query_rows = nn(
        last_hot_t.astype(F32), d_query16.astype(F32) * query_raw, EXACT
    )
    pair_copy.wait_recv()
    whole = jnp.where(even, d_key_rot, d_value) + pair_in[...].astype(F32)
    d_key_raw = head_backward(whole, key_unit, key_inverse, kg, cos_key, sin_key)
    column16 = jnp.where(even, d_key_raw, whole).astype(BF16)
    dkv_all[t] = column16
    dkv_copies = [to_peer(12, k, dkv_all.at[t], dkv_all.at[t]) for k in rest]
    raw = jnp.where(even, key_raw, value_raw)
    rows_all[t] = nt(
        jnp.ones((8, HD), F32), column16.astype(F32) * raw + query_rows, EXACT
    )
    row_copies = [to_peer(13, k, rows_all.at[t], rows_all.at[t]) for k in rest]
    landed(dq_copies)
    landed(dkv_copies)
    landed(row_copies)

    row_sums = rows_all[0]
    for s in slots[1:]:
        row_sums = row_sums + rows_all[s]
    out_copies = []
    for k, p in list(enumerate(peers)) + [(None, t)]:
        rows = pl.ds(pl.multiple_of(p * own, own), own)
        hit = iota((own, N), 1) == p * own + iota((own, N), 0)
        mean = jnp.sum(jnp.where(hit, row_sums[0:1, :], 0.0), axis=1, keepdims=True) / D
        last_here = onehot(
            (iota((own, S), 0) + p * own).astype(F32) == ends_row - 1.0
        )
        d_normed = nt(dkv_all[0, rows], wkv_all[0])
        for b in slots:
            if b > 0:
                d_normed = d_normed + nt(dkv_all[b, rows], wkv_all[b])
            d_normed = d_normed + nt(nn(last_here, dq_all[b]).astype(BF16), wq_all[b])
        inverse = inv_all[rows, 0:1]
        unit = hid_all[rows, :].astype(F32) * inverse
        grad = inverse * (d_normed * gain - unit * mean)
        grad = grad + nn(last_here, d_resid16) + nn(last_here, d_resid_low)
        out16[rows, :] = grad.astype(BF16)
        if k is None:
            local = pltpu.make_async_copy(out16.at[rows], out.at[:, columns], local_sem.at[5])
            local.start()
        else:
            out_copies.append(to_peer(14, k, out16.at[rows], out.at[:, columns]))
    landed(out_copies)
    local.wait()
    for copy in waits:
        copy.wait_send()


def on_device(
    tensors, groups,
    hidden, lengths, positives, negatives, in_gain, wq, wkv, q_gain, k_gain, wo, out_gain
):
    T, G = tensors, groups
    own, D = hidden.shape
    F = D // T
    HD = wq.shape[1]
    N = own * T
    S = lengths.shape[1]
    Q = positives.shape[0]
    Z = G // 2
    vmem = pl.BlockSpec(memory_space=pltpu.VMEM)
    anywhere = pl.BlockSpec(memory_space=pl.ANY)
    scratch = [
        pltpu.VMEM((own, D), BF16),
        pltpu.VMEM((N, F), BF16),
        pltpu.VMEM((T, 8, HD), F32),
        pltpu.VMEM((N, HD), F32),
        pltpu.VMEM((N, F), BF16),
        pltpu.VMEM((T, F, HD), BF16),
        pltpu.VMEM((T, F, HD), BF16),
        pltpu.VMEM((T, HD, F), BF16),
        pltpu.VMEM((T, N, HD), BF16),
        pltpu.VMEM((T, 2, N, HD), BF16),
        pltpu.VMEM((T, S, HD), F32),
        pltpu.VMEM((T, S, HD), F32),
        pltpu.VMEM((T, S, HD), BF16),
        pltpu.VMEM((G * S, F), BF16),
        pltpu.VMEM((T, Q + 8, G * S), F32),
        pltpu.VMEM((T, S, HD), F32),
        pltpu.VMEM((T, S, HD), F32),
        pltpu.VMEM((N, HD), BF16),
        pltpu.VMEM((N, HD), BF16),
        pltpu.VMEM((T, N, HD), BF16),
        pltpu.VMEM((T, S, HD), BF16),
        pltpu.VMEM((T, 8, N), F32),
        pltpu.VMEM((N, F), BF16),
        pltpu.SemaphoreType.DMA((6,)),
        pltpu.SemaphoreType.DMA((15, T - 1)),
        pltpu.SemaphoreType.DMA((15, T - 1)),
        pltpu.SemaphoreType.DMA((3, T - 1)),
        pltpu.SemaphoreType.DMA((3, T - 1)),
        pltpu.SemaphoreType.DMA((Z - 1,)),
        pltpu.SemaphoreType.DMA((Z - 1,)),
        pltpu.SemaphoreType.DMA((Z + 1,)),
        pltpu.SemaphoreType.DMA((Z + 1,)),
    ]
    d_hidden, loss = pl.pallas_call(
        functools.partial(kernel, T, G),
        out_shape=(
            jax.ShapeDtypeStruct((own, D), BF16),
            jax.ShapeDtypeStruct((1, 1), F32),
        ),
        in_specs=[
            anywhere, vmem, vmem, vmem, vmem, anywhere, anywhere, vmem, vmem, anywhere, vmem
        ],
        out_specs=(anywhere, pl.BlockSpec(memory_space=pltpu.SMEM)),
        scratch_shapes=scratch,
        compiler_params=pltpu.CompilerParams(
            collective_id=0, has_side_effects=True, vmem_limit_bytes=60 * 1024 * 1024
        ),
    )(
        hidden, lengths, positives.reshape(1, Q), negatives.T, in_gain.reshape(1, D), wq, wkv,
        q_gain.reshape(1, HD), k_gain.reshape(1, HD), wo, out_gain.reshape(1, D),
    )
    return d_hidden, loss.reshape(())


def solution(mesh):
    placed = (
        P(("dp", "tensor"), None),
        P("dp", None),
        P(),
        P(),
        P(),
        P(None, "tensor"),
        P(None, "tensor"),
        P(),
        P(),
        P("tensor", None),
        P(),
    )
    return jax.shard_map(
        functools.partial(on_device, mesh.shape["tensor"], mesh.shape["dp"]),
        mesh=mesh,
        in_specs=placed,
        out_specs=(P(("dp", "tensor"), None), P()),
        check_vma=False,
    )
```

```python
import functools
import math

import jax
import jax.numpy as jnp
from jax import lax
from jax.experimental import pallas as pl
from jax.experimental.pallas import tpu as pltpu
from jax.sharding import PartitionSpec as P

QDEV = 8
EPSILON = 1e-06
SOFTMAX_TEMPER = 0.05
LOSS_MULTIPLIER = 8192.0
ROPE_BASE = 1000000.0

F32 = jnp.float32
BF16 = jnp.bfloat16
MESH = pl.DeviceIdType.MESH
EXACT = lax.Precision.HIGHEST


def nn(a, b, precision=None):
    return jnp.dot(a, b, preferred_element_type=F32, precision=precision)


def nt(a, b, precision=None):
    dims = (((1,), (1,)), ((), ()))
    return lax.dot_general(a, b, dims, preferred_element_type=F32, precision=precision)


def iota(shape, axis):
    return lax.broadcasted_iota(jnp.int32, shape, axis)


def onehot(mask, kind=BF16):
    return jnp.where(mask, 1.0, 0.0).astype(F32).astype(kind)


def rms_scale(x):
    return lax.rsqrt(jnp.mean(x * x, axis=-1, keepdims=True) + EPSILON)


def rope_tables(position, width):
    half = width // 2
    lane = iota((1, width), 1)
    lane = jnp.where(lane >= half, lane - half, lane).astype(F32)
    frequency = jnp.exp(lane * (-2.0 / width * math.log(ROPE_BASE)))
    angles = position * frequency
    return jnp.cos(angles), jnp.sin(angles)


def rotate(x, cosine, sine):
    half = x.shape[-1] // 2
    sign = jnp.where(iota((1, x.shape[-1]), 1) < half, -1.0, 1.0)
    return x * cosine + pltpu.roll(x, half, 1) * sign * sine


def head_forward(raw, gain, cosine, sine):
    inverse = rms_scale(raw)
    unit = raw * inverse
    return unit, inverse, rotate(unit * gain, cosine, sine)


def head_backward(grad, unit, inverse, gain, cosine, sine):
    scaled = rotate(grad, cosine, -sine) * gain
    return inverse * (scaled - unit * jnp.mean(unit * scaled, axis=-1, keepdims=True))


def kernel(
    tensors, groups,
    hidden, lens, positives, negatives, in_gain, wq, wkv, q_gain, k_gain, wo, out_gain,
    out, loss,
    hid_own, hid_all, inv_rows, inv_all, normed, wkv_all, wq_all, wo_all,
    kvp_out, kvp_in, qp_out, qp_in, attn_all, embeds, logit_all,
    dap_out, dap_in, pair_out, pair_in, dkv_all, dq_all, rows_all, out16,
    local_sem, tsend, trecv, fsend, frecv, zsend, zrecv, psend, precv,
):
    T, G = tensors, groups
    Z = G // 2
    own, D = hidden.shape
    F = D // T
    HD = wq.shape[1]
    N = own * T
    S = lens.shape[1]
    Q = positives.shape[1]
    H = F // 4
    HH = HD // 4
    root = math.sqrt(HD)
    t = lax.axis_index("tensor")
    g = lax.axis_index("dp")
    zz = g // 2
    core = g % 2
    buddy = g + 1 - 2 * core
    mate = t + 1 - 2 * (t % 2)
    z_mate = (zz + 1 - 2 * (zz % 2)) * 2 + core
    quarter = (zz % 2) * 2 + core
    far_quarter = (1 - zz % 2) * 2 + core
    even = t % 2 == 0
    peers = [lax.rem(t + k, T) for k in range(1, T)]
    sources = [lax.rem(t + T - k, T) for k in range(1, T)]
    slots = list(range(T))
    columns = pl.ds(pl.multiple_of(t * F, 128), F)

    def block(p):
        return pl.ds(pl.multiple_of(p * HD, 128), HD)

    own_copies = [
        pltpu.make_async_copy(hidden, hid_own, local_sem.at[0]),
        pltpu.make_async_copy(
            hidden.at[:, columns], hid_all.at[pl.ds(t * own, own)], local_sem.at[1]
        ),
        pltpu.make_async_copy(wkv.at[pl.ds(t * F, F)], wkv_all.at[:, block(t)], local_sem.at[2]),
        pltpu.make_async_copy(wq.at[pl.ds(t * F, F)], wq_all.at[:, block(t)], local_sem.at[3]),
        pltpu.make_async_copy(wo.at[:, columns], wo_all.at[block(t)], local_sem.at[4]),
    ]
    for copy in own_copies:
        copy.start()

    barrier = pltpu.get_barrier_semaphore()
    for p in peers:
        pl.semaphore_signal(barrier, inc=1, device_id=(g, p), device_id_type=MESH)
    for k in range(1, Z):
        far = lax.rem(zz + k, Z) * 2 + core
        pl.semaphore_signal(barrier, inc=1, device_id=(far, t), device_id_type=MESH)
    pl.semaphore_signal(barrier, inc=1, device_id=(buddy, t), device_id_type=MESH)
    pl.semaphore_wait(barrier, T - 1 + Z - 1 + 1)

    waits = []

    def to_peer(kind, k, src, dst):
        copy = pltpu.make_async_remote_copy(
            src_ref=src, dst_ref=dst, send_sem=tsend.at[kind, k], recv_sem=trecv.at[kind, k],
            device_id=(g, peers[k]), device_id_type=MESH,
        )
        copy.start()
        waits.append(copy)
        return copy

    def pass_on(kind, k, spot, target):
        copy = pltpu.make_async_remote_copy(
            src_ref=spot, dst_ref=spot, send_sem=fsend.at[kind, k], recv_sem=frecv.at[kind, k],
            device_id=(target, t), device_id_type=MESH,
        )
        copy.start()
        waits.append(copy)
        return copy

    def landed(copies):
        for copy in copies:
            copy.wait_recv()

    rest = range(T - 1)
    my_rows = pl.ds(pl.multiple_of(t * own, own), own)

    def cols(p):
        return pl.ds(pl.multiple_of(p * F, 128), F)

    def tall_spot(ref):
        def spot(source, part):
            return ref.at[pl.ds(pl.multiple_of(part * H, H), H), block(source)]

        return spot

    def wide_spot(source, part):
        return wo_all.at[pl.ds(pl.multiple_of(source * HD + part * HH, HH), HH)]

    def own_tall(ref, p):
        return ref.at[pl.ds(pl.multiple_of(p * F + quarter * H, H), H)]

    def own_wide(p):
        return wo.at[pl.ds(pl.multiple_of(quarter * HH, HH), HH), cols(p)]

    def spread(kind, fetched, spot):
        near, along = [], []
        for k in rest:
            fetched[k].wait_recv()
            mine = spot(sources[k], quarter)
            along.append(pass_on(kind, k, mine, z_mate))
            near.append(pass_on(kind + 1, k, mine, buddy))
        for k in rest:
            along[k].wait_recv()
            near.append(pass_on(kind + 2, k, spot(sources[k], far_quarter), buddy))
        return near

    wkv_spot, wq_spot = tall_spot(wkv_all), tall_spot(wq_all)
    wkv_copies = [
        to_peer(1, k, own_tall(wkv, peers[k]), wkv_spot(t, quarter)) for k in rest
    ]
    hid_copies = [
        to_peer(0, k, hidden.at[:, cols(peers[k])], hid_all.at[my_rows]) for k in rest
    ]

    own_copies[0].wait()
    mine = hid_own[...].astype(F32)
    diagonal = iota((own, HD), 0) == iota((own, HD), 1)
    inv_rows[t] = jnp.broadcast_to(
        jnp.sum(jnp.where(diagonal, rms_scale(mine), 0.0), axis=0, keepdims=True), (8, HD)
    )
    inv_copies = [to_peer(2, k, inv_rows.at[t], inv_rows.at[t]) for k in rest]

    lens_row = lens[...].astype(F32)
    square_r, square_c = iota((S, S), 0), iota((S, S), 1)
    lens_col = jnp.sum(jnp.where(square_r == square_c, lens_row, 0.0), axis=1, keepdims=True)
    ends_col = jnp.sum(jnp.where(square_c <= square_r, lens_row, 0.0), axis=1, keepdims=True)
    ends_row = jnp.sum(jnp.where(square_r <= square_c, lens_col, 0.0), axis=0, keepdims=True)
    starts_col, starts_row = ends_col - lens_col, ends_row - lens_row
    token_row = iota((S, N), 1).astype(F32)
    token_col = iota((N, S), 0).astype(F32)
    inside = (token_row >= starts_col) & (token_row < ends_col)
    inside_t = (token_col >= starts_row) & (token_col < ends_row)
    offset = jnp.sum(jnp.where(inside_t, starts_row, 0.0), axis=1, keepdims=True)
    position = iota((N, 1), 0).astype(F32) - offset
    last_hot = onehot(token_row == ends_col - 1.0)
    last_hot_t = onehot(token_col == ends_row - 1.0)
    cos_key, sin_key = rope_tables(position, HD)
    cos_query, sin_query = rope_tables(lens_col - 1.0, HD)
    qg, kg = q_gain[...], k_gain[...]
    shift = root * jnp.max(qg, axis=1, keepdims=True) * jnp.max(kg, axis=1, keepdims=True)
    gain = in_gain[:, columns]
    ogain = out_gain[:, columns]

    wkv_near = spread(0, wkv_copies, wkv_spot)
    wq_copies = [to_peer(3, k, own_tall(wq, peers[k]), wq_spot(t, quarter)) for k in rest]

    own_copies[1].wait()
    landed(hid_copies)
    landed(inv_copies)
    for s in slots:
        rows = slice(s * own, (s + 1) * own)
        inverse = jnp.sum(
            jnp.where(diagonal, inv_rows[s, 0:1, :], 0.0), axis=1, keepdims=True
        )
        inv_all[rows, :] = jnp.broadcast_to(inverse, (own, HD))
        normed[rows, :] = (hid_all[rows, :].astype(F32) * inverse * gain).astype(BF16)
    own_copies[2].wait()
    landed(wkv_near)
    kvp_out[...] = nn(normed[...], wkv_all[...]).astype(BF16)

    def pair(p):
        return pl.ds(pl.multiple_of((p // 2) * (2 * HD), 256), 2 * HD)

    kvp_copies = [
        to_peer(4, k, kvp_out.at[:, pair(peers[k])], kvp_in.at[t]) for k in rest
    ]
    kvp_in[t] = kvp_out[:, pair(t)]

    wq_near = spread(3, wq_copies, wq_spot)
    wo_copies = [to_peer(5, k, own_wide(peers[k]), wide_spot(t, quarter)) for k in rest]
    last16 = nn(last_hot, normed[...]).astype(BF16)
    hid_last = nn(last_hot, hid_all[...])
    own_copies[3].wait()
    landed(wq_near)
    qp_out[...] = nn(last16, wq_all[...])
    qp_copies = [to_peer(6, k, qp_out.at[:, block(peers[k])], qp_in.at[t]) for k in rest]
    qp_in[t] = qp_out[:, block(t)]

    landed(kvp_copies)
    key_raw = kvp_in[0, :, 0:HD].astype(F32)
    value_raw = kvp_in[0, :, HD : 2 * HD].astype(F32)
    for s in slots[1:]:
        key_raw = key_raw + kvp_in[s, :, 0:HD].astype(F32)
        value_raw = value_raw + kvp_in[s, :, HD : 2 * HD].astype(F32)
    value16 = value_raw.astype(BF16)
    key_unit, key_inverse, key_rot = head_forward(key_raw, kg, cos_key, sin_key)
    key16 = key_rot.astype(BF16)

    landed(qp_copies)
    query_raw = qp_in[0]
    for s in slots[1:]:
        query_raw = query_raw + qp_in[s]
    query_unit, query_inverse, query_rot = head_forward(query_raw, qg, cos_query, sin_query)
    query16 = query_rot.astype(BF16)
    scores = nt(query16, key16) / root
    weight = jnp.where(inside, jnp.exp(scores - shift), 0.0)
    probs = weight / jnp.sum(weight, axis=-1, keepdims=True)
    probs16 = probs.astype(BF16)
    attn_all[:, block(t)] = nn(probs16, value16).astype(BF16)
    my_attn = attn_all.at[:, block(t)]
    attn_copies = [to_peer(7, k, my_attn, my_attn) for k in rest]

    wo_near = spread(6, wo_copies, wide_spot)
    own_copies[4].wait()
    landed(wo_near)
    landed(attn_copies)

    resid = hid_last + nn(attn_all[...], wo_all[...])
    my_seqs = pl.ds(pl.multiple_of(g * S, S), S)
    embeds[my_seqs, :] = (resid * ogain).astype(BF16)
    z_copies = []
    for k in range(1, Z):
        far = lax.rem(zz + k, Z) * 2 + core
        copy = pltpu.make_async_remote_copy(
            src_ref=embeds.at[my_seqs], dst_ref=embeds.at[my_seqs],
            send_sem=zsend.at[k - 1], recv_sem=zrecv.at[k - 1],
            device_id=(far, t), device_id_type=MESH,
        )
        copy.start()
        waits.append(copy)
        z_copies.append(copy)

    def chip_copy(index, spot):
        copy = pltpu.make_async_remote_copy(
            src_ref=spot, dst_ref=spot, send_sem=psend.at[index], recv_sem=precv.at[index],
            device_id=(buddy, t), device_id_type=MESH,
        )
        copy.start()
        waits.append(copy)
        return copy

    shared = [chip_copy(0, embeds.at[my_seqs])]

    E = G * S
    seq_of = iota((1, E), 1) % S
    passage = jnp.where(seq_of >= QDEV, (iota((1, E), 1) // S) * (S - QDEV) + seq_of - QDEV, -1)
    eye_q = iota((Q, Q), 0) == iota((Q, Q), 1)

    def chosen(row):
        column = jnp.sum(jnp.where(eye_q, row.astype(F32), 0.0), axis=1, keepdims=True)
        return column.astype(jnp.int32) == passage

    pos_hot = chosen(positives[...])
    hard = chosen(negatives[0:1, :])
    for j in range(1, negatives.shape[0]):
        hard = hard | chosen(negatives[j : j + 1, :])
    positive_f = jnp.where(pos_hot, 1.0, 0.0)
    allowed = (jnp.max(positive_f, axis=0, keepdims=True) > 0.5) | hard
    q_id = iota((Q, E), 0)
    pick = iota((Q, E), 1) == (q_id // QDEV) * S + q_id % QDEV
    pick_q = onehot(pick)
    eye_e = iota((E, E), 0) == iota((E, E), 1)
    row_s = iota((S, Q), 0)
    own_q = (row_s < QDEV) & (iota((S, Q), 1) == g * QDEV + row_s)
    own_p = iota((S, E), 1) == g * S + iota((S, E), 0)

    for k in range(1, Z):
        z_copies[k - 1].wait_recv()
        origin = lax.rem(zz + Z - k, Z) * 2 + core
        shared.append(chip_copy(k, embeds.at[pl.ds(pl.multiple_of(origin * S, S), S)]))
    landed(shared)

    queries = nn(pick_q, embeds[...]).astype(BF16)
    plain = (embeds[...].astype(F32) * (1.0 / ogain)).astype(BF16)
    plain_sq = jnp.sum(jnp.where(eye_e, nt(plain, plain), 0.0), axis=0, keepdims=True)
    scaled_sq = jnp.sum(
        jnp.where(eye_e, nt(embeds[...], embeds[...]), 0.0), axis=0, keepdims=True
    )
    logit_all[t, 0:Q] = nt(queries, embeds[...])
    logit_all[t, Q : Q + 8] = jnp.where(iota((8, E), 0) == 0, plain_sq, scaled_sq)
    logit_copies = [to_peer(9, k, logit_all.at[t], logit_all.at[t]) for k in rest]
    landed(logit_copies)
    summed = logit_all[0]
    for s in slots[1:]:
        summed = summed + logit_all[s]
    raw_dots = summed[0:Q]
    inverse_row = lax.rsqrt(summed[Q : Q + 1] / D + EPSILON)
    final_row = lax.rsqrt(inverse_row * inverse_row * summed[Q + 1 : Q + 2] + EPSILON)
    scale_row = inverse_row * final_row
    scale_q = jnp.sum(jnp.where(pick, scale_row, 0.0), axis=1, keepdims=True)
    resid_inverse = jnp.sum(jnp.where(own_p, inverse_row, 0.0), axis=1, keepdims=True)
    final_inverse = jnp.sum(jnp.where(own_p, final_row, 0.0), axis=1, keepdims=True)
    resid_unit = resid * resid_inverse
    embed = resid_unit * ogain * final_inverse
    dots_q, dots_p = raw_dots * scale_q, raw_dots * scale_row
    logits = dots_q * scale_row / SOFTMAX_TEMPER
    grown = jnp.where(allowed, jnp.exp(logits - 1.0 / SOFTMAX_TEMPER), 0.0)
    totals = jnp.sum(grown, axis=1, keepdims=True)
    target = jnp.sum(jnp.where(pos_hot, logits, 0.0), axis=1, keepdims=True)
    each = jnp.log(totals) + 1.0 / SOFTMAX_TEMPER - target
    loss[0, 0] = jnp.sum(each) / Q
    factor = LOSS_MULTIPLIER / (Q * SOFTMAX_TEMPER)
    coef = factor * (grown / totals - positive_f)
    coef_q16 = (coef * scale_row).astype(BF16)
    coef_p16 = (coef * scale_q).astype(BF16)
    coef_q = nn(onehot(own_q), coef_q16).astype(BF16)
    coef_p = nt(onehot(own_p), coef_p16).astype(BF16)
    d_embed = nn(coef_q, embeds[...]) + nn(coef_p, queries)
    along_q = coef_q16.astype(F32) * dots_q
    along_p = coef_p16.astype(F32) * dots_p
    inner = jnp.sum(nn(onehot(own_q, F32), along_q, EXACT), axis=1, keepdims=True) + jnp.sum(
        nt(onehot(own_p, F32), along_p, EXACT), axis=1, keepdims=True
    )
    d_final = final_inverse * (d_embed - embed * inner)
    middle = inner * (EPSILON / D) * final_inverse * final_inverse
    d_resid = resid_inverse * (ogain * d_final - resid_unit * middle)
    d_resid16 = d_resid.astype(BF16)
    d_resid_low = (d_resid - d_resid16.astype(F32)).astype(BF16)

    dap_out[...] = nt(d_resid16, wo_all[...])
    dap_copies = [to_peer(10, k, dap_out.at[:, block(peers[k])], dap_in.at[t]) for k in rest]
    dap_in[t] = dap_out[:, block(t)]
    eye_n = iota((N, N), 0) == iota((N, N), 1)
    eye16 = onehot(eye_n)
    probs16_t = nt(eye16, probs16).astype(BF16)
    landed(dap_copies)
    d_attn = dap_in[0]
    for s in slots[1:]:
        d_attn = d_attn + dap_in[s]
    d_attn16 = d_attn.astype(BF16)
    d_probs = nt(d_attn16, value16)
    d_scores16 = (
        probs * (d_probs - jnp.sum(probs * d_probs, axis=-1, keepdims=True)) / root
    ).astype(BF16)
    d_key_rot = nn(nt(eye16, d_scores16).astype(BF16), query16)
    d_value = nn(probs16_t, d_attn16)
    pair_out[...] = jnp.where(even, d_value, d_key_rot).astype(BF16)
    pair_copy = pltpu.make_async_remote_copy(
        src_ref=pair_out, dst_ref=pair_in, send_sem=psend.at[Z], recv_sem=precv.at[Z],
        device_id=(g, mate), device_id_type=MESH,
    )
    pair_copy.start()
    waits.append(pair_copy)
    d_query_rot = nn(d_scores16, key16)
    d_query16 = head_backward(
        d_query_rot, query_unit, query_inverse, qg, cos_query, sin_query
    ).astype(BF16)
    dq_all[:, block(t)] = d_query16
    my_dq = dq_all.at[:, block(t)]
    dq_copies = [to_peer(11, k, my_dq, my_dq) for k in rest]
    query_rows = nn(
        last_hot_t.astype(F32), d_query16.astype(F32) * query_raw, EXACT
    )
    pair_copy.wait_recv()
    whole = jnp.where(even, d_key_rot, d_value) + pair_in[...].astype(F32)
    d_key_raw = head_backward(whole, key_unit, key_inverse, kg, cos_key, sin_key)
    column16 = jnp.where(even, d_key_raw, whole).astype(BF16)
    dkv_all[:, block(t)] = column16
    my_dkv = dkv_all.at[:, block(t)]
    dkv_copies = [to_peer(12, k, my_dkv, my_dkv) for k in rest]
    raw = jnp.where(even, key_raw, value_raw)
    rows_all[t] = nt(
        jnp.ones((8, HD), F32), column16.astype(F32) * raw + query_rows, EXACT
    )
    row_copies = [to_peer(8, k, rows_all.at[t], rows_all.at[t]) for k in rest]
    landed(dq_copies)
    dq_rows = nn(last_hot_t, dq_all[...]).astype(BF16)
    landed(row_copies)
    row_sums = rows_all[0]
    for s in slots[1:]:
        row_sums = row_sums + rows_all[s]
    mean = jnp.sum(jnp.where(eye_n, row_sums[0:1, :], 0.0), axis=1, keepdims=True) / D
    inverse = inv_all[:, 0:1]
    landed(dkv_copies)
    out_copies, local = [], []
    FC = F // 2
    for c in range(2):
        span = slice(c * FC, (c + 1) * FC)
        there = pl.ds(pl.multiple_of(t * F + c * FC, 128), FC)
        d_normed = nt(dkv_all[...], wkv_all[span, :]) + nt(dq_rows, wq_all[span, :])
        unit = hid_all[:, span].astype(F32) * inverse
        grad = inverse * (d_normed * gain[:, span] - unit * mean)
        grad = grad + nn(last_hot_t, d_resid16[:, span]) + nn(last_hot_t, d_resid_low[:, span])
        out16[:, span] = grad.astype(BF16)
        for k in rest:
            rows = pl.ds(pl.multiple_of(peers[k] * own, own), own)
            out_copies.append(to_peer(13 + c, k, out16.at[rows, span], out.at[:, there]))
        copy = pltpu.make_async_copy(
            out16.at[my_rows, span], out.at[:, there], local_sem.at[5 + c]
        )
        copy.start()
        local.append(copy)
    landed(out_copies)
    for copy in local:
        copy.wait()
    for copy in waits:
        copy.wait_send()


def on_device(
    tensors, groups,
    hidden, lengths, positives, negatives, in_gain, wq, wkv, q_gain, k_gain, wo, out_gain
):
    T, G = tensors, groups
    own, D = hidden.shape
    F = D // T
    HD = wq.shape[1]
    N = own * T
    S = lengths.shape[1]
    Q = positives.shape[0]
    Z = G // 2
    vmem = pl.BlockSpec(memory_space=pltpu.VMEM)
    anywhere = pl.BlockSpec(memory_space=pl.ANY)
    scratch = [
        pltpu.VMEM((own, D), BF16),
        pltpu.VMEM((N, F), BF16),
        pltpu.VMEM((T, 8, HD), F32),
        pltpu.VMEM((N, HD), F32),
        pltpu.VMEM((N, F), BF16),
        pltpu.VMEM((F, T * HD), BF16),
        pltpu.VMEM((F, T * HD), BF16),
        pltpu.VMEM((T * HD, F), BF16),
        pltpu.VMEM((N, T * HD), BF16),
        pltpu.VMEM((T, N, 2 * HD), BF16),
        pltpu.VMEM((S, T * HD), F32),
        pltpu.VMEM((T, S, HD), F32),
        pltpu.VMEM((S, T * HD), BF16),
        pltpu.VMEM((G * S, F), BF16),
        pltpu.VMEM((T, Q + 8, G * S), F32),
        pltpu.VMEM((S, T * HD), F32),
        pltpu.VMEM((T, S, HD), F32),
        pltpu.VMEM((N, HD), BF16),
        pltpu.VMEM((N, HD), BF16),
        pltpu.VMEM((N, T * HD), BF16),
        pltpu.VMEM((S, T * HD), BF16),
        pltpu.VMEM((T, 8, N), F32),
        pltpu.VMEM((N, F), BF16),
        pltpu.SemaphoreType.DMA((7,)),
        pltpu.SemaphoreType.DMA((15, T - 1)),
        pltpu.SemaphoreType.DMA((15, T - 1)),
        pltpu.SemaphoreType.DMA((9, T - 1)),
        pltpu.SemaphoreType.DMA((9, T - 1)),
        pltpu.SemaphoreType.DMA((Z - 1,)),
        pltpu.SemaphoreType.DMA((Z - 1,)),
        pltpu.SemaphoreType.DMA((Z + 1,)),
        pltpu.SemaphoreType.DMA((Z + 1,)),
    ]
    d_hidden, loss = pl.pallas_call(
        functools.partial(kernel, T, G),
        out_shape=(
            jax.ShapeDtypeStruct((own, D), BF16),
            jax.ShapeDtypeStruct((1, 1), F32),
        ),
        in_specs=[
            anywhere, vmem, vmem, vmem, vmem, anywhere, anywhere, vmem, vmem, anywhere, vmem
        ],
        out_specs=(anywhere, pl.BlockSpec(memory_space=pltpu.SMEM)),
        scratch_shapes=scratch,
        compiler_params=pltpu.CompilerParams(
            collective_id=0, has_side_effects=True, vmem_limit_bytes=60 * 1024 * 1024
        ),
    )(
        hidden, lengths, positives.reshape(1, Q), negatives.T, in_gain.reshape(1, D), wq, wkv,
        q_gain.reshape(1, HD), k_gain.reshape(1, HD), wo, out_gain.reshape(1, D),
    )
    return d_hidden, loss.reshape(())


def solution(mesh):
    placed = (
        P(("dp", "tensor"), None),
        P("dp", None),
        P(),
        P(),
        P(),
        P(None, "tensor"),
        P(None, "tensor"),
        P(),
        P(),
        P("tensor", None),
        P(),
    )
    return jax.shard_map(
        functools.partial(on_device, mesh.shape["tensor"], mesh.shape["dp"]),
        mesh=mesh,
        in_specs=placed,
        out_specs=(P(("dp", "tensor"), None), P()),
        check_vma=False,
    )
```

```python
import functools
import math

import jax
import jax.numpy as jnp
from jax import lax
from jax.experimental import pallas as pl
from jax.experimental.pallas import tpu as pltpu
from jax.sharding import PartitionSpec as P

QDEV = 8
EPSILON = 1e-06
SOFTMAX_TEMPER = 0.05
LOSS_MULTIPLIER = 8192.0
CHUNKS = 4
ROPE_BASE = 1000000.0

F32 = jnp.float32
BF16 = jnp.bfloat16
MESH = pl.DeviceIdType.MESH
EXACT = lax.Precision.HIGHEST


def nn(a, b, precision=None):
    return jnp.dot(a, b, preferred_element_type=F32, precision=precision)


def nt(a, b, precision=None):
    dims = (((1,), (1,)), ((), ()))
    return lax.dot_general(a, b, dims, preferred_element_type=F32, precision=precision)


def iota(shape, axis):
    return lax.broadcasted_iota(jnp.int32, shape, axis)


def onehot(mask, kind=BF16):
    return jnp.where(mask, 1.0, 0.0).astype(F32).astype(kind)


def rms_scale(x):
    return lax.rsqrt(jnp.mean(x * x, axis=-1, keepdims=True) + EPSILON)


def rope_tables(position, width):
    half = width // 2
    lane = iota((1, width), 1)
    lane = jnp.where(lane >= half, lane - half, lane).astype(F32)
    frequency = jnp.exp(lane * (-2.0 / width * math.log(ROPE_BASE)))
    angles = position * frequency
    return jnp.cos(angles), jnp.sin(angles)


def rotate(x, cosine, sine):
    half = x.shape[-1] // 2
    sign = jnp.where(iota((1, x.shape[-1]), 1) < half, -1.0, 1.0)
    return x * cosine + pltpu.roll(x, half, 1) * sign * sine


def head_forward(raw, gain, cosine, sine):
    inverse = rms_scale(raw)
    unit = raw * inverse
    return unit, inverse, rotate(unit * gain, cosine, sine)


def head_backward(grad, unit, inverse, gain, cosine, sine):
    scaled = rotate(grad, cosine, -sine) * gain
    return inverse * (scaled - unit * jnp.mean(unit * scaled, axis=-1, keepdims=True))


def kernel(
    tensors, groups,
    hidden, lens_in, positives_in, negatives_in, in_gain, wq, wkv, q_gain, k_gain, wo, out_gain,
    out, loss, lens, positives, negatives, gains, head_gains,
    hid_own, hid_all, inv_rows, inv_all, normed, wkv_all, wq_all, wo_all,
    kvp_out, kvp_in, qp_out, qp_in, attn_all, embeds, logit_all, stats_all,
    dap_out, dap_in, dkv_all, dq_all, rows_all, addend, out16,
    local_sem, tsend, trecv, fsend, frecv, zsend, zrecv, psend, precv,
):
    T, G = tensors, groups
    Z = G // 2
    own, D = hidden.shape
    F = D // T
    HD = wq.shape[1]
    N = own * T
    S = lens_in.shape[1]
    Q = positives_in.shape[1]
    H = F // 4
    HH = HD // 4
    root = math.sqrt(HD)
    t = lax.axis_index("tensor")
    g = lax.axis_index("dp")
    zz = g // 2
    core = g % 2
    buddy = g + 1 - 2 * core
    z_mate = (zz + 1 - 2 * (zz % 2)) * 2 + core
    quarter = (zz % 2) * 2 + core
    far_quarter = (1 - zz % 2) * 2 + core
    even = t % 2 == 0
    peers = [lax.rem(t + k, T) for k in range(1, T)]
    sources = [lax.rem(t + T - k, T) for k in range(1, T)]
    slots = list(range(T))
    columns = pl.ds(pl.multiple_of(t * F, 128), F)

    def block(p):
        return pl.ds(pl.multiple_of(p * HD, 128), HD)

    own_copies = [
        pltpu.make_async_copy(hidden, hid_own, local_sem.at[0]),
        pltpu.make_async_copy(
            hidden.at[:, columns], hid_all.at[pl.ds(t * own, own)], local_sem.at[1]
        ),
        pltpu.make_async_copy(wkv.at[pl.ds(t * F, F)], wkv_all.at[:, block(t)], local_sem.at[2]),
        pltpu.make_async_copy(wq.at[pl.ds(t * F, F)], wq_all.at[:, block(t)], local_sem.at[3]),
        pltpu.make_async_copy(wo.at[:, columns], wo_all.at[block(t)], local_sem.at[4]),
        pltpu.make_async_copy(lens_in, lens, local_sem.at[5]),
        pltpu.make_async_copy(positives_in, positives, local_sem.at[6]),
        pltpu.make_async_copy(negatives_in, negatives, local_sem.at[7]),
        pltpu.make_async_copy(in_gain.at[:, columns], gains.at[0], local_sem.at[8]),
        pltpu.make_async_copy(out_gain.at[:, columns], gains.at[1], local_sem.at[9]),
        pltpu.make_async_copy(q_gain, head_gains.at[0], local_sem.at[10]),
        pltpu.make_async_copy(k_gain, head_gains.at[1], local_sem.at[11]),
    ]
    for copy in own_copies:
        copy.start()

    barrier = pltpu.get_barrier_semaphore()
    for p in peers:
        pl.semaphore_signal(barrier, inc=1, device_id=(g, p), device_id_type=MESH)
    for k in range(1, Z):
        far = lax.rem(zz + k, Z) * 2 + core
        pl.semaphore_signal(barrier, inc=1, device_id=(far, t), device_id_type=MESH)
    pl.semaphore_signal(barrier, inc=1, device_id=(buddy, t), device_id_type=MESH)
    pl.semaphore_wait(barrier, T - 1 + Z - 1 + 1)

    waits = []

    def to_peer(kind, k, src, dst):
        copy = pltpu.make_async_remote_copy(
            src_ref=src, dst_ref=dst, send_sem=tsend.at[kind, k], recv_sem=trecv.at[kind, k],
            device_id=(g, peers[k]), device_id_type=MESH,
        )
        copy.start()
        waits.append(copy)
        return copy

    def pass_on(kind, k, spot, target):
        copy = pltpu.make_async_remote_copy(
            src_ref=spot, dst_ref=spot, send_sem=fsend.at[kind, k], recv_sem=frecv.at[kind, k],
            device_id=(target, t), device_id_type=MESH,
        )
        copy.start()
        waits.append(copy)
        return copy

    def landed(copies):
        for copy in copies:
            copy.wait_recv()

    rest = range(T - 1)
    my_rows = pl.ds(pl.multiple_of(t * own, own), own)

    def cols(p):
        return pl.ds(pl.multiple_of(p * F, 128), F)

    def tall_spot(ref):
        def spot(source, part):
            return ref.at[pl.ds(pl.multiple_of(part * H, H), H), block(source)]

        return spot

    def wide_spot(source, part):
        return wo_all.at[pl.ds(pl.multiple_of(source * HD + part * HH, HH), HH)]

    def own_tall(ref, p):
        return ref.at[pl.ds(pl.multiple_of(p * F + quarter * H, H), H)]

    def own_wide(p):
        return wo.at[pl.ds(pl.multiple_of(quarter * HH, HH), HH), cols(p)]

    def spread(kind, fetched, spot):
        near, along = [], []
        for k in rest:
            fetched[k].wait_recv()
            mine = spot(sources[k], quarter)
            along.append(pass_on(kind, k, mine, z_mate))
            near.append(pass_on(kind + 1, k, mine, buddy))
        for k in rest:
            along[k].wait_recv()
            near.append(pass_on(kind + 2, k, spot(sources[k], far_quarter), buddy))
        return near

    wkv_spot, wq_spot = tall_spot(wkv_all), tall_spot(wq_all)
    wkv_copies = [
        to_peer(1, k, own_tall(wkv, peers[k]), wkv_spot(t, quarter)) for k in rest
    ]
    hid_copies = [
        to_peer(0, k, hidden.at[:, cols(peers[k])], hid_all.at[my_rows]) for k in rest
    ]

    own_copies[0].wait()
    mine = hid_own[...].astype(F32)
    diagonal = iota((own, HD), 0) == iota((own, HD), 1)
    inv_rows[t] = jnp.broadcast_to(
        jnp.sum(jnp.where(diagonal, rms_scale(mine), 0.0), axis=0, keepdims=True), (8, HD)
    )
    inv_copies = [to_peer(2, k, inv_rows.at[t], inv_rows.at[t]) for k in rest]

    for copy in own_copies[5:]:
        copy.wait()

    lens_row = lens[...].astype(F32)
    square_r, square_c = iota((S, S), 0), iota((S, S), 1)
    lens_col = jnp.sum(jnp.where(square_r == square_c, lens_row, 0.0), axis=1, keepdims=True)
    ends_col = jnp.sum(jnp.where(square_c <= square_r, lens_row, 0.0), axis=1, keepdims=True)
    ends_row = jnp.sum(jnp.where(square_r <= square_c, lens_col, 0.0), axis=0, keepdims=True)
    starts_col, starts_row = ends_col - lens_col, ends_row - lens_row
    token_row = iota((S, N), 1).astype(F32)
    token_col = iota((N, S), 0).astype(F32)
    both_starts = jnp.concatenate([starts_col, starts_col], axis=0)
    both_ends = jnp.concatenate([ends_col, ends_col], axis=0)
    both_row = iota((2 * S, N), 1).astype(F32)
    inside = (both_row >= both_starts) & (both_row < both_ends)
    inside_t = (token_col >= starts_row) & (token_col < ends_row)
    offset = jnp.sum(jnp.where(inside_t, starts_row, 0.0), axis=1, keepdims=True)
    position = iota((N, 1), 0).astype(F32) - offset
    is_last = token_row == ends_col - 1.0
    last_hot = onehot(is_last)
    last_hot_t = onehot(token_col == ends_row - 1.0)
    cos_key, sin_key = rope_tables(position, HD)
    cos_query, sin_query = rope_tables(both_ends - both_starts - 1.0, HD)
    qg, kg = head_gains[0], head_gains[1]
    shift = root * jnp.max(qg, axis=1, keepdims=True) * jnp.max(kg, axis=1, keepdims=True)
    gain, ogain = gains[0], gains[1]
    eye_n = iota((N, N), 0) == iota((N, N), 1)
    eye16 = onehot(eye_n)

    wkv_near = spread(0, wkv_copies, wkv_spot)
    wq_copies = [to_peer(3, k, own_tall(wq, peers[k]), wq_spot(t, quarter)) for k in rest]

    own_copies[1].wait()
    landed(hid_copies)
    landed(inv_copies)
    for s in slots:
        rows = slice(s * own, (s + 1) * own)
        inverse = jnp.sum(
            jnp.where(diagonal, inv_rows[s, 0:1, :], 0.0), axis=1, keepdims=True
        )
        inv_all[rows, :] = jnp.broadcast_to(inverse, (own, HD))
        normed[rows, :] = (hid_all[rows, :].astype(F32) * inverse * gain).astype(BF16)
    own_copies[2].wait()
    landed(wkv_near)
    kvp_out[...] = nn(normed[...], wkv_all[...]).astype(BF16)

    def pair(p):
        return pl.ds(pl.multiple_of((p // 2) * (2 * HD), 256), 2 * HD)

    kvp_copies = [
        to_peer(4, k, kvp_out.at[:, pair(peers[k])], kvp_in.at[t]) for k in rest
    ]
    kvp_in[t] = kvp_out[:, pair(t)]

    wq_near = spread(3, wq_copies, wq_spot)
    last16 = nn(last_hot, normed[...]).astype(BF16)
    own_copies[3].wait()
    landed(wq_near)
    qp_out[...] = nn(last16, wq_all[...])
    qp_copies = [to_peer(6, k, qp_out.at[:, pair(peers[k])], qp_in.at[t]) for k in rest]
    qp_in[t] = qp_out[:, pair(t)]
    wo_copies = [to_peer(5, k, own_wide(peers[k]), wide_spot(t, quarter)) for k in rest]
    hid_last = nn(last_hot, hid_all[...])
    inverse_last = nn(last_hot.astype(F32), inv_all[...], EXACT)[:, 0:1]

    landed(kvp_copies)
    key_raw = kvp_in[0, :, 0:HD].astype(F32)
    value_raw = kvp_in[0, :, HD : 2 * HD].astype(F32)
    for s in slots[1:]:
        key_raw = key_raw + kvp_in[s, :, 0:HD].astype(F32)
        value_raw = value_raw + kvp_in[s, :, HD : 2 * HD].astype(F32)
    value16 = value_raw.astype(BF16)
    key_unit, key_inverse, key_rot = head_forward(key_raw, kg, cos_key, sin_key)
    key16 = key_rot.astype(BF16)

    landed(qp_copies)
    query_raw = qp_in[0]
    for s in slots[1:]:
        query_raw = query_raw + qp_in[s]
    query_raw = jnp.concatenate([query_raw[:, :HD], query_raw[:, HD:]], axis=0)
    query_unit, query_inverse, query_rot = head_forward(query_raw, qg, cos_query, sin_query)
    query16 = query_rot.astype(BF16)
    scores = nt(query16, key16) / root
    weight = jnp.where(inside, jnp.exp(scores - shift), 0.0)
    probs = weight / jnp.sum(weight, axis=-1, keepdims=True)
    probs16 = probs.astype(BF16)
    attn = nn(probs16, value16)
    attn_all[:, block(t)] = jnp.where(even, attn[:S], attn[S:]).astype(BF16)
    my_attn = attn_all.at[:, block(t)]
    attn_copies = [to_peer(10, k, my_attn, my_attn) for k in rest]

    wo_near = spread(6, wo_copies, wide_spot)
    own_copies[4].wait()
    landed(wo_near)
    landed(attn_copies)

    resid = hid_last + nn(attn_all[...], wo_all[...])
    my_seqs = pl.ds(pl.multiple_of(g * S, S), S)
    embeds[my_seqs, :] = (resid * ogain).astype(BF16)
    z_copies = []
    for k in range(1, Z):
        far = lax.rem(zz + k, Z) * 2 + core
        copy = pltpu.make_async_remote_copy(
            src_ref=embeds.at[my_seqs], dst_ref=embeds.at[my_seqs],
            send_sem=zsend.at[k - 1], recv_sem=zrecv.at[k - 1],
            device_id=(far, t), device_id_type=MESH,
        )
        copy.start()
        waits.append(copy)
        z_copies.append(copy)

    def chip_copy(index, spot):
        copy = pltpu.make_async_remote_copy(
            src_ref=spot, dst_ref=spot, send_sem=psend.at[index], recv_sem=precv.at[index],
            device_id=(buddy, t), device_id_type=MESH,
        )
        copy.start()
        waits.append(copy)
        return copy

    shared = [chip_copy(0, embeds.at[my_seqs])]

    E = G * S
    seq_of = iota((1, E), 1) % S
    passage = jnp.where(seq_of >= QDEV, (iota((1, E), 1) // S) * (S - QDEV) + seq_of - QDEV, -1)
    eye_q = iota((Q, Q), 0) == iota((Q, Q), 1)

    def chosen(row):
        column = jnp.sum(jnp.where(eye_q, row.astype(F32), 0.0), axis=1, keepdims=True)
        return column.astype(jnp.int32) == passage

    pos_hot = chosen(positives[...])
    hard = chosen(negatives[0:1, :])
    for j in range(1, negatives.shape[0]):
        hard = hard | chosen(negatives[j : j + 1, :])
    positive_f = jnp.where(pos_hot, 1.0, 0.0)
    allowed = (jnp.max(positive_f, axis=0, keepdims=True) > 0.5) | hard
    q_id = iota((Q, E), 0)
    pick = iota((Q, E), 1) == (q_id // QDEV) * S + q_id % QDEV
    pick_q = onehot(pick)
    eye_e = iota((E, E), 0) == iota((E, E), 1)
    row_s = iota((S, Q), 0)
    own_q = (row_s < QDEV) & (iota((S, Q), 1) == g * QDEV + row_s)
    own_p = iota((S, E), 1) == g * S + iota((S, E), 0)
    own_q16, own_p16 = onehot(own_q), onehot(own_p)
    plain_gain = 1.0 / ogain

    for k in range(1, Z):
        z_copies[k - 1].wait_recv()
        origin = lax.rem(zz + Z - k, Z) * 2 + core
        shared.append(chip_copy(k, embeds.at[pl.ds(pl.multiple_of(origin * S, S), S)]))
    landed(shared)

    queries = nn(pick_q, embeds[...]).astype(BF16)
    logit_all[t] = nt(queries, embeds[...])
    logit_copies = [to_peer(9, k, logit_all.at[t], logit_all.at[t]) for k in rest]
    plain = (embeds[...].astype(F32) * plain_gain).astype(BF16)
    plain_sq = jnp.sum(jnp.where(eye_e, nt(plain, plain), 0.0), axis=0, keepdims=True)
    scaled_sq = jnp.sum(
        jnp.where(eye_e, nt(embeds[...], embeds[...]), 0.0), axis=0, keepdims=True
    )
    stats_all[t] = jnp.where(iota((8, E), 0) == 0, plain_sq, scaled_sq)
    stats_copies = [to_peer(7, k, stats_all.at[t], stats_all.at[t]) for k in rest]
    landed(logit_copies)
    landed(stats_copies)
    raw_dots, stats = logit_all[0], stats_all[0]
    for s in slots[1:]:
        raw_dots = raw_dots + logit_all[s]
        stats = stats + stats_all[s]
    inverse_row = lax.rsqrt(stats[0:1] / D + EPSILON)
    final_row = lax.rsqrt(inverse_row * inverse_row * stats[1:2] + EPSILON)
    scale_row = inverse_row * final_row
    scale_q = jnp.sum(jnp.where(pick, scale_row, 0.0), axis=1, keepdims=True)
    resid_inverse = jnp.sum(jnp.where(own_p, inverse_row, 0.0), axis=1, keepdims=True)
    final_inverse = jnp.sum(jnp.where(own_p, final_row, 0.0), axis=1, keepdims=True)
    resid_unit = resid * resid_inverse
    embed = resid_unit * ogain * final_inverse
    dots_q, dots_p = raw_dots * scale_q, raw_dots * scale_row
    logits = dots_q * scale_row / SOFTMAX_TEMPER
    grown = jnp.where(allowed, jnp.exp(logits - 1.0 / SOFTMAX_TEMPER), 0.0)
    totals = jnp.sum(grown, axis=1, keepdims=True)
    factor = LOSS_MULTIPLIER / (Q * SOFTMAX_TEMPER)
    coef = factor * (grown / totals - positive_f)
    coef_q16 = (coef * scale_row).astype(BF16)
    coef_p16 = (coef * scale_q).astype(BF16)
    coef_q = nn(own_q16, coef_q16).astype(BF16)
    coef_p = nt(own_p16, coef_p16).astype(BF16)
    d_embed = nn(coef_q, embeds[...]) + nn(coef_p, queries)
    along_q = jnp.sum(coef_q16.astype(F32) * dots_q, axis=1, keepdims=True)
    along_p = jnp.sum(coef_p16.astype(F32) * dots_p, axis=0, keepdims=True)
    along_q = jnp.sum(jnp.where(eye_q, along_q, 0.0), axis=0, keepdims=True)
    inner = jnp.sum(jnp.where(own_q, along_q, 0.0), axis=1, keepdims=True) + jnp.sum(
        jnp.where(own_p, along_p, 0.0), axis=1, keepdims=True
    )
    d_final = final_inverse * (d_embed - embed * inner)
    middle = inner * (EPSILON / D) * final_inverse * final_inverse
    d_resid = resid_inverse * (ogain * d_final - resid_unit * middle)
    d_resid16 = d_resid.astype(BF16)

    dap_out[...] = nt(d_resid16, wo_all[...])
    dap_copies = [to_peer(11, k, dap_out.at[:, pair(peers[k])], dap_in.at[t]) for k in rest]
    dap_in[t] = dap_out[:, pair(t)]
    target = jnp.sum(jnp.where(pos_hot, logits, 0.0), axis=1, keepdims=True)
    loss[0, 0] = jnp.sum(jnp.log(totals) + 1.0 / SOFTMAX_TEMPER - target) / Q
    probs16_t = nt(eye16, probs16).astype(BF16)
    landed(dap_copies)
    d_attn = dap_in[0]
    for s in slots[1:]:
        d_attn = d_attn + dap_in[s]
    d_attn16 = jnp.concatenate([d_attn[:, :HD], d_attn[:, HD:]], axis=0).astype(BF16)
    d_probs = nt(d_attn16, value16)
    d_scores16 = (
        probs * (d_probs - jnp.sum(probs * d_probs, axis=-1, keepdims=True)) / root
    ).astype(BF16)
    d_key_rot = nn(nt(eye16, d_scores16).astype(BF16), query16)
    d_value = nn(probs16_t, d_attn16)
    d_key_raw = head_backward(d_key_rot, key_unit, key_inverse, kg, cos_key, sin_key)
    column16 = jnp.where(even, d_key_raw, d_value).astype(BF16)
    dkv_all[:, block(t)] = column16
    my_dkv = dkv_all.at[:, block(t)]
    dkv_copies = [to_peer(12, k, my_dkv, my_dkv) for k in rest]
    d_query_rot = nn(d_scores16, key16)
    d_query_raw = head_backward(
        d_query_rot, query_unit, query_inverse, qg, cos_query, sin_query
    )
    d_query16 = jnp.where(even, d_query_raw[:S], d_query_raw[S:]).astype(BF16)
    dq_all[:, block(t)] = d_query16
    my_dq = dq_all.at[:, block(t)]
    dq_copies = [to_peer(13, k, my_dq, my_dq) for k in rest]
    raw = jnp.where(even, key_raw, value_raw)
    kv_sums = jnp.sum(column16.astype(F32) * raw, axis=1, keepdims=True)
    own_query = jnp.where(even, query_raw[:S], query_raw[S:])
    query_sums = jnp.sum(d_query16.astype(F32) * own_query, axis=1, keepdims=True)
    rows_all[t] = jnp.broadcast_to(
        jnp.sum(jnp.where(eye_n, kv_sums, 0.0), axis=0, keepdims=True)
        + jnp.sum(jnp.where(is_last, query_sums, 0.0), axis=0, keepdims=True),
        (8, N),
    )
    row_copies = [to_peer(8, k, rows_all.at[t], rows_all.at[t]) for k in rest]
    landed(dq_copies)
    extra = inverse_last * gain * nt(dq_all[...], wq_all[...]) + d_resid
    extra16 = extra.astype(BF16)
    extra_low = (extra - extra16.astype(F32)).astype(BF16)
    addend[...] = nn(last_hot_t, extra16) + nn(last_hot_t, extra_low)
    landed(row_copies)
    row_sums = rows_all[0]
    for s in slots[1:]:
        row_sums = row_sums + rows_all[s]
    mean = jnp.sum(jnp.where(eye_n, row_sums[0:1, :], 0.0), axis=1, keepdims=True) / D
    inverse = inv_all[:, 0:1]
    landed(dkv_copies)
    out_copies, local = [], []
    FC = F // CHUNKS if F % (128 * CHUNKS) == 0 else F // 2
    for c in range(F // FC):
        span = slice(c * FC, (c + 1) * FC)
        there = pl.ds(pl.multiple_of(t * F + c * FC, 128), FC)
        d_normed = nt(dkv_all[...], wkv_all[span, :])
        unit = hid_all[:, span].astype(F32) * inverse
        grad = inverse * (d_normed * gain[:, span] - unit * mean) + addend[:, span]
        out16[:, span] = grad.astype(BF16)
        for k in rest:
            rows = pl.ds(pl.multiple_of(peers[k] * own, own), own)
            out_copies.append(to_peer(14 + c, k, out16.at[rows, span], out.at[:, there]))
        copy = pltpu.make_async_copy(
            out16.at[my_rows, span], out.at[:, there], local_sem.at[12 + c]
        )
        copy.start()
        local.append(copy)
    landed(out_copies)
    for copy in local:
        copy.wait()
    for copy in waits:
        copy.wait_send()


def on_device(
    tensors, groups,
    hidden, lengths, positives, negatives, in_gain, wq, wkv, q_gain, k_gain, wo, out_gain
):
    T, G = tensors, groups
    own, D = hidden.shape
    F = D // T
    HD = wq.shape[1]
    N = own * T
    S = lengths.shape[1]
    Q = positives.shape[0]
    Z = G // 2
    hbm = pl.BlockSpec(memory_space=pltpu.HBM)
    anywhere = pl.BlockSpec(memory_space=pl.ANY)
    scratch = [
        pltpu.VMEM((1, S), jnp.int32),
        pltpu.VMEM((1, Q), jnp.int32),
        pltpu.VMEM((negatives.shape[1], Q), jnp.int32),
        pltpu.VMEM((2, 1, F), F32),
        pltpu.VMEM((2, 1, HD), F32),
        pltpu.VMEM((own, D), BF16),
        pltpu.VMEM((N, F), BF16),
        pltpu.VMEM((T, 8, HD), F32),
        pltpu.VMEM((N, HD), F32),
        pltpu.VMEM((N, F), BF16),
        pltpu.VMEM((F, T * HD), BF16),
        pltpu.VMEM((F, T * HD), BF16),
        pltpu.VMEM((T * HD, F), BF16),
        pltpu.VMEM((N, T * HD), BF16),
        pltpu.VMEM((T, N, 2 * HD), BF16),
        pltpu.VMEM((S, T * HD), F32),
        pltpu.VMEM((T, S, 2 * HD), F32),
        pltpu.VMEM((S, T * HD), BF16),
        pltpu.VMEM((G * S, F), BF16),
        pltpu.VMEM((T, Q, G * S), F32),
        pltpu.VMEM((T, 8, G * S), F32),
        pltpu.VMEM((S, T * HD), F32),
        pltpu.VMEM((T, S, 2 * HD), F32),
        pltpu.VMEM((N, T * HD), BF16),
        pltpu.VMEM((S, T * HD), BF16),
        pltpu.VMEM((T, 8, N), F32),
        pltpu.VMEM((N, F), F32),
        pltpu.VMEM((N, F), BF16),
        pltpu.SemaphoreType.DMA((12 + CHUNKS,)),
        pltpu.SemaphoreType.DMA((14 + CHUNKS, T - 1)),
        pltpu.SemaphoreType.DMA((14 + CHUNKS, T - 1)),
        pltpu.SemaphoreType.DMA((9, T - 1)),
        pltpu.SemaphoreType.DMA((9, T - 1)),
        pltpu.SemaphoreType.DMA((Z,)),
        pltpu.SemaphoreType.DMA((Z,)),
        pltpu.SemaphoreType.DMA((Z,)),
        pltpu.SemaphoreType.DMA((Z,)),
    ]
    d_hidden, loss = pl.pallas_call(
        functools.partial(kernel, T, G),
        out_shape=(
            jax.ShapeDtypeStruct((own, D), BF16),
            jax.ShapeDtypeStruct((1, 1), F32),
        ),
        in_specs=[hbm] * 11,
        out_specs=(anywhere, pl.BlockSpec(memory_space=pltpu.SMEM)),
        scratch_shapes=scratch,
        compiler_params=pltpu.CompilerParams(
            collective_id=0, has_side_effects=True, vmem_limit_bytes=60 * 1024 * 1024
        ),
    )(
        hidden, lengths, positives.reshape(1, Q), negatives.T, in_gain.reshape(1, D), wq, wkv,
        q_gain.reshape(1, HD), k_gain.reshape(1, HD), wo, out_gain.reshape(1, D),
    )
    return d_hidden, loss.reshape(())


def solution(mesh):
    placed = (
        P(("dp", "tensor"), None),
        P("dp", None),
        P(),
        P(),
        P(),
        P(None, "tensor"),
        P(None, "tensor"),
        P(),
        P(),
        P("tensor", None),
        P(),
    )
    return jax.shard_map(
        functools.partial(on_device, mesh.shape["tensor"], mesh.shape["dp"]),
        mesh=mesh,
        in_specs=placed,
        out_specs=(P(("dp", "tensor"), None), P()),
        check_vma=False,
    )
```

```python
import functools
import math

import jax
import jax.numpy as jnp
from jax import lax
from jax.experimental import pallas as pl
from jax.experimental.pallas import tpu as pltpu
from jax.sharding import PartitionSpec as P

QDEV = 8
EPSILON = 1e-06
SOFTMAX_TEMPER = 0.05
LOSS_MULTIPLIER = 8192.0
CHUNKS = 4
ROPE_BASE = 1000000.0

F32 = jnp.float32
BF16 = jnp.bfloat16
MESH = pl.DeviceIdType.MESH
EXACT = lax.Precision.HIGHEST


def nn(a, b, precision=None):
    return jnp.dot(a, b, preferred_element_type=F32, precision=precision)


def nt(a, b, precision=None):
    dims = (((1,), (1,)), ((), ()))
    return lax.dot_general(a, b, dims, preferred_element_type=F32, precision=precision)


def iota(shape, axis):
    return lax.broadcasted_iota(jnp.int32, shape, axis)


def onehot(mask, kind=BF16):
    return jnp.where(mask, 1.0, 0.0).astype(F32).astype(kind)


def rms_scale(x):
    return lax.rsqrt(jnp.mean(x * x, axis=-1, keepdims=True) + EPSILON)


def rope_tables(position, width):
    half = width // 2
    lane = iota((1, width), 1)
    lane = jnp.where(lane >= half, lane - half, lane).astype(F32)
    frequency = jnp.exp(lane * (-2.0 / width * math.log(ROPE_BASE)))
    angles = position * frequency
    return jnp.cos(angles), jnp.sin(angles)


def rotate(x, cosine, sine):
    half = x.shape[-1] // 2
    sign = jnp.where(iota((1, x.shape[-1]), 1) < half, -1.0, 1.0)
    return x * cosine + pltpu.roll(x, half, 1) * sign * sine


def head_forward(raw, gain, cosine, sine):
    inverse = rms_scale(raw)
    unit = raw * inverse
    return unit, inverse, rotate(unit * gain, cosine, sine)


def head_backward(grad, unit, inverse, gain, cosine, sine):
    scaled = rotate(grad, cosine, -sine) * gain
    return inverse * (scaled - unit * jnp.mean(unit * scaled, axis=-1, keepdims=True))


def kernel(
    tensors, groups,
    hidden, lens_in, positives_in, negatives_in, in_gain, wq, wkv, q_gain, k_gain, wo, out_gain,
    out, loss, lens, positives, negatives, gains, head_gains,
    hid_own, hid_all, inv_rows, inv_all, normed, wkv_all, wq_all, wo_all,
    kvp_out, kvp_in, qp_out, qp_in, attn_all, embeds, logit_all, stats_all,
    dap_out, dap_in, dkv_all, dq_all, rows_all, addend, out16,
    local_sem, tsend, trecv, fsend, frecv, zsend, zrecv, psend, precv,
):
    T, G = tensors, groups
    Z = G // 2
    own, D = hidden.shape
    F = D // T
    HD = wq.shape[1]
    N = own * T
    S = lens_in.shape[1]
    Q = positives_in.shape[1]
    H = F // 4
    HH = HD // 4
    root = math.sqrt(HD)
    t = lax.axis_index("tensor")
    g = lax.axis_index("dp")
    zz = g // 2
    core = g % 2
    buddy = g + 1 - 2 * core
    z_mate = (zz + 1 - 2 * (zz % 2)) * 2 + core
    quarter = (zz % 2) * 2 + core
    far_quarter = (1 - zz % 2) * 2 + core
    even = t % 2 == 0
    peers = [lax.rem(t + k, T) for k in range(1, T)]
    sources = [lax.rem(t + T - k, T) for k in range(1, T)]
    slots = list(range(T))
    columns = pl.ds(pl.multiple_of(t * F, 128), F)

    def block(p):
        return pl.ds(pl.multiple_of(p * HD, 128), HD)

    own_copies = [
        pltpu.make_async_copy(hidden, hid_own, local_sem.at[0]),
        pltpu.make_async_copy(
            hidden.at[:, columns], hid_all.at[pl.ds(t * own, own)], local_sem.at[1]
        ),
        pltpu.make_async_copy(wkv.at[pl.ds(t * F, F)], wkv_all.at[:, block(t)], local_sem.at[2]),
        pltpu.make_async_copy(wq.at[pl.ds(t * F, F)], wq_all.at[:, block(t)], local_sem.at[3]),
        pltpu.make_async_copy(wo.at[:, columns], wo_all.at[block(t)], local_sem.at[4]),
        pltpu.make_async_copy(lens_in, lens, local_sem.at[5]),
        pltpu.make_async_copy(positives_in, positives, local_sem.at[6]),
        pltpu.make_async_copy(negatives_in, negatives, local_sem.at[7]),
        pltpu.make_async_copy(in_gain.at[:, columns], gains.at[0], local_sem.at[8]),
        pltpu.make_async_copy(out_gain.at[:, columns], gains.at[1], local_sem.at[9]),
        pltpu.make_async_copy(q_gain, head_gains.at[0], local_sem.at[10]),
        pltpu.make_async_copy(k_gain, head_gains.at[1], local_sem.at[11]),
    ]
    for copy in own_copies:
        copy.start()

    barrier = pltpu.get_barrier_semaphore()
    for p in peers:
        pl.semaphore_signal(barrier, inc=1, device_id=(g, p), device_id_type=MESH)
    for k in range(1, Z):
        far = lax.rem(zz + k, Z) * 2 + core
        pl.semaphore_signal(barrier, inc=1, device_id=(far, t), device_id_type=MESH)
    pl.semaphore_signal(barrier, inc=1, device_id=(buddy, t), device_id_type=MESH)
    pl.semaphore_wait(barrier, T - 1 + Z - 1 + 1)

    waits = []

    def to_peer(kind, k, src, dst):
        copy = pltpu.make_async_remote_copy(
            src_ref=src, dst_ref=dst, send_sem=tsend.at[kind, k], recv_sem=trecv.at[kind, k],
            device_id=(g, peers[k]), device_id_type=MESH,
        )
        copy.start()
        waits.append(copy)
        return copy

    def pass_on(kind, k, spot, target):
        copy = pltpu.make_async_remote_copy(
            src_ref=spot, dst_ref=spot, send_sem=fsend.at[kind, k], recv_sem=frecv.at[kind, k],
            device_id=(target, t), device_id_type=MESH,
        )
        copy.start()
        waits.append(copy)
        return copy

    def landed(copies):
        for copy in copies:
            copy.wait_recv()

    rest = range(T - 1)
    my_rows = pl.ds(pl.multiple_of(t * own, own), own)

    def cols(p):
        return pl.ds(pl.multiple_of(p * F, 128), F)

    def tall_spot(ref):
        def spot(source, part):
            return ref.at[pl.ds(pl.multiple_of(part * H, H), H), block(source)]

        return spot

    def wide_spot(source, part):
        return wo_all.at[pl.ds(pl.multiple_of(source * HD + part * HH, HH), HH)]

    def own_tall(ref, p):
        return ref.at[pl.ds(pl.multiple_of(p * F + quarter * H, H), H)]

    def own_wide(p):
        return wo.at[pl.ds(pl.multiple_of(quarter * HH, HH), HH), cols(p)]

    def spread(kind, fetched, spot):
        near, along = [], []
        for k in rest:
            fetched[k].wait_recv()
            mine = spot(sources[k], quarter)
            along.append(pass_on(kind, k, mine, z_mate))
            near.append(pass_on(kind + 1, k, mine, buddy))
        return near, along

    def finish(kind, begun, spot):
        near, along = begun
        for k in rest:
            along[k].wait_recv()
            near.append(pass_on(kind + 2, k, spot(sources[k], far_quarter), buddy))
        landed(near)

    wkv_spot, wq_spot = tall_spot(wkv_all), tall_spot(wq_all)
    wkv_copies = [
        to_peer(1, k, own_tall(wkv, peers[k]), wkv_spot(t, quarter)) for k in rest
    ]
    hid_copies = [
        to_peer(0, k, hidden.at[:, cols(peers[k])], hid_all.at[my_rows]) for k in rest
    ]

    own_copies[0].wait()
    mine = hid_own[...].astype(F32)
    diagonal = iota((own, HD), 0) == iota((own, HD), 1)
    inv_rows[t] = jnp.broadcast_to(
        jnp.sum(jnp.where(diagonal, rms_scale(mine), 0.0), axis=0, keepdims=True), (8, HD)
    )
    inv_copies = [to_peer(2, k, inv_rows.at[t], inv_rows.at[t]) for k in rest]

    wkv_begun = spread(0, wkv_copies, wkv_spot)
    for copy in own_copies[5:]:
        copy.wait()

    lens_row = lens[...].astype(F32)
    square_r, square_c = iota((S, S), 0), iota((S, S), 1)
    lens_col = jnp.sum(jnp.where(square_r == square_c, lens_row, 0.0), axis=1, keepdims=True)
    ends_col = jnp.sum(jnp.where(square_c <= square_r, lens_row, 0.0), axis=1, keepdims=True)
    ends_row = jnp.sum(jnp.where(square_r <= square_c, lens_col, 0.0), axis=0, keepdims=True)
    starts_col, starts_row = ends_col - lens_col, ends_row - lens_row
    token_row = iota((S, N), 1).astype(F32)
    token_col = iota((N, S), 0).astype(F32)
    both_starts = jnp.concatenate([starts_col, starts_col], axis=0)
    both_ends = jnp.concatenate([ends_col, ends_col], axis=0)
    both_row = iota((2 * S, N), 1).astype(F32)
    inside = (both_row >= both_starts) & (both_row < both_ends)
    inside_t = (token_col >= starts_row) & (token_col < ends_row)
    offset = jnp.sum(jnp.where(inside_t, starts_row, 0.0), axis=1, keepdims=True)
    position = iota((N, 1), 0).astype(F32) - offset
    is_last = token_row == ends_col - 1.0
    last_hot = onehot(is_last)
    last_hot_t = onehot(token_col == ends_row - 1.0)
    cos_key, sin_key = rope_tables(position, HD)
    cos_query, sin_query = rope_tables(both_ends - both_starts - 1.0, HD)
    qg, kg = head_gains[0], head_gains[1]
    shift = root * jnp.max(qg, axis=1, keepdims=True) * jnp.max(kg, axis=1, keepdims=True)
    gain, ogain = gains[0], gains[1]
    eye_n = iota((N, N), 0) == iota((N, N), 1)
    eye16 = onehot(eye_n)

    wq_copies = [to_peer(3, k, own_tall(wq, peers[k]), wq_spot(t, quarter)) for k in rest]
    finish(0, wkv_begun, wkv_spot)
    own_copies[1].wait()
    landed(hid_copies)
    landed(inv_copies)
    for s in slots:
        rows = slice(s * own, (s + 1) * own)
        inverse = jnp.sum(
            jnp.where(diagonal, inv_rows[s, 0:1, :], 0.0), axis=1, keepdims=True
        )
        inv_all[rows, :] = jnp.broadcast_to(inverse, (own, HD))
        normed[rows, :] = (hid_all[rows, :].astype(F32) * inverse * gain).astype(BF16)
    own_copies[2].wait()
    kvp_out[...] = nn(normed[...], wkv_all[...]).astype(BF16)

    wq_begun = spread(3, wq_copies, wq_spot)

    def pair(p):
        return pl.ds(pl.multiple_of((p // 2) * (2 * HD), 256), 2 * HD)

    kvp_copies = [
        to_peer(4, k, kvp_out.at[:, pair(peers[k])], kvp_in.at[t]) for k in rest
    ]
    kvp_in[t] = kvp_out[:, pair(t)]

    last16 = nn(last_hot, normed[...]).astype(BF16)
    own_copies[3].wait()
    finish(3, wq_begun, wq_spot)
    qp_out[...] = nn(last16, wq_all[...])
    qp_copies = [to_peer(6, k, qp_out.at[:, pair(peers[k])], qp_in.at[t]) for k in rest]
    qp_in[t] = qp_out[:, pair(t)]
    wo_copies = [to_peer(5, k, own_wide(peers[k]), wide_spot(t, quarter)) for k in rest]
    hid_last = nn(last_hot, hid_all[...])
    inverse_last = nn(last_hot.astype(F32), inv_all[...], EXACT)[:, 0:1]

    landed(kvp_copies)
    key_raw = kvp_in[0, :, 0:HD].astype(F32)
    value_raw = kvp_in[0, :, HD : 2 * HD].astype(F32)
    for s in slots[1:]:
        key_raw = key_raw + kvp_in[s, :, 0:HD].astype(F32)
        value_raw = value_raw + kvp_in[s, :, HD : 2 * HD].astype(F32)
    value16 = value_raw.astype(BF16)
    key_unit, key_inverse, key_rot = head_forward(key_raw, kg, cos_key, sin_key)
    key16 = key_rot.astype(BF16)

    landed(qp_copies)
    query_raw = qp_in[0]
    for s in slots[1:]:
        query_raw = query_raw + qp_in[s]
    query_raw = jnp.concatenate([query_raw[:, :HD], query_raw[:, HD:]], axis=0)
    query_unit, query_inverse, query_rot = head_forward(query_raw, qg, cos_query, sin_query)
    query16 = query_rot.astype(BF16)
    scores = nt(query16, key16) / root
    wo_begun = spread(6, wo_copies, wide_spot)
    weight = jnp.where(inside, jnp.exp(scores - shift), 0.0)
    probs = weight / jnp.sum(weight, axis=-1, keepdims=True)
    probs16 = probs.astype(BF16)
    attn = nn(probs16, value16)
    attn_all[:, block(t)] = jnp.where(even, attn[:S], attn[S:]).astype(BF16)
    my_attn = attn_all.at[:, block(t)]
    attn_copies = [to_peer(10, k, my_attn, my_attn) for k in rest]

    own_copies[4].wait()
    finish(6, wo_begun, wide_spot)
    landed(attn_copies)

    resid = hid_last + nn(attn_all[...], wo_all[...])
    my_seqs = pl.ds(pl.multiple_of(g * S, S), S)
    embeds[my_seqs, :] = (resid * ogain).astype(BF16)
    z_copies = []
    for k in range(1, Z):
        far = lax.rem(zz + k, Z) * 2 + core
        copy = pltpu.make_async_remote_copy(
            src_ref=embeds.at[my_seqs], dst_ref=embeds.at[my_seqs],
            send_sem=zsend.at[k - 1], recv_sem=zrecv.at[k - 1],
            device_id=(far, t), device_id_type=MESH,
        )
        copy.start()
        waits.append(copy)
        z_copies.append(copy)

    def chip_copy(index, spot):
        copy = pltpu.make_async_remote_copy(
            src_ref=spot, dst_ref=spot, send_sem=psend.at[index], recv_sem=precv.at[index],
            device_id=(buddy, t), device_id_type=MESH,
        )
        copy.start()
        waits.append(copy)
        return copy

    shared = [chip_copy(0, embeds.at[my_seqs])]

    E = G * S
    seq_of = iota((1, E), 1) % S
    passage = jnp.where(seq_of >= QDEV, (iota((1, E), 1) // S) * (S - QDEV) + seq_of - QDEV, -1)
    eye_q = iota((Q, Q), 0) == iota((Q, Q), 1)

    def chosen(row):
        column = jnp.sum(jnp.where(eye_q, row.astype(F32), 0.0), axis=1, keepdims=True)
        return column.astype(jnp.int32) == passage

    pos_hot = chosen(positives[...])
    hard = chosen(negatives[0:1, :])
    for j in range(1, negatives.shape[0]):
        hard = hard | chosen(negatives[j : j + 1, :])
    positive_f = jnp.where(pos_hot, 1.0, 0.0)
    allowed = (jnp.max(positive_f, axis=0, keepdims=True) > 0.5) | hard
    q_id = iota((Q, E), 0)
    pick = iota((Q, E), 1) == (q_id // QDEV) * S + q_id % QDEV
    pick_q = onehot(pick)
    eye_e = iota((E, E), 0) == iota((E, E), 1)
    row_s = iota((S, Q), 0)
    own_q = (row_s < QDEV) & (iota((S, Q), 1) == g * QDEV + row_s)
    own_p = iota((S, E), 1) == g * S + iota((S, E), 0)
    own_q16, own_p16 = onehot(own_q), onehot(own_p)
    plain_gain = 1.0 / ogain

    for k in range(1, Z):
        z_copies[k - 1].wait_recv()
        origin = lax.rem(zz + Z - k, Z) * 2 + core
        shared.append(chip_copy(k, embeds.at[pl.ds(pl.multiple_of(origin * S, S), S)]))
    landed(shared)

    queries = nn(pick_q, embeds[...]).astype(BF16)
    logit_all[t] = nt(queries, embeds[...])
    logit_copies = [to_peer(9, k, logit_all.at[t], logit_all.at[t]) for k in rest]
    plain = (embeds[...].astype(F32) * plain_gain).astype(BF16)
    plain_sq = jnp.sum(jnp.where(eye_e, nt(plain, plain), 0.0), axis=0, keepdims=True)
    scaled_sq = jnp.sum(
        jnp.where(eye_e, nt(embeds[...], embeds[...]), 0.0), axis=0, keepdims=True
    )
    stats_all[t] = jnp.where(iota((8, E), 0) == 0, plain_sq, scaled_sq)
    stats_copies = [to_peer(7, k, stats_all.at[t], stats_all.at[t]) for k in rest]
    landed(logit_copies)
    landed(stats_copies)
    raw_dots, stats = logit_all[0], stats_all[0]
    for s in slots[1:]:
        raw_dots = raw_dots + logit_all[s]
        stats = stats + stats_all[s]
    inverse_row = lax.rsqrt(stats[0:1] / D + EPSILON)
    final_row = lax.rsqrt(inverse_row * inverse_row * stats[1:2] + EPSILON)
    scale_row = inverse_row * final_row
    scale_q = jnp.sum(jnp.where(pick, scale_row, 0.0), axis=1, keepdims=True)
    resid_inverse = jnp.sum(jnp.where(own_p, inverse_row, 0.0), axis=1, keepdims=True)
    final_inverse = jnp.sum(jnp.where(own_p, final_row, 0.0), axis=1, keepdims=True)
    resid_unit = resid * resid_inverse
    embed = resid_unit * ogain * final_inverse
    dots_q, dots_p = raw_dots * scale_q, raw_dots * scale_row
    logits = dots_q * scale_row / SOFTMAX_TEMPER
    grown = jnp.where(allowed, jnp.exp(logits - 1.0 / SOFTMAX_TEMPER), 0.0)
    totals = jnp.sum(grown, axis=1, keepdims=True)
    factor = LOSS_MULTIPLIER / (Q * SOFTMAX_TEMPER)
    coef = factor * (grown / totals - positive_f)
    coef_q16 = (coef * scale_row).astype(BF16)
    coef_p16 = (coef * scale_q).astype(BF16)
    coef_q = nn(own_q16, coef_q16).astype(BF16)
    coef_p = nt(own_p16, coef_p16).astype(BF16)
    d_embed = nn(coef_q, embeds[...]) + nn(coef_p, queries)
    along_q = jnp.sum(coef_q16.astype(F32) * dots_q, axis=1, keepdims=True)
    along_p = jnp.sum(coef_p16.astype(F32) * dots_p, axis=0, keepdims=True)
    along_q = jnp.sum(jnp.where(eye_q, along_q, 0.0), axis=0, keepdims=True)
    inner = jnp.sum(jnp.where(own_q, along_q, 0.0), axis=1, keepdims=True) + jnp.sum(
        jnp.where(own_p, along_p, 0.0), axis=1, keepdims=True
    )
    d_final = final_inverse * (d_embed - embed * inner)
    middle = inner * (EPSILON / D) * final_inverse * final_inverse
    d_resid = resid_inverse * (ogain * d_final - resid_unit * middle)
    d_resid16 = d_resid.astype(BF16)

    dap_out[...] = nt(d_resid16, wo_all[...])
    dap_copies = [to_peer(11, k, dap_out.at[:, pair(peers[k])], dap_in.at[t]) for k in rest]
    dap_in[t] = dap_out[:, pair(t)]
    target = jnp.sum(jnp.where(pos_hot, logits, 0.0), axis=1, keepdims=True)
    loss[0, 0] = jnp.sum(jnp.log(totals) + 1.0 / SOFTMAX_TEMPER - target) / Q
    probs16_t = nt(eye16, probs16).astype(BF16)
    landed(dap_copies)
    d_attn = dap_in[0]
    for s in slots[1:]:
        d_attn = d_attn + dap_in[s]
    d_attn16 = jnp.concatenate([d_attn[:, :HD], d_attn[:, HD:]], axis=0).astype(BF16)
    d_probs = nt(d_attn16, value16)
    d_scores16 = (
        probs * (d_probs - jnp.sum(probs * d_probs, axis=-1, keepdims=True)) / root
    ).astype(BF16)
    d_key_rot = nn(nt(eye16, d_scores16).astype(BF16), query16)
    d_value = nn(probs16_t, d_attn16)
    d_key_raw = head_backward(d_key_rot, key_unit, key_inverse, kg, cos_key, sin_key)
    column16 = jnp.where(even, d_key_raw, d_value).astype(BF16)
    dkv_all[:, block(t)] = column16
    my_dkv = dkv_all.at[:, block(t)]
    dkv_copies = [to_peer(12, k, my_dkv, my_dkv) for k in rest]
    d_query_rot = nn(d_scores16, key16)
    d_query_raw = head_backward(
        d_query_rot, query_unit, query_inverse, qg, cos_query, sin_query
    )
    d_query16 = jnp.where(even, d_query_raw[:S], d_query_raw[S:]).astype(BF16)
    dq_all[:, block(t)] = d_query16
    my_dq = dq_all.at[:, block(t)]
    dq_copies = [to_peer(13, k, my_dq, my_dq) for k in rest]
    raw = jnp.where(even, key_raw, value_raw)
    kv_sums = jnp.sum(column16.astype(F32) * raw, axis=1, keepdims=True)
    own_query = jnp.where(even, query_raw[:S], query_raw[S:])
    query_sums = jnp.sum(d_query16.astype(F32) * own_query, axis=1, keepdims=True)
    rows_all[t] = jnp.broadcast_to(
        jnp.sum(jnp.where(eye_n, kv_sums, 0.0), axis=0, keepdims=True)
        + jnp.sum(jnp.where(is_last, query_sums, 0.0), axis=0, keepdims=True),
        (8, N),
    )
    row_copies = [to_peer(8, k, rows_all.at[t], rows_all.at[t]) for k in rest]
    landed(dq_copies)
    extra = inverse_last * gain * nt(dq_all[...], wq_all[...]) + d_resid
    extra16 = extra.astype(BF16)
    extra_low = (extra - extra16.astype(F32)).astype(BF16)
    addend[...] = nn(last_hot_t, extra16) + nn(last_hot_t, extra_low)
    landed(row_copies)
    row_sums = rows_all[0]
    for s in slots[1:]:
        row_sums = row_sums + rows_all[s]
    mean = jnp.sum(jnp.where(eye_n, row_sums[0:1, :], 0.0), axis=1, keepdims=True) / D
    inverse = inv_all[:, 0:1]
    landed(dkv_copies)
    out_copies, local, earlier = [], [], list(waits)
    FC = F // CHUNKS if F % (128 * CHUNKS) == 0 else F // 2
    for c in range(F // FC):
        span = slice(c * FC, (c + 1) * FC)
        there = pl.ds(pl.multiple_of(t * F + c * FC, 128), FC)
        d_normed = nt(dkv_all[...], wkv_all[span, :])
        unit = hid_all[:, span].astype(F32) * inverse
        grad = inverse * (d_normed * gain[:, span] - unit * mean) + addend[:, span]
        out16[:, span] = grad.astype(BF16)
        for k in rest:
            rows = pl.ds(pl.multiple_of(peers[k] * own, own), own)
            out_copies.append(to_peer(14 + c, k, out16.at[rows, span], out.at[:, there]))
        copy = pltpu.make_async_copy(
            out16.at[my_rows, span], out.at[:, there], local_sem.at[12 + c]
        )
        copy.start()
        local.append(copy)
    for copy in earlier:
        copy.wait_send()
    for copy in local:
        copy.wait()
    for copy in out_copies:
        copy.wait()


def on_device(
    tensors, groups,
    hidden, lengths, positives, negatives, in_gain, wq, wkv, q_gain, k_gain, wo, out_gain
):
    T, G = tensors, groups
    own, D = hidden.shape
    F = D // T
    HD = wq.shape[1]
    N = own * T
    S = lengths.shape[1]
    Q = positives.shape[0]
    Z = G // 2
    hbm = pl.BlockSpec(memory_space=pltpu.HBM)
    anywhere = pl.BlockSpec(memory_space=pl.ANY)
    scratch = [
        pltpu.VMEM((1, S), jnp.int32),
        pltpu.VMEM((1, Q), jnp.int32),
        pltpu.VMEM((negatives.shape[1], Q), jnp.int32),
        pltpu.VMEM((2, 1, F), F32),
        pltpu.VMEM((2, 1, HD), F32),
        pltpu.VMEM((own, D), BF16),
        pltpu.VMEM((N, F), BF16),
        pltpu.VMEM((T, 8, HD), F32),
        pltpu.VMEM((N, HD), F32),
        pltpu.VMEM((N, F), BF16),
        pltpu.VMEM((F, T * HD), BF16),
        pltpu.VMEM((F, T * HD), BF16),
        pltpu.VMEM((T * HD, F), BF16),
        pltpu.VMEM((N, T * HD), BF16),
        pltpu.VMEM((T, N, 2 * HD), BF16),
        pltpu.VMEM((S, T * HD), F32),
        pltpu.VMEM((T, S, 2 * HD), F32),
        pltpu.VMEM((S, T * HD), BF16),
        pltpu.VMEM((G * S, F), BF16),
        pltpu.VMEM((T, Q, G * S), F32),
        pltpu.VMEM((T, 8, G * S), F32),
        pltpu.VMEM((S, T * HD), F32),
        pltpu.VMEM((T, S, 2 * HD), F32),
        pltpu.VMEM((N, T * HD), BF16),
        pltpu.VMEM((S, T * HD), BF16),
        pltpu.VMEM((T, 8, N), F32),
        pltpu.VMEM((N, F), F32),
        pltpu.VMEM((N, F), BF16),
        pltpu.SemaphoreType.DMA((12 + CHUNKS,)),
        pltpu.SemaphoreType.DMA((14 + CHUNKS, T - 1)),
        pltpu.SemaphoreType.DMA((14 + CHUNKS, T - 1)),
        pltpu.SemaphoreType.DMA((9, T - 1)),
        pltpu.SemaphoreType.DMA((9, T - 1)),
        pltpu.SemaphoreType.DMA((Z,)),
        pltpu.SemaphoreType.DMA((Z,)),
        pltpu.SemaphoreType.DMA((Z,)),
        pltpu.SemaphoreType.DMA((Z,)),
    ]
    d_hidden, loss = pl.pallas_call(
        functools.partial(kernel, T, G),
        out_shape=(
            jax.ShapeDtypeStruct((own, D), BF16),
            jax.ShapeDtypeStruct((1, 1), F32),
        ),
        in_specs=[hbm] * 11,
        out_specs=(anywhere, pl.BlockSpec(memory_space=pltpu.SMEM)),
        scratch_shapes=scratch,
        compiler_params=pltpu.CompilerParams(
            collective_id=0, has_side_effects=True, vmem_limit_bytes=60 * 1024 * 1024
        ),
    )(
        hidden, lengths, positives.reshape(1, Q), negatives.T, in_gain.reshape(1, D), wq, wkv,
        q_gain.reshape(1, HD), k_gain.reshape(1, HD), wo, out_gain.reshape(1, D),
    )
    return d_hidden, loss.reshape(())


def solution(mesh):
    placed = (
        P(("dp", "tensor"), None),
        P("dp", None),
        P(),
        P(),
        P(),
        P(None, "tensor"),
        P(None, "tensor"),
        P(),
        P(),
        P("tensor", None),
        P(),
    )
    return jax.shard_map(
        functools.partial(on_device, mesh.shape["tensor"], mesh.shape["dp"]),
        mesh=mesh,
        in_specs=placed,
        out_specs=(P(("dp", "tensor"), None), P()),
        check_vma=False,
    )
```

```python
import functools
import math

import jax
import jax.numpy as jnp
from jax import lax
from jax.experimental import pallas as pl
from jax.experimental.pallas import tpu as pltpu
from jax.sharding import PartitionSpec as P

QDEV = 8
EPSILON = 1e-06
SOFTMAX_TEMPER = 0.05
LOSS_MULTIPLIER = 8192.0
CHUNKS = 4
ROPE_BASE = 1000000.0

F32 = jnp.float32
BF16 = jnp.bfloat16
MESH = pl.DeviceIdType.MESH
EXACT = lax.Precision.HIGHEST


def nn(a, b, precision=None):
    return jnp.dot(a, b, preferred_element_type=F32, precision=precision)


def nt(a, b, precision=None):
    dims = (((1,), (1,)), ((), ()))
    return lax.dot_general(a, b, dims, preferred_element_type=F32, precision=precision)


def iota(shape, axis):
    return lax.broadcasted_iota(jnp.int32, shape, axis)


def onehot(mask, kind=BF16):
    return jnp.where(mask, 1.0, 0.0).astype(F32).astype(kind)


def rms_scale(x):
    return lax.rsqrt(jnp.mean(x * x, axis=-1, keepdims=True) + EPSILON)


def rope_tables(position, width):
    half = width // 2
    lane = iota((1, width), 1)
    lane = jnp.where(lane >= half, lane - half, lane).astype(F32)
    frequency = jnp.exp(lane * (-2.0 / width * math.log(ROPE_BASE)))
    angles = position * frequency
    return jnp.cos(angles), jnp.sin(angles)


def rotate(x, cosine, sine):
    half = x.shape[-1] // 2
    sign = jnp.where(iota((1, x.shape[-1]), 1) < half, -1.0, 1.0)
    return x * cosine + pltpu.roll(x, half, 1) * sign * sine


def head_forward(raw, gain, cosine, sine):
    inverse = rms_scale(raw)
    unit = raw * inverse
    return unit, inverse, rotate(unit * gain, cosine, sine)


def head_backward(grad, unit, inverse, gain, cosine, sine):
    scaled = rotate(grad, cosine, -sine) * gain
    return inverse * (scaled - unit * jnp.mean(unit * scaled, axis=-1, keepdims=True))


def kernel(
    tensors, groups,
    hidden, lens_in, positives_in, negatives_in, in_gain, wq, wkv, q_gain, k_gain, wo, out_gain,
    out, loss, lens, positives, negatives, gains, head_gains,
    hid_own, hid_all, inv_rows, inv_all, normed, wkv_all, wq_all, wo_all,
    kvp_out, kvp_in, qp_out, qp_in, hid_seqs, attn_seqs, plain, embeds, logit_all, stats_all,
    dap_out, dap_in, dkv_all, dq_all, rows_all, addend, out16,
    local_sem, tsend, trecv, fsend, frecv, zsend, zrecv, psend, precv,
):
    T, G = tensors, groups
    Z = G // 2
    own, D = hidden.shape
    F = D // T
    HD = wq.shape[1]
    N = own * T
    S = lens_in.shape[1]
    Q = positives_in.shape[1]
    H = F // 4
    HH = HD // 4
    root = math.sqrt(HD)
    t = lax.axis_index("tensor")
    g = lax.axis_index("dp")
    zz = g // 2
    core = g % 2
    buddy = g + 1 - 2 * core
    z_mate = (zz + 1 - 2 * (zz % 2)) * 2 + core
    quarter = (zz % 2) * 2 + core
    far_quarter = (1 - zz % 2) * 2 + core
    even = t % 2 == 0
    peers = [lax.rem(t + k, T) for k in range(1, T)]
    sources = [lax.rem(t + T - k, T) for k in range(1, T)]
    slots = list(range(T))
    columns = pl.ds(pl.multiple_of(t * F, 128), F)

    def block(p):
        return pl.ds(pl.multiple_of(p * HD, 128), HD)

    own_copies = [
        pltpu.make_async_copy(hidden, hid_own, local_sem.at[0]),
        pltpu.make_async_copy(
            hidden.at[:, columns], hid_all.at[pl.ds(t * own, own)], local_sem.at[1]
        ),
        pltpu.make_async_copy(wkv.at[pl.ds(t * F, F)], wkv_all.at[:, block(t)], local_sem.at[2]),
        pltpu.make_async_copy(wq.at[pl.ds(t * F, F)], wq_all.at[:, block(t)], local_sem.at[3]),
        pltpu.make_async_copy(wo.at[:, columns], wo_all.at[block(t)], local_sem.at[4]),
        pltpu.make_async_copy(lens_in, lens, local_sem.at[5]),
        pltpu.make_async_copy(positives_in, positives, local_sem.at[6]),
        pltpu.make_async_copy(negatives_in, negatives, local_sem.at[7]),
        pltpu.make_async_copy(in_gain.at[:, columns], gains.at[0], local_sem.at[8]),
        pltpu.make_async_copy(out_gain.at[:, columns], gains.at[1], local_sem.at[9]),
        pltpu.make_async_copy(q_gain, head_gains.at[0], local_sem.at[10]),
        pltpu.make_async_copy(k_gain, head_gains.at[1], local_sem.at[11]),
    ]
    for copy in own_copies:
        copy.start()

    barrier = pltpu.get_barrier_semaphore()
    for p in peers:
        pl.semaphore_signal(barrier, inc=1, device_id=(g, p), device_id_type=MESH)
    for k in range(1, Z):
        far = lax.rem(zz + k, Z) * 2 + core
        pl.semaphore_signal(barrier, inc=1, device_id=(far, t), device_id_type=MESH)
    pl.semaphore_signal(barrier, inc=1, device_id=(buddy, t), device_id_type=MESH)
    pl.semaphore_wait(barrier, T - 1 + Z - 1 + 1)

    waits = []

    def to_peer(kind, k, src, dst):
        copy = pltpu.make_async_remote_copy(
            src_ref=src, dst_ref=dst, send_sem=tsend.at[kind, k], recv_sem=trecv.at[kind, k],
            device_id=(g, peers[k]), device_id_type=MESH,
        )
        copy.start()
        waits.append(copy)
        return copy

    def pass_on(kind, k, spot, target):
        copy = pltpu.make_async_remote_copy(
            src_ref=spot, dst_ref=spot, send_sem=fsend.at[kind, k], recv_sem=frecv.at[kind, k],
            device_id=(target, t), device_id_type=MESH,
        )
        copy.start()
        waits.append(copy)
        return copy

    def landed(copies):
        for copy in copies:
            copy.wait_recv()

    rest = range(T - 1)
    my_rows = pl.ds(pl.multiple_of(t * own, own), own)

    def cols(p):
        return pl.ds(pl.multiple_of(p * F, 128), F)

    def tall_spot(ref):
        def spot(source, part):
            return ref.at[pl.ds(pl.multiple_of(part * H, H), H), block(source)]

        return spot

    def wide_spot(source, part):
        return wo_all.at[pl.ds(pl.multiple_of(source * HD + part * HH, HH), HH)]

    def own_tall(ref, p):
        return ref.at[pl.ds(pl.multiple_of(p * F + quarter * H, H), H)]

    def own_wide(p):
        return wo.at[pl.ds(pl.multiple_of(quarter * HH, HH), HH), cols(p)]

    def spread(kind, fetched, spot):
        near, along = [], []
        for k in rest:
            fetched[k].wait_recv()
            mine = spot(sources[k], quarter)
            along.append(pass_on(kind, k, mine, z_mate))
            near.append(pass_on(kind + 1, k, mine, buddy))
        return near, along

    def finish(kind, begun, spot):
        near, along = begun
        for k in rest:
            along[k].wait_recv()
            near.append(pass_on(kind + 2, k, spot(sources[k], far_quarter), buddy))
        landed(near)

    my_seqs = pl.ds(pl.multiple_of(g * S, S), S)

    def chip_copy(row, index, spot):
        copy = pltpu.make_async_remote_copy(
            src_ref=spot, dst_ref=spot, send_sem=psend.at[row, index],
            recv_sem=precv.at[row, index], device_id=(buddy, t), device_id_type=MESH,
        )
        copy.start()
        waits.append(copy)
        return copy

    def gather_seqs(row, ref):
        mine = ref.at[my_seqs]
        copies = []
        for k in range(1, Z):
            far = lax.rem(zz + k, Z) * 2 + core
            copy = pltpu.make_async_remote_copy(
                src_ref=mine, dst_ref=mine, send_sem=zsend.at[row, k],
                recv_sem=zrecv.at[row, k], device_id=(far, t), device_id_type=MESH,
            )
            copy.start()
            waits.append(copy)
            copies.append(copy)
        return copies, [chip_copy(row, 0, mine)]

    def share_seqs(row, ref, begun):
        copies, shared = begun
        for k in range(1, Z):
            copies[k - 1].wait_recv()
            origin = lax.rem(zz + Z - k, Z) * 2 + core
            spot = ref.at[pl.ds(pl.multiple_of(origin * S, S), S)]
            shared.append(chip_copy(row, k, spot))
        return shared

    wkv_spot, wq_spot = tall_spot(wkv_all), tall_spot(wq_all)
    wkv_copies = [
        to_peer(1, k, own_tall(wkv, peers[k]), wkv_spot(t, quarter)) for k in rest
    ]
    hid_copies = [
        to_peer(0, k, hidden.at[:, cols(peers[k])], hid_all.at[my_rows]) for k in rest
    ]

    own_copies[0].wait()
    mine = hid_own[...].astype(F32)
    diagonal = iota((own, HD), 0) == iota((own, HD), 1)
    inv_rows[t] = jnp.broadcast_to(
        jnp.sum(jnp.where(diagonal, rms_scale(mine), 0.0), axis=0, keepdims=True), (8, HD)
    )
    inv_copies = [to_peer(2, k, inv_rows.at[t], inv_rows.at[t]) for k in rest]

    wkv_begun = spread(0, wkv_copies, wkv_spot)
    for copy in own_copies[5:]:
        copy.wait()

    lens_row = lens[...].astype(F32)
    square_r, square_c = iota((S, S), 0), iota((S, S), 1)
    lens_col = jnp.sum(jnp.where(square_r == square_c, lens_row, 0.0), axis=1, keepdims=True)
    ends_col = jnp.sum(jnp.where(square_c <= square_r, lens_row, 0.0), axis=1, keepdims=True)
    ends_row = jnp.sum(jnp.where(square_r <= square_c, lens_col, 0.0), axis=0, keepdims=True)
    starts_col, starts_row = ends_col - lens_col, ends_row - lens_row
    token_row = iota((S, N), 1).astype(F32)
    token_col = iota((N, S), 0).astype(F32)
    both_starts = jnp.concatenate([starts_col, starts_col], axis=0)
    both_ends = jnp.concatenate([ends_col, ends_col], axis=0)
    both_row = iota((2 * S, N), 1).astype(F32)
    inside = (both_row >= both_starts) & (both_row < both_ends)
    inside_t = (token_col >= starts_row) & (token_col < ends_row)
    offset = jnp.sum(jnp.where(inside_t, starts_row, 0.0), axis=1, keepdims=True)
    position = iota((N, 1), 0).astype(F32) - offset
    is_last = token_row == ends_col - 1.0
    last_hot = onehot(is_last)
    last_hot_t = onehot(token_col == ends_row - 1.0)
    cos_key, sin_key = rope_tables(position, HD)
    cos_query, sin_query = rope_tables(both_ends - both_starts - 1.0, HD)
    qg, kg = head_gains[0], head_gains[1]
    shift = root * jnp.max(qg, axis=1, keepdims=True) * jnp.max(kg, axis=1, keepdims=True)
    gain, ogain = gains[0], gains[1]
    eye_n = iota((N, N), 0) == iota((N, N), 1)
    eye16 = onehot(eye_n)

    wq_copies = [to_peer(3, k, own_tall(wq, peers[k]), wq_spot(t, quarter)) for k in rest]
    finish(0, wkv_begun, wkv_spot)
    own_copies[1].wait()
    landed(hid_copies)
    landed(inv_copies)
    for s in slots:
        rows = slice(s * own, (s + 1) * own)
        inverse = jnp.sum(
            jnp.where(diagonal, inv_rows[s, 0:1, :], 0.0), axis=1, keepdims=True
        )
        inv_all[rows, :] = jnp.broadcast_to(inverse, (own, HD))
        normed[rows, :] = (hid_all[rows, :].astype(F32) * inverse * gain).astype(BF16)
    own_copies[2].wait()
    kvp_out[...] = nn(normed[...], wkv_all[...]).astype(BF16)

    wq_begun = spread(3, wq_copies, wq_spot)

    def pair(p):
        return pl.ds(pl.multiple_of((p // 2) * (2 * HD), 256), 2 * HD)

    kvp_copies = [
        to_peer(4, k, kvp_out.at[:, pair(peers[k])], kvp_in.at[t]) for k in rest
    ]
    kvp_in[t] = kvp_out[:, pair(t)]

    last16 = nn(last_hot, normed[...]).astype(BF16)
    own_copies[3].wait()
    finish(3, wq_begun, wq_spot)
    qp_out[...] = nn(last16, wq_all[...])
    qp_copies = [to_peer(6, k, qp_out.at[:, pair(peers[k])], qp_in.at[t]) for k in rest]
    qp_in[t] = qp_out[:, pair(t)]
    wo_copies = [to_peer(5, k, own_wide(peers[k]), wide_spot(t, quarter)) for k in rest]
    hid_seqs[my_seqs, :] = nn(last_hot, hid_all[...]).astype(BF16)
    hid_begun = gather_seqs(0, hid_seqs)
    inverse_last = nn(last_hot.astype(F32), inv_all[...], EXACT)[:, 0:1]

    landed(kvp_copies)
    key_raw = kvp_in[0, :, 0:HD].astype(F32)
    value_raw = kvp_in[0, :, HD : 2 * HD].astype(F32)
    for s in slots[1:]:
        key_raw = key_raw + kvp_in[s, :, 0:HD].astype(F32)
        value_raw = value_raw + kvp_in[s, :, HD : 2 * HD].astype(F32)
    value16 = value_raw.astype(BF16)
    key_unit, key_inverse, key_rot = head_forward(key_raw, kg, cos_key, sin_key)
    key16 = key_rot.astype(BF16)

    landed(qp_copies)
    query_raw = qp_in[0]
    for s in slots[1:]:
        query_raw = query_raw + qp_in[s]
    query_raw = jnp.concatenate([query_raw[:, :HD], query_raw[:, HD:]], axis=0)
    query_unit, query_inverse, query_rot = head_forward(query_raw, qg, cos_query, sin_query)
    query16 = query_rot.astype(BF16)
    scores = nt(query16, key16) / root
    wo_begun = spread(6, wo_copies, wide_spot)
    weight = jnp.where(inside, jnp.exp(scores - shift), 0.0)
    probs = weight / jnp.sum(weight, axis=-1, keepdims=True)
    probs16 = probs.astype(BF16)
    attn = nn(probs16, value16)
    attn_seqs[my_seqs, block(t)] = jnp.where(even, attn[:S], attn[S:]).astype(BF16)
    my_attn = attn_seqs.at[my_seqs, block(t)]
    attn_copies = [to_peer(10, k, my_attn, my_attn) for k in rest]

    landed(attn_copies)
    attn_begun = gather_seqs(1, attn_seqs)
    finish(6, wo_begun, wide_spot)
    own_copies[4].wait()
    hid_shared = share_seqs(0, hid_seqs, hid_begun)

    resid = hid_seqs[my_seqs, :].astype(F32) + nn(attn_seqs[my_seqs, :], wo_all[...])
    E = G * S
    seq_of = iota((1, E), 1) % S
    passage = jnp.where(seq_of >= QDEV, (iota((1, E), 1) // S) * (S - QDEV) + seq_of - QDEV, -1)
    eye_q = iota((Q, Q), 0) == iota((Q, Q), 1)

    def chosen(row):
        column = jnp.sum(jnp.where(eye_q, row.astype(F32), 0.0), axis=1, keepdims=True)
        return column.astype(jnp.int32) == passage

    pos_hot = chosen(positives[...])
    hard = chosen(negatives[0:1, :])
    for j in range(1, negatives.shape[0]):
        hard = hard | chosen(negatives[j : j + 1, :])
    positive_f = jnp.where(pos_hot, 1.0, 0.0)
    allowed = (jnp.max(positive_f, axis=0, keepdims=True) > 0.5) | hard
    q_id = iota((Q, E), 0)
    pick = iota((Q, E), 1) == (q_id // QDEV) * S + q_id % QDEV
    pick_q = onehot(pick)
    eye_e = iota((E, E), 0) == iota((E, E), 1)
    row_s = iota((S, Q), 0)
    own_q = (row_s < QDEV) & (iota((S, Q), 1) == g * QDEV + row_s)
    own_p = iota((S, E), 1) == g * S + iota((S, E), 0)
    own_q16, own_p16 = onehot(own_q), onehot(own_p)

    attn_shared = share_seqs(1, attn_seqs, attn_begun)
    landed(hid_shared)
    landed(attn_shared)

    every = hid_seqs[...].astype(F32) + nn(attn_seqs[...], wo_all[...])
    embeds[...] = (every * ogain).astype(BF16)
    plain[...] = every.astype(BF16)
    queries = nn(pick_q, embeds[...]).astype(BF16)
    logit_all[t] = nt(queries, embeds[...])
    logit_copies = [to_peer(9, k, logit_all.at[t], logit_all.at[t]) for k in rest]
    plain_sq = jnp.sum(jnp.where(eye_e, nt(plain[...], plain[...]), 0.0), axis=0, keepdims=True)
    scaled_sq = jnp.sum(
        jnp.where(eye_e, nt(embeds[...], embeds[...]), 0.0), axis=0, keepdims=True
    )
    stats_all[t] = jnp.where(iota((8, E), 0) == 0, plain_sq, scaled_sq)
    stats_copies = [to_peer(7, k, stats_all.at[t], stats_all.at[t]) for k in rest]
    landed(logit_copies)
    landed(stats_copies)
    raw_dots, stats = logit_all[0], stats_all[0]
    for s in slots[1:]:
        raw_dots = raw_dots + logit_all[s]
        stats = stats + stats_all[s]
    inverse_row = lax.rsqrt(stats[0:1] / D + EPSILON)
    final_row = lax.rsqrt(inverse_row * inverse_row * stats[1:2] + EPSILON)
    scale_row = inverse_row * final_row
    scale_q = jnp.sum(jnp.where(pick, scale_row, 0.0), axis=1, keepdims=True)
    resid_inverse = jnp.sum(jnp.where(own_p, inverse_row, 0.0), axis=1, keepdims=True)
    final_inverse = jnp.sum(jnp.where(own_p, final_row, 0.0), axis=1, keepdims=True)
    resid_unit = resid * resid_inverse
    embed = resid_unit * ogain * final_inverse
    dots_q, dots_p = raw_dots * scale_q, raw_dots * scale_row
    logits = dots_q * scale_row / SOFTMAX_TEMPER
    grown = jnp.where(allowed, jnp.exp(logits - 1.0 / SOFTMAX_TEMPER), 0.0)
    totals = jnp.sum(grown, axis=1, keepdims=True)
    factor = LOSS_MULTIPLIER / (Q * SOFTMAX_TEMPER)
    coef = factor * (grown / totals - positive_f)
    coef_q16 = (coef * scale_row).astype(BF16)
    coef_p16 = (coef * scale_q).astype(BF16)
    coef_q = nn(own_q16, coef_q16).astype(BF16)
    coef_p = nt(own_p16, coef_p16).astype(BF16)
    d_embed = nn(coef_q, embeds[...]) + nn(coef_p, queries)
    along_q = jnp.sum(coef_q16.astype(F32) * dots_q, axis=1, keepdims=True)
    along_p = jnp.sum(coef_p16.astype(F32) * dots_p, axis=0, keepdims=True)
    along_q = jnp.sum(jnp.where(eye_q, along_q, 0.0), axis=0, keepdims=True)
    inner = jnp.sum(jnp.where(own_q, along_q, 0.0), axis=1, keepdims=True) + jnp.sum(
        jnp.where(own_p, along_p, 0.0), axis=1, keepdims=True
    )
    d_final = final_inverse * (d_embed - embed * inner)
    middle = inner * (EPSILON / D) * final_inverse * final_inverse
    d_resid = resid_inverse * (ogain * d_final - resid_unit * middle)
    d_resid16 = d_resid.astype(BF16)

    dap_out[...] = nt(d_resid16, wo_all[...])
    dap_copies = [to_peer(11, k, dap_out.at[:, pair(peers[k])], dap_in.at[t]) for k in rest]
    dap_in[t] = dap_out[:, pair(t)]
    target = jnp.sum(jnp.where(pos_hot, logits, 0.0), axis=1, keepdims=True)
    loss[0, 0] = jnp.sum(jnp.log(totals) + 1.0 / SOFTMAX_TEMPER - target) / Q
    probs16_t = nt(eye16, probs16).astype(BF16)
    landed(dap_copies)
    d_attn = dap_in[0]
    for s in slots[1:]:
        d_attn = d_attn + dap_in[s]
    d_attn16 = jnp.concatenate([d_attn[:, :HD], d_attn[:, HD:]], axis=0).astype(BF16)
    d_probs = nt(d_attn16, value16)
    d_scores16 = (
        probs * (d_probs - jnp.sum(probs * d_probs, axis=-1, keepdims=True)) / root
    ).astype(BF16)
    d_key_rot = nn(nt(eye16, d_scores16).astype(BF16), query16)
    d_value = nn(probs16_t, d_attn16)
    d_key_raw = head_backward(d_key_rot, key_unit, key_inverse, kg, cos_key, sin_key)
    column16 = jnp.where(even, d_key_raw, d_value).astype(BF16)
    dkv_all[:, block(t)] = column16
    my_dkv = dkv_all.at[:, block(t)]
    dkv_copies = [to_peer(12, k, my_dkv, my_dkv) for k in rest]
    d_query_rot = nn(d_scores16, key16)
    d_query_raw = head_backward(
        d_query_rot, query_unit, query_inverse, qg, cos_query, sin_query
    )
    d_query16 = jnp.where(even, d_query_raw[:S], d_query_raw[S:]).astype(BF16)
    dq_all[:, block(t)] = d_query16
    my_dq = dq_all.at[:, block(t)]
    dq_copies = [to_peer(13, k, my_dq, my_dq) for k in rest]
    raw = jnp.where(even, key_raw, value_raw)
    kv_sums = jnp.sum(column16.astype(F32) * raw, axis=1, keepdims=True)
    own_query = jnp.where(even, query_raw[:S], query_raw[S:])
    query_sums = jnp.sum(d_query16.astype(F32) * own_query, axis=1, keepdims=True)
    rows_all[t] = jnp.broadcast_to(
        jnp.sum(jnp.where(eye_n, kv_sums, 0.0), axis=0, keepdims=True)
        + jnp.sum(jnp.where(is_last, query_sums, 0.0), axis=0, keepdims=True),
        (8, N),
    )
    row_copies = [to_peer(8, k, rows_all.at[t], rows_all.at[t]) for k in rest]
    landed(dq_copies)
    extra = inverse_last * gain * nt(dq_all[...], wq_all[...]) + d_resid
    extra16 = extra.astype(BF16)
    extra_low = (extra - extra16.astype(F32)).astype(BF16)
    addend[...] = nn(last_hot_t, extra16) + nn(last_hot_t, extra_low)
    landed(row_copies)
    row_sums = rows_all[0]
    for s in slots[1:]:
        row_sums = row_sums + rows_all[s]
    mean = jnp.sum(jnp.where(eye_n, row_sums[0:1, :], 0.0), axis=1, keepdims=True) / D
    inverse = inv_all[:, 0:1]
    landed(dkv_copies)
    out_copies, local, earlier = [], [], list(waits)
    FC = F // CHUNKS if F % (128 * CHUNKS) == 0 else F // 2
    for c in range(F // FC):
        span = slice(c * FC, (c + 1) * FC)
        there = pl.ds(pl.multiple_of(t * F + c * FC, 128), FC)
        d_normed = nt(dkv_all[...], wkv_all[span, :])
        unit = hid_all[:, span].astype(F32) * inverse
        grad = inverse * (d_normed * gain[:, span] - unit * mean) + addend[:, span]
        out16[:, span] = grad.astype(BF16)
        for k in rest:
            rows = pl.ds(pl.multiple_of(peers[k] * own, own), own)
            out_copies.append(to_peer(14 + c, k, out16.at[rows, span], out.at[:, there]))
        copy = pltpu.make_async_copy(
            out16.at[my_rows, span], out.at[:, there], local_sem.at[12 + c]
        )
        copy.start()
        local.append(copy)
    for copy in earlier:
        copy.wait_send()
    for copy in local:
        copy.wait()
    for copy in out_copies:
        copy.wait()


def on_device(
    tensors, groups,
    hidden, lengths, positives, negatives, in_gain, wq, wkv, q_gain, k_gain, wo, out_gain
):
    T, G = tensors, groups
    own, D = hidden.shape
    F = D // T
    HD = wq.shape[1]
    N = own * T
    S = lengths.shape[1]
    Q = positives.shape[0]
    Z = G // 2
    hbm = pl.BlockSpec(memory_space=pltpu.HBM)
    anywhere = pl.BlockSpec(memory_space=pl.ANY)
    scratch = [
        pltpu.VMEM((1, S), jnp.int32),
        pltpu.VMEM((1, Q), jnp.int32),
        pltpu.VMEM((negatives.shape[1], Q), jnp.int32),
        pltpu.VMEM((2, 1, F), F32),
        pltpu.VMEM((2, 1, HD), F32),
        pltpu.VMEM((own, D), BF16),
        pltpu.VMEM((N, F), BF16),
        pltpu.VMEM((T, 8, HD), F32),
        pltpu.VMEM((N, HD), F32),
        pltpu.VMEM((N, F), BF16),
        pltpu.VMEM((F, T * HD), BF16),
        pltpu.VMEM((F, T * HD), BF16),
        pltpu.VMEM((T * HD, F), BF16),
        pltpu.VMEM((N, T * HD), BF16),
        pltpu.VMEM((T, N, 2 * HD), BF16),
        pltpu.VMEM((S, T * HD), F32),
        pltpu.VMEM((T, S, 2 * HD), F32),
        pltpu.VMEM((G * S, F), BF16),
        pltpu.VMEM((G * S, T * HD), BF16),
        pltpu.VMEM((G * S, F), BF16),
        pltpu.VMEM((G * S, F), BF16),
        pltpu.VMEM((T, Q, G * S), F32),
        pltpu.VMEM((T, 8, G * S), F32),
        pltpu.VMEM((S, T * HD), F32),
        pltpu.VMEM((T, S, 2 * HD), F32),
        pltpu.VMEM((N, T * HD), BF16),
        pltpu.VMEM((S, T * HD), BF16),
        pltpu.VMEM((T, 8, N), F32),
        pltpu.VMEM((N, F), F32),
        pltpu.VMEM((N, F), BF16),
        pltpu.SemaphoreType.DMA((12 + CHUNKS,)),
        pltpu.SemaphoreType.DMA((14 + CHUNKS, T - 1)),
        pltpu.SemaphoreType.DMA((14 + CHUNKS, T - 1)),
        pltpu.SemaphoreType.DMA((9, T - 1)),
        pltpu.SemaphoreType.DMA((9, T - 1)),
        pltpu.SemaphoreType.DMA((2, Z)),
        pltpu.SemaphoreType.DMA((2, Z)),
        pltpu.SemaphoreType.DMA((2, Z)),
        pltpu.SemaphoreType.DMA((2, Z)),
    ]
    d_hidden, loss = pl.pallas_call(
        functools.partial(kernel, T, G),
        out_shape=(
            jax.ShapeDtypeStruct((own, D), BF16),
            jax.ShapeDtypeStruct((1, 1), F32),
        ),
        in_specs=[hbm] * 11,
        out_specs=(anywhere, pl.BlockSpec(memory_space=pltpu.SMEM)),
        scratch_shapes=scratch,
        compiler_params=pltpu.CompilerParams(
            collective_id=0, has_side_effects=True, vmem_limit_bytes=60 * 1024 * 1024
        ),
    )(
        hidden, lengths, positives.reshape(1, Q), negatives.T, in_gain.reshape(1, D), wq, wkv,
        q_gain.reshape(1, HD), k_gain.reshape(1, HD), wo, out_gain.reshape(1, D),
    )
    return d_hidden, loss.reshape(())


def solution(mesh):
    placed = (
        P(("dp", "tensor"), None),
        P("dp", None),
        P(),
        P(),
        P(),
        P(None, "tensor"),
        P(None, "tensor"),
        P(),
        P(),
        P("tensor", None),
        P(),
    )
    return jax.shard_map(
        functools.partial(on_device, mesh.shape["tensor"], mesh.shape["dp"]),
        mesh=mesh,
        in_specs=placed,
        out_specs=(P(("dp", "tensor"), None), P()),
        check_vma=False,
    )
```

```python
import functools
import math

import jax
import jax.numpy as jnp
from jax import lax
from jax.experimental import pallas as pl
from jax.experimental.pallas import tpu as pltpu
from jax.sharding import PartitionSpec as P

QDEV = 8
EPSILON = 1e-06
SOFTMAX_TEMPER = 0.05
LOSS_MULTIPLIER = 8192.0
CHUNKS = 4
ROPE_BASE = 1000000.0

F32 = jnp.float32
BF16 = jnp.bfloat16
MESH = pl.DeviceIdType.MESH
EXACT = lax.Precision.HIGHEST


def nn(a, b, precision=None):
    return jnp.dot(a, b, preferred_element_type=F32, precision=precision)


def nt(a, b, precision=None):
    dims = (((1,), (1,)), ((), ()))
    return lax.dot_general(a, b, dims, preferred_element_type=F32, precision=precision)


def iota(shape, axis):
    return lax.broadcasted_iota(jnp.int32, shape, axis)


def onehot(mask, kind=BF16):
    return jnp.where(mask, 1.0, 0.0).astype(F32).astype(kind)


def rms_scale(x):
    return lax.rsqrt(jnp.mean(x * x, axis=-1, keepdims=True) + EPSILON)


def rope_tables(position, width):
    half = width // 2
    lane = iota((1, width), 1)
    lane = jnp.where(lane >= half, lane - half, lane).astype(F32)
    frequency = jnp.exp(lane * (-2.0 / width * math.log(ROPE_BASE)))
    angles = position * frequency
    return jnp.cos(angles), jnp.sin(angles)


def rotate(x, cosine, sine):
    half = x.shape[-1] // 2
    sign = jnp.where(iota((1, x.shape[-1]), 1) < half, -1.0, 1.0)
    return x * cosine + pltpu.roll(x, half, 1) * sign * sine


def head_forward(raw, gain, cosine, sine):
    inverse = rms_scale(raw)
    unit = raw * inverse
    return unit, inverse, rotate(unit * gain, cosine, sine)


def head_backward(grad, unit, inverse, gain, cosine, sine):
    scaled = rotate(grad, cosine, -sine) * gain
    return inverse * (scaled - unit * jnp.mean(unit * scaled, axis=-1, keepdims=True))


def kernel(
    tensors, groups,
    hidden, lens_in, positives_in, negatives_in, in_gain, wq, wkv, q_gain, k_gain, wo, out_gain,
    out, loss, lens, positives, negatives, gains, head_gains,
    hid_own, hid_all, inv_rows, inv_all, normed, wkv_all, wq_all, wo_all,
    kvp_out, kvp_in, qp_out, qp_in, hid_seqs, attn_seqs, plain, embeds, logit_all, stats_all,
    dap_out, dap_in, dkv_all, dq_all, rows_all, addend, out16,
    local_sem, tsend, trecv, fsend, frecv, zsend, zrecv, psend, precv,
):
    T, G = tensors, groups
    Z = G // 2
    own, D = hidden.shape
    F = D // T
    HD = wq.shape[1]
    N = own * T
    S = lens_in.shape[1]
    Q = positives_in.shape[1]
    H = F // 4
    HH = HD // 4
    root = math.sqrt(HD)
    t = lax.axis_index("tensor")
    g = lax.axis_index("dp")
    zz = g // 2
    core = g % 2
    buddy = g + 1 - 2 * core
    z_mate = (zz + 1 - 2 * (zz % 2)) * 2 + core
    quarter = (zz % 2) * 2 + core
    far_quarter = (1 - zz % 2) * 2 + core
    even = t % 2 == 0
    peers = [lax.rem(t + k, T) for k in range(1, T)]
    sources = [lax.rem(t + T - k, T) for k in range(1, T)]
    slots = list(range(T))
    columns = pl.ds(pl.multiple_of(t * F, 128), F)

    def block(p):
        return pl.ds(pl.multiple_of(p * HD, 128), HD)

    own_copies = [
        pltpu.make_async_copy(hidden, hid_own, local_sem.at[0]),
        pltpu.make_async_copy(
            hidden.at[:, columns], hid_all.at[pl.ds(t * own, own)], local_sem.at[1]
        ),
        pltpu.make_async_copy(wkv.at[pl.ds(t * F, F)], wkv_all.at[:, block(t)], local_sem.at[2]),
        pltpu.make_async_copy(wq.at[pl.ds(t * F, F)], wq_all.at[:, block(t)], local_sem.at[3]),
        pltpu.make_async_copy(wo.at[:, columns], wo_all.at[block(t)], local_sem.at[4]),
        pltpu.make_async_copy(lens_in, lens, local_sem.at[5]),
        pltpu.make_async_copy(positives_in, positives, local_sem.at[6]),
        pltpu.make_async_copy(negatives_in, negatives, local_sem.at[7]),
        pltpu.make_async_copy(in_gain.at[:, columns], gains.at[0], local_sem.at[8]),
        pltpu.make_async_copy(out_gain.at[:, columns], gains.at[1], local_sem.at[9]),
        pltpu.make_async_copy(q_gain, head_gains.at[0], local_sem.at[10]),
        pltpu.make_async_copy(k_gain, head_gains.at[1], local_sem.at[11]),
    ]
    for copy in own_copies:
        copy.start()

    barrier = pltpu.get_barrier_semaphore()
    for p in peers:
        pl.semaphore_signal(barrier, inc=1, device_id=(g, p), device_id_type=MESH)
    for k in range(1, Z):
        far = lax.rem(zz + k, Z) * 2 + core
        pl.semaphore_signal(barrier, inc=1, device_id=(far, t), device_id_type=MESH)
    pl.semaphore_signal(barrier, inc=1, device_id=(buddy, t), device_id_type=MESH)
    pl.semaphore_wait(barrier, T - 1 + Z - 1 + 1)

    waits = []

    def to_peer(kind, k, src, dst):
        copy = pltpu.make_async_remote_copy(
            src_ref=src, dst_ref=dst, send_sem=tsend.at[kind, k], recv_sem=trecv.at[kind, k],
            device_id=(g, peers[k]), device_id_type=MESH,
        )
        copy.start()
        waits.append(copy)
        return copy

    def pass_on(kind, k, spot, target):
        copy = pltpu.make_async_remote_copy(
            src_ref=spot, dst_ref=spot, send_sem=fsend.at[kind, k], recv_sem=frecv.at[kind, k],
            device_id=(target, t), device_id_type=MESH,
        )
        copy.start()
        waits.append(copy)
        return copy

    def landed(copies):
        for copy in copies:
            copy.wait_recv()

    rest = range(T - 1)
    my_rows = pl.ds(pl.multiple_of(t * own, own), own)

    def cols(p):
        return pl.ds(pl.multiple_of(p * F, 128), F)

    def tall_spot(ref):
        def spot(source, part):
            return ref.at[pl.ds(pl.multiple_of(part * H, H), H), block(source)]

        return spot

    def wide_spot(source, part):
        return wo_all.at[pl.ds(pl.multiple_of(source * HD + part * HH, HH), HH)]

    def own_tall(ref, p):
        return ref.at[pl.ds(pl.multiple_of(p * F + quarter * H, H), H)]

    def own_wide(p):
        return wo.at[pl.ds(pl.multiple_of(quarter * HH, HH), HH), cols(p)]

    def spread(kind, fetched, spot):
        near, along = [], []
        for k in rest:
            fetched[k].wait_recv()
            mine = spot(sources[k], quarter)
            along.append(pass_on(kind, k, mine, z_mate))
            near.append(pass_on(kind + 1, k, mine, buddy))
        return near, along

    def finish(kind, begun, spot):
        near, along = begun
        for k in rest:
            along[k].wait_recv()
            near.append(pass_on(kind + 2, k, spot(sources[k], far_quarter), buddy))
        landed(near)

    my_seqs = pl.ds(pl.multiple_of(g * S, S), S)

    def chip_copy(row, index, spot):
        copy = pltpu.make_async_remote_copy(
            src_ref=spot, dst_ref=spot, send_sem=psend.at[row, index],
            recv_sem=precv.at[row, index], device_id=(buddy, t), device_id_type=MESH,
        )
        copy.start()
        waits.append(copy)
        return copy

    def gather_seqs(row, ref):
        mine = ref.at[my_seqs]
        copies = []
        for k in range(1, Z):
            far = lax.rem(zz + k, Z) * 2 + core
            copy = pltpu.make_async_remote_copy(
                src_ref=mine, dst_ref=mine, send_sem=zsend.at[row, k],
                recv_sem=zrecv.at[row, k], device_id=(far, t), device_id_type=MESH,
            )
            copy.start()
            waits.append(copy)
            copies.append(copy)
        return copies, [chip_copy(row, 0, mine)]

    def share_seqs(row, ref, begun):
        copies, shared = begun
        for k in range(1, Z):
            copies[k - 1].wait_recv()
            origin = lax.rem(zz + Z - k, Z) * 2 + core
            spot = ref.at[pl.ds(pl.multiple_of(origin * S, S), S)]
            shared.append(chip_copy(row, k, spot))
        return shared

    wkv_spot, wq_spot = tall_spot(wkv_all), tall_spot(wq_all)
    wkv_copies = [
        to_peer(1, k, own_tall(wkv, peers[k]), wkv_spot(t, quarter)) for k in rest
    ]
    hid_copies = [
        to_peer(0, k, hidden.at[:, cols(peers[k])], hid_all.at[my_rows]) for k in rest
    ]

    own_copies[0].wait()
    mine = hid_own[...].astype(F32)
    diagonal = iota((own, HD), 0) == iota((own, HD), 1)
    inv_rows[t] = jnp.broadcast_to(
        jnp.sum(jnp.where(diagonal, rms_scale(mine), 0.0), axis=0, keepdims=True), (8, HD)
    )
    inv_copies = [to_peer(2, k, inv_rows.at[t], inv_rows.at[t]) for k in rest]

    wkv_begun = spread(0, wkv_copies, wkv_spot)
    for copy in own_copies[5:]:
        copy.wait()

    lens_row = lens[...].astype(F32)
    square_r, square_c = iota((S, S), 0), iota((S, S), 1)
    lens_col = jnp.sum(jnp.where(square_r == square_c, lens_row, 0.0), axis=1, keepdims=True)
    ends_col = jnp.sum(jnp.where(square_c <= square_r, lens_row, 0.0), axis=1, keepdims=True)
    ends_row = jnp.sum(jnp.where(square_r <= square_c, lens_col, 0.0), axis=0, keepdims=True)
    starts_col, starts_row = ends_col - lens_col, ends_row - lens_row
    token_row = iota((S, N), 1).astype(F32)
    token_col = iota((N, S), 0).astype(F32)
    both_starts = jnp.concatenate([starts_col, starts_col], axis=0)
    both_ends = jnp.concatenate([ends_col, ends_col], axis=0)
    both_row = iota((2 * S, N), 1).astype(F32)
    inside = (both_row >= both_starts) & (both_row < both_ends)
    inside_t = (token_col >= starts_row) & (token_col < ends_row)
    offset = jnp.sum(jnp.where(inside_t, starts_row, 0.0), axis=1, keepdims=True)
    position = iota((N, 1), 0).astype(F32) - offset
    is_last = token_row == ends_col - 1.0
    last_hot = onehot(is_last)
    last_hot_t = onehot(token_col == ends_row - 1.0)
    cos_key, sin_key = rope_tables(position, HD)
    cos_query, sin_query = rope_tables(both_ends - both_starts - 1.0, HD)
    qg, kg = head_gains[0], head_gains[1]
    shift = root * jnp.max(qg, axis=1, keepdims=True) * jnp.max(kg, axis=1, keepdims=True)
    gain, ogain = gains[0], gains[1]
    eye_n = iota((N, N), 0) == iota((N, N), 1)
    eye16 = onehot(eye_n)

    wq_copies = [to_peer(3, k, own_tall(wq, peers[k]), wq_spot(t, quarter)) for k in rest]
    finish(0, wkv_begun, wkv_spot)
    own_copies[1].wait()
    own_copies[2].wait()
    for k, source in [(None, t)] + list(enumerate(sources)):
        if k is not None:
            inv_copies[k].wait_recv()
            hid_copies[k].wait_recv()
        rows = pl.ds(pl.multiple_of(source * own, own), own)
        inverse = jnp.sum(
            jnp.where(diagonal, inv_rows[source, 0:1, :], 0.0), axis=1, keepdims=True
        )
        inv_all[rows, :] = jnp.broadcast_to(inverse, (own, HD))
        part = (hid_all[rows, :].astype(F32) * inverse * gain).astype(BF16)
        normed[rows, :] = part
        kvp_out[rows, :] = nn(part, wkv_all[...]).astype(BF16)
    wq_begun = spread(3, wq_copies, wq_spot)

    def pair(p):
        return pl.ds(pl.multiple_of((p // 2) * (2 * HD), 256), 2 * HD)

    kvp_copies = [
        to_peer(4, k, kvp_out.at[:, pair(peers[k])], kvp_in.at[t]) for k in rest
    ]
    kvp_in[t] = kvp_out[:, pair(t)]

    last16 = nn(last_hot, normed[...]).astype(BF16)
    own_copies[3].wait()
    finish(3, wq_begun, wq_spot)
    qp_out[...] = nn(last16, wq_all[...])
    qp_copies = [to_peer(6, k, qp_out.at[:, pair(peers[k])], qp_in.at[t]) for k in rest]
    qp_in[t] = qp_out[:, pair(t)]
    wo_copies = [to_peer(5, k, own_wide(peers[k]), wide_spot(t, quarter)) for k in rest]
    hid_seqs[my_seqs, :] = nn(last_hot, hid_all[...]).astype(BF16)
    hid_begun = gather_seqs(0, hid_seqs)
    inverse_last = nn(last_hot.astype(F32), inv_all[...], EXACT)[:, 0:1]

    landed(kvp_copies)
    key_raw = kvp_in[0, :, 0:HD].astype(F32)
    value_raw = kvp_in[0, :, HD : 2 * HD].astype(F32)
    for s in slots[1:]:
        key_raw = key_raw + kvp_in[s, :, 0:HD].astype(F32)
        value_raw = value_raw + kvp_in[s, :, HD : 2 * HD].astype(F32)
    value16 = value_raw.astype(BF16)
    key_unit, key_inverse, key_rot = head_forward(key_raw, kg, cos_key, sin_key)
    key16 = key_rot.astype(BF16)

    landed(qp_copies)
    query_raw = qp_in[0]
    for s in slots[1:]:
        query_raw = query_raw + qp_in[s]
    query_raw = jnp.concatenate([query_raw[:, :HD], query_raw[:, HD:]], axis=0)
    query_unit, query_inverse, query_rot = head_forward(query_raw, qg, cos_query, sin_query)
    query16 = query_rot.astype(BF16)
    scores = nt(query16, key16) / root
    wo_begun = spread(6, wo_copies, wide_spot)
    weight = jnp.where(inside, jnp.exp(scores - shift), 0.0)
    probs = weight / jnp.sum(weight, axis=-1, keepdims=True)
    probs16 = probs.astype(BF16)
    attn = nn(probs16, value16)
    attn_seqs[my_seqs, block(t)] = jnp.where(even, attn[:S], attn[S:]).astype(BF16)
    my_attn = attn_seqs.at[my_seqs, block(t)]
    attn_copies = [to_peer(10, k, my_attn, my_attn) for k in rest]

    landed(attn_copies)
    attn_begun = gather_seqs(1, attn_seqs)
    finish(6, wo_begun, wide_spot)
    own_copies[4].wait()
    hid_shared = share_seqs(0, hid_seqs, hid_begun)

    resid = hid_seqs[my_seqs, :].astype(F32) + nn(attn_seqs[my_seqs, :], wo_all[...])
    E = G * S
    seq_of = iota((1, E), 1) % S
    passage = jnp.where(seq_of >= QDEV, (iota((1, E), 1) // S) * (S - QDEV) + seq_of - QDEV, -1)
    eye_q = iota((Q, Q), 0) == iota((Q, Q), 1)

    def chosen(row):
        column = jnp.sum(jnp.where(eye_q, row.astype(F32), 0.0), axis=1, keepdims=True)
        return column.astype(jnp.int32) == passage

    pos_hot = chosen(positives[...])
    hard = chosen(negatives[0:1, :])
    for j in range(1, negatives.shape[0]):
        hard = hard | chosen(negatives[j : j + 1, :])
    positive_f = jnp.where(pos_hot, 1.0, 0.0)
    allowed = (jnp.max(positive_f, axis=0, keepdims=True) > 0.5) | hard
    q_id = iota((Q, E), 0)
    pick = iota((Q, E), 1) == (q_id // QDEV) * S + q_id % QDEV
    pick_q = onehot(pick)
    eye_e = iota((E, E), 0) == iota((E, E), 1)
    row_s = iota((S, Q), 0)
    own_q = (row_s < QDEV) & (iota((S, Q), 1) == g * QDEV + row_s)
    own_p = iota((S, E), 1) == g * S + iota((S, E), 0)
    own_q16, own_p16 = onehot(own_q), onehot(own_p)

    attn_shared = share_seqs(1, attn_seqs, attn_begun)
    landed(hid_shared)
    landed(attn_shared)

    every = hid_seqs[...].astype(F32) + nn(attn_seqs[...], wo_all[...])
    embeds[...] = (every * ogain).astype(BF16)
    plain[...] = every.astype(BF16)
    queries = nn(pick_q, embeds[...]).astype(BF16)
    logit_all[t] = nt(queries, embeds[...])
    logit_copies = [to_peer(9, k, logit_all.at[t], logit_all.at[t]) for k in rest]
    plain_sq = jnp.sum(jnp.where(eye_e, nt(plain[...], plain[...]), 0.0), axis=0, keepdims=True)
    scaled_sq = jnp.sum(
        jnp.where(eye_e, nt(embeds[...], embeds[...]), 0.0), axis=0, keepdims=True
    )
    stats_all[t] = jnp.where(iota((8, E), 0) == 0, plain_sq, scaled_sq)
    stats_copies = [to_peer(7, k, stats_all.at[t], stats_all.at[t]) for k in rest]
    landed(logit_copies)
    landed(stats_copies)
    raw_dots, stats = logit_all[0], stats_all[0]
    for s in slots[1:]:
        raw_dots = raw_dots + logit_all[s]
        stats = stats + stats_all[s]
    inverse_row = lax.rsqrt(stats[0:1] / D + EPSILON)
    final_row = lax.rsqrt(inverse_row * inverse_row * stats[1:2] + EPSILON)
    scale_row = inverse_row * final_row
    scale_q = jnp.sum(jnp.where(pick, scale_row, 0.0), axis=1, keepdims=True)
    resid_inverse = jnp.sum(jnp.where(own_p, inverse_row, 0.0), axis=1, keepdims=True)
    final_inverse = jnp.sum(jnp.where(own_p, final_row, 0.0), axis=1, keepdims=True)
    resid_unit = resid * resid_inverse
    embed = resid_unit * ogain * final_inverse
    dots_q, dots_p = raw_dots * scale_q, raw_dots * scale_row
    logits = dots_q * scale_row / SOFTMAX_TEMPER
    grown = jnp.where(allowed, jnp.exp(logits - 1.0 / SOFTMAX_TEMPER), 0.0)
    totals = jnp.sum(grown, axis=1, keepdims=True)
    factor = LOSS_MULTIPLIER / (Q * SOFTMAX_TEMPER)
    coef = factor * (grown / totals - positive_f)
    coef_q16 = (coef * scale_row).astype(BF16)
    coef_p16 = (coef * scale_q).astype(BF16)
    coef_q = nn(own_q16, coef_q16).astype(BF16)
    coef_p = nt(own_p16, coef_p16).astype(BF16)
    d_embed = nn(coef_q, embeds[...]) + nn(coef_p, queries)
    along_q = jnp.sum(coef_q16.astype(F32) * dots_q, axis=1, keepdims=True)
    along_p = jnp.sum(coef_p16.astype(F32) * dots_p, axis=0, keepdims=True)
    along_q = jnp.sum(jnp.where(eye_q, along_q, 0.0), axis=0, keepdims=True)
    inner = jnp.sum(jnp.where(own_q, along_q, 0.0), axis=1, keepdims=True) + jnp.sum(
        jnp.where(own_p, along_p, 0.0), axis=1, keepdims=True
    )
    d_final = final_inverse * (d_embed - embed * inner)
    middle = inner * (EPSILON / D) * final_inverse * final_inverse
    d_resid = resid_inverse * (ogain * d_final - resid_unit * middle)
    d_resid16 = d_resid.astype(BF16)

    dap_out[...] = nt(d_resid16, wo_all[...])
    dap_copies = [to_peer(11, k, dap_out.at[:, pair(peers[k])], dap_in.at[t]) for k in rest]
    dap_in[t] = dap_out[:, pair(t)]
    target = jnp.sum(jnp.where(pos_hot, logits, 0.0), axis=1, keepdims=True)
    loss[0, 0] = jnp.sum(jnp.log(totals) + 1.0 / SOFTMAX_TEMPER - target) / Q
    probs16_t = nt(eye16, probs16).astype(BF16)
    landed(dap_copies)
    d_attn = dap_in[0]
    for s in slots[1:]:
        d_attn = d_attn + dap_in[s]
    d_attn16 = jnp.concatenate([d_attn[:, :HD], d_attn[:, HD:]], axis=0).astype(BF16)
    d_probs = nt(d_attn16, value16)
    d_scores16 = (
        probs * (d_probs - jnp.sum(probs * d_probs, axis=-1, keepdims=True)) / root
    ).astype(BF16)
    d_key_rot = nn(nt(eye16, d_scores16).astype(BF16), query16)
    d_value = nn(probs16_t, d_attn16)
    d_key_raw = head_backward(d_key_rot, key_unit, key_inverse, kg, cos_key, sin_key)
    column16 = jnp.where(even, d_key_raw, d_value).astype(BF16)
    dkv_all[:, block(t)] = column16
    my_dkv = dkv_all.at[:, block(t)]
    dkv_copies = [to_peer(12, k, my_dkv, my_dkv) for k in rest]
    d_query_rot = nn(d_scores16, key16)
    d_query_raw = head_backward(
        d_query_rot, query_unit, query_inverse, qg, cos_query, sin_query
    )
    d_query16 = jnp.where(even, d_query_raw[:S], d_query_raw[S:]).astype(BF16)
    dq_all[:, block(t)] = d_query16
    my_dq = dq_all.at[:, block(t)]
    dq_copies = [to_peer(13, k, my_dq, my_dq) for k in rest]
    raw = jnp.where(even, key_raw, value_raw)
    kv_sums = jnp.sum(column16.astype(F32) * raw, axis=1, keepdims=True)
    own_query = jnp.where(even, query_raw[:S], query_raw[S:])
    query_sums = jnp.sum(d_query16.astype(F32) * own_query, axis=1, keepdims=True)
    rows_all[t] = jnp.broadcast_to(
        jnp.sum(jnp.where(eye_n, kv_sums, 0.0), axis=0, keepdims=True)
        + jnp.sum(jnp.where(is_last, query_sums, 0.0), axis=0, keepdims=True),
        (8, N),
    )
    row_copies = [to_peer(8, k, rows_all.at[t], rows_all.at[t]) for k in rest]
    landed(dq_copies)
    extra = inverse_last * gain * nt(dq_all[...], wq_all[...]) + d_resid
    extra16 = extra.astype(BF16)
    extra_low = (extra - extra16.astype(F32)).astype(BF16)
    addend[...] = nn(last_hot_t, extra16) + nn(last_hot_t, extra_low)
    landed(row_copies)
    row_sums = rows_all[0]
    for s in slots[1:]:
        row_sums = row_sums + rows_all[s]
    mean = jnp.sum(jnp.where(eye_n, row_sums[0:1, :], 0.0), axis=1, keepdims=True) / D
    inverse = inv_all[:, 0:1]
    landed(dkv_copies)
    out_copies, local, earlier = [], [], list(waits)
    FC = F // CHUNKS if F % (128 * CHUNKS) == 0 else F // 2
    for c in range(F // FC):
        span = slice(c * FC, (c + 1) * FC)
        there = pl.ds(pl.multiple_of(t * F + c * FC, 128), FC)
        d_normed = nt(dkv_all[...], wkv_all[span, :])
        unit = hid_all[:, span].astype(F32) * inverse
        grad = inverse * (d_normed * gain[:, span] - unit * mean) + addend[:, span]
        out16[:, span] = grad.astype(BF16)
        for k in rest:
            rows = pl.ds(pl.multiple_of(peers[k] * own, own), own)
            out_copies.append(to_peer(14 + c, k, out16.at[rows, span], out.at[:, there]))
        copy = pltpu.make_async_copy(
            out16.at[my_rows, span], out.at[:, there], local_sem.at[12 + c]
        )
        copy.start()
        local.append(copy)
    for copy in earlier:
        copy.wait_send()
    for copy in local:
        copy.wait()
    for copy in out_copies:
        copy.wait()


def on_device(
    tensors, groups,
    hidden, lengths, positives, negatives, in_gain, wq, wkv, q_gain, k_gain, wo, out_gain
):
    T, G = tensors, groups
    own, D = hidden.shape
    F = D // T
    HD = wq.shape[1]
    N = own * T
    S = lengths.shape[1]
    Q = positives.shape[0]
    Z = G // 2
    hbm = pl.BlockSpec(memory_space=pltpu.HBM)
    anywhere = pl.BlockSpec(memory_space=pl.ANY)
    scratch = [
        pltpu.VMEM((1, S), jnp.int32),
        pltpu.VMEM((1, Q), jnp.int32),
        pltpu.VMEM((negatives.shape[1], Q), jnp.int32),
        pltpu.VMEM((2, 1, F), F32),
        pltpu.VMEM((2, 1, HD), F32),
        pltpu.VMEM((own, D), BF16),
        pltpu.VMEM((N, F), BF16),
        pltpu.VMEM((T, 8, HD), F32),
        pltpu.VMEM((N, HD), F32),
        pltpu.VMEM((N, F), BF16),
        pltpu.VMEM((F, T * HD), BF16),
        pltpu.VMEM((F, T * HD), BF16),
        pltpu.VMEM((T * HD, F), BF16),
        pltpu.VMEM((N, T * HD), BF16),
        pltpu.VMEM((T, N, 2 * HD), BF16),
        pltpu.VMEM((S, T * HD), F32),
        pltpu.VMEM((T, S, 2 * HD), F32),
        pltpu.VMEM((G * S, F), BF16),
        pltpu.VMEM((G * S, T * HD), BF16),
        pltpu.VMEM((G * S, F), BF16),
        pltpu.VMEM((G * S, F), BF16),
        pltpu.VMEM((T, Q, G * S), F32),
        pltpu.VMEM((T, 8, G * S), F32),
        pltpu.VMEM((S, T * HD), F32),
        pltpu.VMEM((T, S, 2 * HD), F32),
        pltpu.VMEM((N, T * HD), BF16),
        pltpu.VMEM((S, T * HD), BF16),
        pltpu.VMEM((T, 8, N), F32),
        pltpu.VMEM((N, F), F32),
        pltpu.VMEM((N, F), BF16),
        pltpu.SemaphoreType.DMA((12 + CHUNKS,)),
        pltpu.SemaphoreType.DMA((14 + CHUNKS, T - 1)),
        pltpu.SemaphoreType.DMA((14 + CHUNKS, T - 1)),
        pltpu.SemaphoreType.DMA((9, T - 1)),
        pltpu.SemaphoreType.DMA((9, T - 1)),
        pltpu.SemaphoreType.DMA((2, Z)),
        pltpu.SemaphoreType.DMA((2, Z)),
        pltpu.SemaphoreType.DMA((2, Z)),
        pltpu.SemaphoreType.DMA((2, Z)),
    ]
    d_hidden, loss = pl.pallas_call(
        functools.partial(kernel, T, G),
        out_shape=(
            jax.ShapeDtypeStruct((own, D), BF16),
            jax.ShapeDtypeStruct((1, 1), F32),
        ),
        in_specs=[hbm] * 11,
        out_specs=(anywhere, pl.BlockSpec(memory_space=pltpu.SMEM)),
        scratch_shapes=scratch,
        compiler_params=pltpu.CompilerParams(
            collective_id=0, has_side_effects=True, vmem_limit_bytes=60 * 1024 * 1024
        ),
    )(
        hidden, lengths, positives.reshape(1, Q), negatives.T, in_gain.reshape(1, D), wq, wkv,
        q_gain.reshape(1, HD), k_gain.reshape(1, HD), wo, out_gain.reshape(1, D),
    )
    return d_hidden, loss.reshape(())


def solution(mesh):
    placed = (
        P(("dp", "tensor"), None),
        P("dp", None),
        P(),
        P(),
        P(),
        P(None, "tensor"),
        P(None, "tensor"),
        P(),
        P(),
        P("tensor", None),
        P(),
    )
    return jax.shard_map(
        functools.partial(on_device, mesh.shape["tensor"], mesh.shape["dp"]),
        mesh=mesh,
        in_specs=placed,
        out_specs=(P(("dp", "tensor"), None), P()),
        check_vma=False,
    )
```
